128 devices in a mesh: tile: 64 (over z, y, x_hi, core), batch: 2 (over x_lo).
Axes of the slice: x: 4 (x_hi: 2, x_lo: 2; x = x_hi * 2 + x_lo), y: 4, z: 4, core: 2. Of those that a mesh axis runs over, the one named last changes fastest.
Arguments:
- fields: bfloat16 [2, 192, 32, 2048], P('batch', 'tile'), may hold values from -6 to 6
- cotangent: bfloat16 [2, 192, 32, 2048], P('batch', 'tile'), may hold values from -6 to 6
- first_kernel: float32 [3, 3, 64, 64], replicated, may hold values from -0.25 to 0.25
- second_kernel: float32 [3, 3, 64, 64], replicated, may hold values from -0.25 to 0.25
- adjacency: int32 [192, 4], replicated, may hold values from 0 to 191, as said below
- seam_codes: int32 [192, 4], replicated, may hold values from 0 to 7
- corner_map: int32 [192, 4], replicated, may hold values from 0 to 767, as said below
Outputs:
- output: bfloat16 [2, 192, 32, 2048], P('batch', 'tile')
- field_grad: bfloat16 [2, 192, 32, 2048], P('batch', 'tile')
- first_grad: float32 [3, 3, 64, 64], replicated
- second_grad: float32 [3, 3, 64, 64], replicated
The draws below stay inside these ranges and needn't reach their ends.
Inputs may be any that keep to these rules, and one draw needn't show every extreme that they name: `adjacency`: tile t lies on device t // 3 of the tile axis; which sphere region each device holds is decided at run time, so the tables are data, not compile-time constants. Every edge of every tile meets exactly one edge of another tile, and mutually: if edge e of t meets edge e' of u then edge e' of u meets edge e of t with the same reversal. The edges joining one device's tiles to another device's tiles number at most 3, and some pair of devices reaches 3. `corner_map`: every entry names a corner pixel of a tile other than the tile itself.
All inputs are finite; a program needn't handle non-finite values.
Results may differ from the reference program's by a relative error of at most 0.0057.
Values may be sent and summed in bfloat16 or wider, within the bound.
A program may use at most 128 MiB of HBM per device.

```python
import math
import jax
import jax.numpy as jnp
import numpy as np
from jax import lax

C = 64
S = 32
TILES = 192
BATCH = 2


def face_links():
    link_table = []
    for face_id in range(12):
        cycle_id = face_id // 4
        within = face_id % 4
        if cycle_id == 0:
            link_table.append([(4 + (within + 1) % 4, 2, 0), (4 + within, 3, 0), ((within + 3) % 4, 3, 1), ((within + 1) % 4, 2, 1)])
        elif cycle_id == 1:
            link_table.append([(8 + within, 2, 0), (8 + (within + 3) % 4, 3, 0), ((within + 3) % 4, 0, 0), (within, 1, 0)])
        else:
            link_table.append([(8 + (within + 1) % 4, 1, 1), (8 + (within + 3) % 4, 0, 1), (4 + within, 0, 0), (4 + (within + 1) % 4, 1, 0)])
    return link_table


def landing(edge_id, position, length):
    if edge_id == 0:
        return (length - 1, position)
    if edge_id == 1:
        return (position, 0)
    if edge_id == 2:
        return (0, position)
    return (position, length - 1)


def base_tables(tile_total):
    face_side = math.isqrt(tile_total // 12)
    link_table = face_links()

    def number(face_id, tile_row, tile_col):
        cycle_id = face_id // 4
        within = face_id % 4
        column = within if cycle_id == 0 else (within + 3) % 4
        return ((column * face_side + tile_row) * face_side + tile_col) * 3 + cycle_id

    def resolve(face_id, pixel_row, pixel_col, length):
        for attempt in range(3):
            if pixel_row < 0 or pixel_row >= length:
                edge_id = 2 if pixel_row < 0 else 0
                position = pixel_col
            elif pixel_col < 0 or pixel_col >= length:
                edge_id = 1 if pixel_col < 0 else 3
                position = pixel_row
            else:
                return (face_id, pixel_row, pixel_col)
            next_face, next_edge, reverse = link_table[face_id][edge_id]
            if reverse:
                position = length - 1 - position
            pixel_row, pixel_col = landing(next_edge, position, length)
            face_id = next_face
        return (face_id, pixel_row, pixel_col)
    steps = [(1, 0), (0, -1), (-1, 0), (0, 1)]
    sub_side = 3
    corner_offsets = [(-1, -1), (-1, sub_side), (sub_side, -1), (sub_side, sub_side)]
    neighbours = np.zeros((tile_total, 4), np.int32)
    codes = np.zeros((tile_total, 4), np.int32)
    corners = np.zeros((tile_total, 4), np.int32)
    for face_id in range(12):
        for tile_row in range(face_side):
            for tile_col in range(face_side):
                tile_id = number(face_id, tile_row, tile_col)
                for edge_id in range(4):
                    next_row = tile_row + steps[edge_id][0]
                    next_col = tile_col + steps[edge_id][1]
                    if 0 <= next_row < face_side and 0 <= next_col < face_side:
                        neighbours[tile_id, edge_id] = number(face_id, next_row, next_col)
                        codes[tile_id, edge_id] = (edge_id + 2) % 4
                    else:
                        next_face, next_edge, reverse = link_table[face_id][edge_id]
                        position = tile_col if edge_id in (0, 2) else tile_row
                        if reverse:
                            position = face_side - 1 - position
                        land_row, land_col = landing(next_edge, position, face_side)
                        neighbours[tile_id, edge_id] = number(next_face, land_row, land_col)
                        codes[tile_id, edge_id] = next_edge + 4 * reverse
                for corner_id in range(4):
                    pixel_row = tile_row * sub_side + corner_offsets[corner_id][0]
                    pixel_col = tile_col * sub_side + corner_offsets[corner_id][1]
                    found_face, found_row, found_col = resolve(face_id, pixel_row, pixel_col, face_side * sub_side)
                    found_tile = number(found_face, found_row // sub_side, found_col // sub_side)
                    which = 2 * int(found_row % sub_side == sub_side - 1) + int(found_col % sub_side == sub_side - 1)
                    corners[tile_id, corner_id] = found_tile * 4 + which
    return (neighbours, codes, corners)


def placed_tables(key):
    neighbours, codes, corners = base_tables(TILES)
    placement = jax.random.permutation(key, TILES // 3).astype(jnp.int32)
    base_ids = jnp.arange(TILES, dtype=jnp.int32)
    new_ids = placement[base_ids // 3] * 3 + base_ids % 3
    new_neighbours = jnp.zeros((TILES, 4), jnp.int32).at[new_ids].set(new_ids[jnp.asarray(neighbours)])
    new_codes = jnp.zeros((TILES, 4), jnp.int32).at[new_ids].set(jnp.asarray(codes))
    corner_arr = jnp.asarray(corners)
    new_corners = jnp.zeros((TILES, 4), jnp.int32).at[new_ids].set(new_ids[corner_arr // 4] * 4 + corner_arr % 4)
    return (new_neighbours, new_codes, new_corners)


def draw_adjacency(key, part):
    return placed_tables(key)[0]


def draw_seam_codes(key, part):
    return placed_tables(key)[1]


def draw_corner_map(key, part):
    return placed_tables(key)[2]


def levels(key, dims, pieces, low, top_value):
    def one(dim, blocks):
        draws = jax.random.uniform(jax.random.fold_in(jax.random.fold_in(key, 6), dim), (blocks,), jnp.float32, low / len(pieces), top_value / len(pieces))
        return jnp.repeat(jnp.exp(draws), dims[dim] // blocks).reshape((-1,) + (1,) * (len(dims) - dim - 1))

    gain = one(*pieces[0])
    for cut in pieces[1:]:
        gain = gain * one(*cut)
    return gain


def bell_draw(key, shape, width, most, shards=(), held_as=jnp.bfloat16):
    loudness = levels(key, shape, shards, -0.22, 0.18) if shards else 1.0
    drawn = jax.random.normal(key, shape, jnp.float32) * width * loudness
    return jnp.minimum(jnp.maximum(drawn, -most), most).astype(held_as)


def setup_inputs(seed: int = 0) -> dict:
    streams_of = jax.random.split(jax.random.key(seed), 8)
    return {
        "fields": bell_draw(streams_of[0], (BATCH, TILES, S, S * C), 1.0, 6.0, ((0, 2), (1, 64))),
        "cotangent": bell_draw(streams_of[1], (BATCH, TILES, S, S * C), 1.0, 6.0, ((0, 2), (1, 64))),
        "first_kernel": bell_draw(streams_of[2], (3, 3, C, C), (9 * C) ** -0.5, 0.25, (), jnp.float32),
        "second_kernel": bell_draw(streams_of[3], (3, 3, C, C), (9 * C) ** -0.5, 0.25, (), jnp.float32),
        "adjacency": draw_adjacency(jax.random.fold_in(streams_of[7], 71), 0),
        "seam_codes": draw_seam_codes(jax.random.fold_in(streams_of[7], 71), 0),
        "corner_map": draw_corner_map(jax.random.fold_in(streams_of[7], 71), 0),
    }


def edge_strips(values):
    return jnp.stack([values[..., -1, :, :], values[..., :, 0, :], values[..., 0, :, :], values[..., :, -1, :]], axis=-3)

def corner_cells(values):
    return jnp.stack([values[..., 0, 0, :], values[..., 0, -1, :], values[..., -1, 0, :], values[..., -1, -1, :]], axis=-2)

def orient(strips, seam_codes):
    reverse = (seam_codes >= 4)[:, :, None, None]
    return jnp.where(reverse, strips[..., ::-1, :], strips)

def framed(values, rim_vals, corner_vals):
    upper = jnp.concatenate([corner_vals[..., 0:1, :], rim_vals[..., 2, :, :], corner_vals[..., 1:2, :]], axis=-2)
    lower = jnp.concatenate([corner_vals[..., 2:3, :], rim_vals[..., 0, :, :], corner_vals[..., 3:4, :]], axis=-2)
    middle = jnp.concatenate([rim_vals[..., 1, :, None, :], values, rim_vals[..., 3, :, None, :]], axis=-2)
    return jnp.concatenate([upper[..., None, :, :], middle, lower[..., None, :, :]], axis=-3)

def rim_parts(padded):
    interior = padded[..., 1:-1, 1:-1, :]
    rim_vals = jnp.stack([padded[..., -1, 1:-1, :], padded[..., 1:-1, 0, :], padded[..., 0, 1:-1, :], padded[..., 1:-1, -1, :]], axis=-3)
    corner_vals = jnp.stack([padded[..., 0, 0, :], padded[..., 0, -1, :], padded[..., -1, 0, :], padded[..., -1, -1, :]], axis=-2)
    return (interior, rim_vals, corner_vals)

def add_rims(interior, rim_vals, corner_vals):
    interior = interior.at[..., -1, :, :].add(rim_vals[..., 0, :, :])
    interior = interior.at[..., :, 0, :].add(rim_vals[..., 1, :, :])
    interior = interior.at[..., 0, :, :].add(rim_vals[..., 2, :, :])
    interior = interior.at[..., :, -1, :].add(rim_vals[..., 3, :, :])
    interior = interior.at[..., 0, 0, :].add(corner_vals[..., 0, :])
    interior = interior.at[..., 0, -1, :].add(corner_vals[..., 1, :])
    interior = interior.at[..., -1, 0, :].add(corner_vals[..., 2, :])
    interior = interior.at[..., -1, -1, :].add(corner_vals[..., 3, :])
    return interior

def conv_valid(padded, kernel):
    return lax.conv_general_dilated(padded, kernel, (1, 1), 'VALID', dimension_numbers=('NHWC', 'HWIO', 'NHWC'), preferred_element_type=jnp.float32)

def conv_full(tile_grad, kernel):
    turned = jnp.transpose(kernel[::-1, ::-1], (0, 1, 3, 2))
    return lax.conv_general_dilated(tile_grad, turned, (1, 1), ((2, 2), (2, 2)), dimension_numbers=('NHWC', 'HWIO', 'NHWC'), preferred_element_type=jnp.float32)

def kernel_grad(padded, tile_grad):
    tile_side = tile_grad.shape[1]
    channels = tile_grad.shape[3]
    flat_grad = tile_grad.reshape(-1, channels)
    row_terms = []
    for shift_row in range(3):
        column_terms = []
        for shift_col in range(3):
            window = padded[:, shift_row:shift_row + tile_side, shift_col:shift_col + tile_side, :].reshape(-1, channels)
            column_terms.append(lax.dot_general(window, flat_grad, (((0,), (0,)), ((), ())), preferred_element_type=jnp.float32))
        row_terms.append(jnp.stack(column_terms))
    return jnp.stack(row_terms)

def blocks_in(array):
    return jnp.moveaxis(array.reshape((array.shape[0], array.shape[1] // 3, 3) + array.shape[2:]), 1, 0)

def blocks_out(array):
    moved_axes = jnp.moveaxis(array, 0, 1)
    return moved_axes.reshape((moved_axes.shape[0], moved_axes.shape[1] * moved_axes.shape[2]) + moved_axes.shape[3:])

def reference(fields, cotangent, first_kernel, second_kernel, adjacency, seam_codes, corner_map):
    tile_field = fields.reshape(BATCH, TILES, S, S, C)
    tile_grad = cotangent.reshape(BATCH, TILES, S, S, C)
    w_first = first_kernel.astype(jnp.bfloat16)
    w_second = second_kernel.astype(jnp.bfloat16)
    need_rows = adjacency * 4 + seam_codes % 4

    def halo_parts(values):
        strips = edge_strips(values).reshape(BATCH, TILES * 4, S, C)
        corner_vals = corner_cells(values).reshape(BATCH, TILES * 4, C)
        return (orient(strips[:, need_rows], seam_codes), corner_vals[:, corner_map])

    def adjoint_parts(rim_vals, corner_vals):
        routed = orient(rim_vals.reshape(BATCH, TILES * 4, S, C)[:, need_rows], seam_codes)
        summed = jnp.zeros((BATCH, TILES * 4, C), jnp.float32).at[:, corner_map.reshape(-1)].add(corner_vals.reshape(BATCH, TILES * 4, C))
        return (routed, summed.reshape(BATCH, TILES, 4, C))

    def section_one(members):
        field_blk, rim_blk, corner_blk = members
        pre_act = conv_valid(framed(field_blk, rim_blk, corner_blk).reshape(-1, S + 2, S + 2, C), w_first)
        return jax.nn.silu(pre_act).astype(jnp.bfloat16).reshape(field_blk.shape)
    field_rims, field_corners = halo_parts(tile_field)
    hidden = blocks_out(lax.map(section_one, (blocks_in(tile_field), blocks_in(field_rims), blocks_in(field_corners))))
    hidden_rims, hidden_corners = halo_parts(hidden)

    def section_two(members):
        field_blk, grad_blk, hidden_blk, rim_blk, corner_blk = members
        padded = framed(hidden_blk, rim_blk, corner_blk).reshape(-1, S + 2, S + 2, C)
        flat_grad = grad_blk.reshape(-1, S, S, C)
        output_blk = (field_blk.astype(jnp.float32) + conv_valid(padded, w_second).reshape(field_blk.shape)).astype(jnp.bfloat16)
        interior, rim_vals, corner_vals = rim_parts(conv_full(flat_grad, w_second))
        return (output_blk, rim_vals.astype(jnp.bfloat16).reshape(BATCH, 3, 4, S, C), corner_vals.astype(jnp.bfloat16).reshape(BATCH, 3, 4, C), kernel_grad(padded, flat_grad))
    output_b, back_rims, back_corners, second_parts = lax.map(section_two, (blocks_in(tile_field), blocks_in(tile_grad), blocks_in(hidden), blocks_in(hidden_rims), blocks_in(hidden_corners)))
    output = blocks_out(output_b)
    routed, summed = adjoint_parts(blocks_out(back_rims), blocks_out(back_corners))

    def section_three(members):
        field_blk, grad_blk, rim_blk, corner_blk, routed_blk, summed_blk = members
        padded = framed(field_blk, rim_blk, corner_blk).reshape(-1, S + 2, S + 2, C)
        pre_act = conv_valid(padded, w_first)
        interior, rim_vals, corner_vals = rim_parts(conv_full(grad_blk.reshape(-1, S, S, C), w_second))
        hidden_grad = add_rims(interior, routed_blk.reshape(-1, 4, S, C), summed_blk.reshape(-1, 4, C))
        sigmoid_pre = jax.nn.sigmoid(pre_act)
        pre_grad = (hidden_grad * sigmoid_pre * (1.0 + pre_act * (1.0 - sigmoid_pre))).astype(jnp.bfloat16)
        interior_two, rims_two, corners_two = rim_parts(conv_full(pre_grad, w_first))
        return (pre_grad.reshape(BATCH, 3, S, S, C), rims_two.astype(jnp.bfloat16).reshape(BATCH, 3, 4, S, C), corners_two.astype(jnp.bfloat16).reshape(BATCH, 3, 4, C), kernel_grad(padded, pre_grad))
    pre_grad_b, rims_two, corners_two, first_parts = lax.map(section_three, (blocks_in(tile_field), blocks_in(tile_grad), blocks_in(field_rims), blocks_in(field_corners), blocks_in(routed), blocks_in(summed)))
    pre_grad = blocks_out(pre_grad_b)
    routed_two, summed_two = adjoint_parts(blocks_out(rims_two), blocks_out(corners_two))

    def section_four(members):
        grad_blk, pre_blk, routed_blk, summed_blk = members
        interior, rim_vals, corner_vals = rim_parts(conv_full(pre_blk.reshape(-1, S, S, C), w_first))
        back = add_rims(interior, routed_blk.reshape(-1, 4, S, C), summed_blk.reshape(-1, 4, C))
        return (grad_blk.reshape(-1, S, S, C).astype(jnp.float32) + back).astype(jnp.bfloat16).reshape(grad_blk.shape)
    field_grad = blocks_out(lax.map(section_four, (blocks_in(tile_grad), blocks_in(pre_grad), blocks_in(routed_two), blocks_in(summed_two))))
    grad_scale = 1.0 / math.sqrt(BATCH * TILES * S * S)
    first_grad = lax.optimization_barrier(jnp.sum(first_parts, axis=0)) * grad_scale
    second_grad = lax.optimization_barrier(jnp.sum(second_parts, axis=0)) * grad_scale
    return (output.reshape(BATCH, TILES, S, S * C), field_grad.reshape(BATCH, TILES, S, S * C), first_grad, second_grad)
```

```python
import functools
import math

import jax
import jax.numpy as jnp
from jax import lax
from jax.experimental import pallas as pl
from jax.experimental.pallas import tpu as pltpu
from jax.sharding import PartitionSpec as P

TL = 3
S = 32
C = 64
NP = 16
R = TL * S
EDGES = TL * 4
LINES = EDGES * S
PARTS = EDGES + 1
PAIRS = NP + 2
PR = 128
MESH = pl.DeviceIdType.MESH
F32 = jnp.float32
BF = jnp.bfloat16
VM = pl.BlockSpec(memory_space=pltpu.VMEM)
SM = pl.BlockSpec(memory_space=pltpu.SMEM)


def rows_at(t):
    return t * 40 + 8


def low_lanes(rows):
    return lax.broadcasted_iota(jnp.int32, (rows, 128), 1) < C


def swap(v):
    return pltpu.roll(v, C, 1)


def put_lines(lines, first, second, place, out):
    low16, low32 = low_lanes(16), low_lanes(32)
    step = place(1, 0) - place(0, 0)
    for t in range(TL):
        for e, i in ((0, S - 1), (2, 0)):
            where = pl.ds(place(0, t) + i, NP, stride=step)
            a, b = first[where, :], second[where, :]
            base = (t * 4 + e) * S
            lines[pl.ds(base, NP, stride=2), :] = jnp.where(low16, a, swap(b))
            lines[pl.ds(base + 1, NP, stride=2), :] = jnp.where(low16, swap(a), b)
        for e, pair in ((1, 0), (3, NP - 1)):
            where = pl.ds(place(pair, t), S)
            a, b = first[where, :], second[where, :]
            line = jnp.where(low32, a, swap(b)) if e == 1 else jnp.where(low32, swap(a), b)
            lines[pl.ds((t * 4 + e) * S, S), :] = line
        for corner, (e, s) in enumerate(((2, 0), (2, S - 1), (0, 0), (0, S - 1))):
            lines[pl.ds(LINES + t * 4 + corner, 1), :] = lines[pl.ds((t * 4 + e) * S + s, 1), :]
    lines[pl.ds(LINES + EDGES, S - EDGES), :] = jnp.zeros((S - EDGES, 128), F32)
    for j in range(PARTS):
        out[j] = lines[pl.ds(j * S, S), :].astype(BF)


def fill_pad(pad, src):
    for p in (0, PAIRS - 1):
        pad[pl.ds(p * PR, PR), :] = jnp.zeros((PR, 128), F32)
    for p in range(NP):
        for t in range(TL):
            base = (p + 1) * PR + rows_at(t)
            pad[pl.ds(base - 8, 8), :] = jnp.zeros((8, 128), F32)
            pad[pl.ds(base, S), :] = src[t * S : (t + 1) * S, p * 128 : (p + 1) * 128].astype(F32)
        pad[pl.ds((p + 1) * PR + 120, 8), :] = jnp.zeros((8, 128), F32)


def pad_place(pair, t):
    return (pair + 1) * PR + rows_at(t)


def flat_place(pair, t):
    return pair * R + t * S


def make_shifts(xp, pad):
    for a in range(3):
        for p in range(PAIRS):
            for t in range(TL):
                xp[a, p, t * S : (t + 1) * S, :] = pad[pl.ds(p * PR + rows_at(t) - 1 + a, S), :].astype(BF)


def build_forward(w_out, w):
    w_out[...] = jnp.zeros_like(w_out)
    for a in range(3):
        for c in range(3):
            block = w[a, c].astype(BF)
            for n in range(4):
                m = n + 1 + c
                w_out[a, m * C : (m + 1) * C, n * C : (n + 1) * C] = block


def build_backward(w_out, w_rim, w_corner, w):
    w_out[...] = jnp.zeros_like(w_out)
    w_rim[...] = jnp.zeros_like(w_rim)
    w_corner[...] = jnp.zeros_like(w_corner)
    for a in range(3):
        for c in range(3):
            block = w[a, c].T.astype(BF)
            for n in range(4):
                m = n + 3 - c
                w_out[2 - a, m * C : (m + 1) * C, n * C : (n + 1) * C] = block
            spots = []
            if a == 2:
                spots.append((0, c))
            if c == 0:
                spots.append((1, a))
            if a == 0:
                spots.append((2, c))
            if c == 2:
                spots.append((3, a))
            for e, tap in spots:
                w_rim[tap * 128 + C : tap * 128 + 128, e * C : (e + 1) * C] = block
            if a != 1 and c != 1:
                corner = (a // 2) * 2 + c // 2
                w_corner[C:128, corner * C : (corner + 1) * C] = block


def conv(xp, w):
    total = None
    for a in range(3):
        left = jnp.concatenate(
            [
                jnp.concatenate([xp[a, 2 * q + s] for q in range(NP // 2)], axis=0)
                for s in range(4)
            ],
            axis=1,
        )
        part = jnp.dot(left, w[a], preferred_element_type=F32)
        total = part if total is None else total + part
    return total


def kernel_grad(xp, q, a, upper):
    wide = jnp.concatenate(
        [jnp.concatenate([xp[a, d + p] for p in range(NP)], axis=0) for d in range(3)], axis=1
    )
    out = lax.dot_general(q, wide, (((0,), (0,)), ((), ())), preferred_element_type=F32)
    turned = jnp.concatenate([out[:, d * 128 : (d + 1) * 128].T for d in range(3)], axis=0)
    here, there = turned[64:256], turned[128:320]
    return swap(here) + there if upper else here + swap(there)


def orient(lines_ref, tab, me, w_rim, turned):
    lines = lines_ref[...].astype(F32)
    low = low_lanes(S)
    spot = lax.broadcasted_iota(jnp.int32, (LINES, 128), 0) % S
    after = jnp.where(spot == S - 1, 0.0, pltpu.roll(lines, LINES - 1, 0)).astype(BF)
    before = jnp.where(spot == 0, 0.0, pltpu.roll(lines, 1, 0)).astype(BF)
    wide = jnp.concatenate([after, lines_ref[...], before], axis=1)
    rims = jnp.dot(wide, w_rim[...], preferred_element_type=F32)
    flip = (
        lax.broadcasted_iota(jnp.int32, (S, S), 0) + lax.broadcasted_iota(jnp.int32, (S, S), 1)
        == S - 1
    )
    flip = jnp.where(flip, 1.0, 0.0).astype(BF)
    kept = []
    codes = [tab[768 + me * EDGES + j] for j in range(EDGES)]
    for j in range(EDGES):
        e = codes[j] % 4
        at = slice(j * S, (j + 1) * S)
        pair = jnp.where(e >= 2, rims[at, 128:], rims[at, :128])
        rim = jnp.where(e % 2 == 1, pair, swap(pair))
        kept.append(jnp.where(low, lines[at], rim).astype(BF))
    flipped = jnp.dot(flip, jnp.concatenate(kept, axis=1), preferred_element_type=F32)
    for j in range(EDGES):
        turned[pl.ds(j * S, S), :] = jnp.where(
            codes[j] >= 4, flipped[:, j * 128 : (j + 1) * 128], kept[j].astype(F32)
        )


def halo_in(pad, turned, cells):
    low16 = low_lanes(16)
    cells_swapped = swap(cells[...])
    for t in range(TL):
        for e, row in ((0, rows_at(t) + S), (2, rows_at(t) - 1)):
            base = (t * 4 + e) * S
            even = turned[pl.ds(base, NP, stride=2), :]
            odd = turned[pl.ds(base + 1, NP, stride=2), :]
            pad[pl.ds(PR + row, NP, stride=PR), :] = jnp.where(low16, even, swap(odd))
        pad[pl.ds(rows_at(t), S), :] = swap(turned[pl.ds((t * 4 + 1) * S, S), :])
        pad[pl.ds((PAIRS - 1) * PR + rows_at(t), S), :] = turned[pl.ds((t * 4 + 3) * S, S), :]
        for corner, (row, p) in enumerate(((-1, 0), (-1, 1), (S, 0), (S, 1))):
            at = t * 4 + corner
            value = (cells[...] if p else cells_swapped)[at : at + 1]
            pad[pl.ds(p * (PAIRS - 1) * PR + rows_at(t) + row, 1), :] = value


def corner_sums(corners_ref, corner_row, me, w_corner):
    every = jnp.dot(corners_ref[...], w_corner[...], preferred_element_type=F32)
    kind = lax.broadcasted_iota(jnp.int32, (1024, 128), 0) % 4
    pair = jnp.where(kind >= 2, every[:, 128:], every[:, :128])
    other = swap(pair)
    low = low_lanes(1024)
    both = jnp.where((kind % 2 == 1) == low, other, pair).astype(BF)
    mine = me * EDGES + lax.broadcasted_iota(jnp.int32, (16, 1024), 0)
    real = lax.broadcasted_iota(jnp.int32, (16, 1024), 0) < EDGES
    pick = jnp.where((corner_row[...] == mine) & real, 1.0, 0.0).astype(BF)
    return jnp.dot(pick, both, preferred_element_type=F32)


def rims_in(back, turned, sums):
    low16, low32, low1 = low_lanes(16), low_lanes(S), low_lanes(16)
    for t in range(TL):
        for e, i in ((0, S - 1), (2, 0)):
            base = (t * 4 + e) * S
            even = turned[pl.ds(base, NP, stride=2), :]
            odd = turned[pl.ds(base + 1, NP, stride=2), :]
            at = pl.ds(t * S + i, NP, stride=R)
            back[at, :] = back[at, :] + jnp.where(low16, swap(even), odd)
        at = pl.ds(t * S, S)
        line = swap(turned[pl.ds((t * 4 + 1) * S, S), :])
        back[at, :] = back[at, :] + jnp.where(low32, line, 0.0)
        at = pl.ds((NP - 1) * R + t * S, S)
        back[at, :] = back[at, :] + jnp.where(low32, 0.0, turned[pl.ds((t * 4 + 3) * S, S), :])
    lows, highs = jnp.where(low1, sums, 0.0), jnp.where(low1, 0.0, sums)
    for t in range(TL):
        for corner, (i, p) in enumerate(((0, 0), (0, 1), (S - 1, 0), (S - 1, 1))):
            at = pl.ds(p * (NP - 1) * R + t * S + i, 1)
            s = t * 4 + corner
            back[at, :] = back[at, :] + (highs if p else lows)[s : s + 1]


def both_convs(
    x_ref, q_ref, wf_ref, wb_ref, lines_ref, corners_ref, corner_row, tab,
    pad, xp, qp, w_conv, w_rim, w_corner, turned, cells_all, cells, main, back,
):
    me = lax.axis_index("tile")
    build_backward(w_conv, w_rim, w_corner, wb_ref)
    fill_pad(pad, q_ref)
    make_shifts(qp, pad)
    out = conv(qp, w_conv)
    for q in range(NP // 2):
        for half in range(2):
            back[pl.ds((2 * q + half) * R, R), :] = out[q * R : (q + 1) * R, half * 128 : (half + 1) * 128]
    orient(lines_ref, tab, me, w_rim, turned)
    sums = corner_sums(corners_ref, corner_row, me, w_corner)
    rims_in(back, turned, sums)
    cells_all[...] = corners_ref[...].astype(F32)
    for s in range(EDGES):
        v = tab[1536 + me * EDGES + s]
        tile = v // 4
        device = tile // 3
        row = device * 16 + (tile - device * 3) * 4 + v % 4
        cells[pl.ds(s, 1), :] = cells_all[pl.ds(row, 1), :]
    cells[pl.ds(EDGES, 4), :] = jnp.zeros((4, 128), F32)
    fill_pad(pad, x_ref)
    halo_in(pad, turned, cells)
    make_shifts(xp, pad)
    build_forward(w_conv, wf_ref)
    main[...] = conv(xp, w_conv)


CONV_SCRATCH = [
    pltpu.VMEM((PAIRS * PR, 128), F32),
    pltpu.VMEM((3, PAIRS, R, 128), BF),
    pltpu.VMEM((3, PAIRS, R, 128), BF),
    pltpu.VMEM((3, 512, 256), BF),
    pltpu.VMEM((384, 256), BF),
    pltpu.VMEM((128, 256), BF),
    pltpu.VMEM((LINES, 128), F32),
    pltpu.VMEM((1024, 128), F32),
    pltpu.VMEM((16, 128), F32),
    pltpu.VMEM((NP // 2 * R, 256), F32),
    pltpu.VMEM((NP * R, 128), F32),
]


def start_kernel(f_ref, c_ref, out, pad_a, pad_b, lines):
    fill_pad(pad_a, f_ref)
    fill_pad(pad_b, c_ref)
    put_lines(lines, pad_a, pad_b, pad_place, out)


def middle_kernel(
    f_ref, c_ref, w1_ref, w2_ref, lines_ref, corners_ref, corner_row, tab,
    hidden, pre_grad, grad, out,
    pad, xp, qp, w_conv, w_rim, w_corner, turned, cells_all, cells, main, back, hid, lines, grads,
):
    both_convs(
        f_ref, c_ref, w1_ref, w2_ref, lines_ref, corners_ref, corner_row, tab,
        pad, xp, qp, w_conv, w_rim, w_corner, turned, cells_all, cells, main, back,
    )
    for p in range(NP):
        pre = main[pl.ds((p // 2) * R, R), (p % 2) * 128 : (p % 2) * 128 + 128]
        at = pl.ds(p * R, R)
        s = 1.0 / (1.0 + jnp.exp(-pre))
        h = (pre * s).astype(BF)
        g = (back[at, :] * s * (1.0 + pre * (1.0 - s))).astype(BF)
        hidden[:, p * 128 : (p + 1) * 128] = h
        pre_grad[:, p * 128 : (p + 1) * 128] = g
        hid[at, :] = h.astype(F32)
        back[at, :] = g.astype(F32)
        grads[at, :] = g
    put_lines(lines, hid, back, flat_place, out)
    for a in range(3):
        grad[pl.ds(a * 192, 192), :] = kernel_grad(xp, grads[...], a, False)


def last_kernel(
    h_ref, g_ref, f_ref, c_ref, w1_ref, w2_ref, lines_ref, corners_ref, corner_row, tab, grad_one,
    output, field_grad, grad,
    pad, xp, qp, w_conv, w_rim, w_corner, turned, cells_all, cells, main, back, grads,
):
    both_convs(
        h_ref, g_ref, w2_ref, w1_ref, lines_ref, corners_ref, corner_row, tab,
        pad, xp, qp, w_conv, w_rim, w_corner, turned, cells_all, cells, main, back,
    )
    for p in range(NP):
        at, lanes = pl.ds(p * R, R), slice(p * 128, (p + 1) * 128)
        made = main[pl.ds((p // 2) * R, R), (p % 2) * 128 : (p % 2) * 128 + 128]
        output[:, lanes] = (f_ref[:, lanes].astype(F32) + made).astype(BF)
        c = c_ref[:, lanes]
        field_grad[:, lanes] = (c.astype(F32) + back[at, :]).astype(BF)
        grads[at, :] = c
    low = low_lanes(192)
    for a in range(3):
        at = pl.ds(a * 192, 192)
        grad[at, :] = jnp.where(low, grad_one[at, :], kernel_grad(xp, grads[...], a, True))


def exchange_kernel(x_ref, tab, out_lines, out_corners, held, stage, got, s_z, r_z, s_c, r_c, s_p, r_p):
    t = lax.axis_index("tile")
    b = lax.axis_index("batch")
    z, plane, core = t // 16, (t // 2) % 8, t % 2

    def device(z, plane, core):
        return (z * 16 + plane * 2 + core, b)

    partners = [device((z + k) % 4, plane, core) for k in range(1, 4)]
    partners.append(device(z, plane, 1 - core))
    partners += [device(z, (plane + k) % 8, core) for k in range(1, 8)]
    barrier = pltpu.get_barrier_semaphore()
    for other in partners:
        pl.semaphore_signal(barrier, inc=1, device_id=other, device_id_type=MESH)
    pl.semaphore_wait(barrier, len(partners))

    def slot(z, core):
        return held.at[pl.ds((z * 2 + core) * PARTS, PARTS)]

    def remote(src, dst, send, recv, other):
        copy = pltpu.make_async_remote_copy(
            src_ref=src, dst_ref=dst, send_sem=send, recv_sem=recv, device_id=other, device_id_type=MESH
        )
        copy.start()
        return copy

    along = [remote(x_ref, slot(z, core), s_z.at[k], r_z.at[k], partners[k]) for k in range(3)]
    across = [remote(x_ref, slot(z, core), s_c.at[0], r_c.at[0], partners[3])]
    held[pl.ds((z * 2 + core) * PARTS, PARTS)] = x_ref[...]
    for k in range(3):
        along[k].wait_recv()
        here = slot((z + 3 - k) % 4, core)
        across.append(remote(here, here, s_c.at[k + 1], r_c.at[k + 1], partners[3]))
    for copy in across:
        copy.wait_recv()

    def entry(dev, j):
        tile, code = tab[dev * EDGES + j], tab[768 + dev * EDGES + j]
        source = (tile * 171) >> 9
        return source, (tile - source * 3) * 4 + (code & 3)

    planes = []
    for k in range(8):
        other = (plane + k) % 8

        def take(j, _, k=k, other=other):
            source, line = entry(z * 16 + other * 2 + core, j)
            stage[k, j] = held[((source >> 4) * 2 + (source & 1)) * PARTS + line]
            return 0

        lax.fori_loop(0, EDGES, take, 0)
        for s in range(8):
            stage[k, EDGES + s // 2, (s % 2) * 16 : (s % 2) * 16 + 16, :] = held[s * PARTS + EDGES, :16, :]
        if k:
            planes.append(
                remote(stage.at[k], got.at[pl.ds(plane * 16, 16)], s_p.at[k - 1], r_p.at[k - 1], partners[3 + k])
            )
        else:
            got[pl.ds(plane * 16, 16)] = stage[0]
    for copy in planes:
        copy.wait_recv()

    def give(j, _):
        source, _line = entry(t, j)
        out_lines[pl.ds(pl.multiple_of(j * S, S), S), :] = got[((source >> 1) & 7) * 16 + j]
        return 0

    lax.fori_loop(0, EDGES, give, 0)
    for zz in range(4):
        for pp in range(8):
            out_corners[(zz * 8 + pp) * 32 : (zz * 8 + pp) * 32 + 32, :] = got[pp * 16 + EDGES + zz]
    for copy in along + across + planes:
        copy.wait_send()


def exchange(lines, tab, ident):
    sem = pltpu.SemaphoreType.DMA
    return pl.pallas_call(
        exchange_kernel,
        out_shape=(jax.ShapeDtypeStruct((LINES, 128), BF), jax.ShapeDtypeStruct((1024, 128), BF)),
        in_specs=[VM, SM],
        out_specs=(VM, VM),
        scratch_shapes=[
            pltpu.VMEM((8 * PARTS, S, 128), BF),
            pltpu.VMEM((8, 16, S, 128), BF),
            pltpu.VMEM((8 * 16, S, 128), BF),
            sem((3,)), sem((3,)), sem((4,)), sem((4,)), sem((7,)), sem((7,)),
        ],
        name="exchange",
        compiler_params=pltpu.CompilerParams(
            collective_id=ident, has_side_effects=True, vmem_limit_bytes=40 * 2**20
        ),
    )(lines, tab)


def total_kernel(x_ref, out, mine, parts, ys, zs, s_a, r_a, s_y, r_y, s_z, r_z, s_g, r_g):
    t = lax.axis_index("tile")
    b = lax.axis_index("batch")
    z, y, hi, core = t // 16, (t // 4) % 4, (t // 2) % 2, t % 2
    group = hi * 4 + b * 2 + core
    rows = 72

    def device(z, y, g):
        return (z * 16 + y * 4 + (g // 4) * 2 + g % 2, (g // 2) % 2)

    near = [device(z, y, (group + k) % 8) for k in range(1, 8)]
    along_y = [device(z, (y + k) % 4, group) for k in range(1, 4)]
    along_z = [device((z + k) % 4, y, group) for k in range(1, 4)]
    barrier = pltpu.get_barrier_semaphore()
    for other in near + along_y + along_z:
        pl.semaphore_signal(barrier, inc=1, device_id=other, device_id_type=MESH)
    pl.semaphore_wait(barrier, 13)

    def remote(src, dst, send, recv, other):
        copy = pltpu.make_async_remote_copy(
            src_ref=src, dst_ref=dst, send_sem=send, recv_sem=recv, device_id=other, device_id_type=MESH
        )
        copy.start()
        return copy

    def piece(ref, g):
        return ref.at[pl.ds(pl.multiple_of(g * rows, 8), rows)]

    copies = [
        remote(piece(x_ref, (group + k) % 8), parts.at[group], s_a.at[k - 1], r_a.at[k - 1], near[k - 1])
        for k in range(1, 8)
    ]
    parts[group] = x_ref[pl.ds(pl.multiple_of(group * rows, 8), rows), :]
    for copy in copies:
        copy.wait_recv()
    total = parts[0]
    for g in range(1, 8):
        total = total + parts[g]
    for ref, me, others, send, recv in ((ys, y, along_y, s_y, r_y), (zs, z, along_z, s_z, r_z)):
        ref[me] = total
        step = [remote(ref.at[me], ref.at[me], send.at[k], recv.at[k], others[k]) for k in range(3)]
        for copy in step:
            copy.wait_recv()
        total = ((ref[0] + ref[1]) + ref[2]) + ref[3]
        copies += step
    mine[...] = total
    last = [remote(mine, piece(out, group), s_g.at[k], r_g.at[k], near[k]) for k in range(7)]
    out[pl.ds(pl.multiple_of(group * rows, 8), rows), :] = total
    for copy in last:
        copy.wait_recv()
    for copy in copies + last:
        copy.wait_send()


def total(x, ident):
    sem = pltpu.SemaphoreType.DMA
    return pl.pallas_call(
        total_kernel,
        out_shape=jax.ShapeDtypeStruct((576, 128), F32),
        in_specs=[VM],
        out_specs=VM,
        scratch_shapes=[
            pltpu.VMEM((72, 128), F32),
            pltpu.VMEM((8, 72, 128), F32),
            pltpu.VMEM((4, 72, 128), F32),
            pltpu.VMEM((4, 72, 128), F32),
            sem((7,)), sem((7,)), sem((3,)), sem((3,)), sem((3,)), sem((3,)), sem((7,)), sem((7,)),
        ],
        name="total",
        compiler_params=pltpu.CompilerParams(collective_id=ident, has_side_effects=True),
    )(x)


def body(fields, cotangent, first_kernel, second_kernel, adjacency, seam_codes, corner_map):
    f = fields.reshape(R, S * C)
    c = cotangent.reshape(R, S * C)
    tab = jnp.concatenate([adjacency.reshape(-1), seam_codes.reshape(-1), corner_map.reshape(-1)])
    corner_row = jnp.pad(corner_map.reshape(64, EDGES), ((0, 0), (0, 4)), constant_values=-1)
    corner_row = corner_row.reshape(1, 1024)
    wide = jax.ShapeDtypeStruct((R, S * C), BF)
    sent = jax.ShapeDtypeStruct((PARTS, S, 128), BF)
    sums = jax.ShapeDtypeStruct((576, 128), F32)
    params = pltpu.CompilerParams(vmem_limit_bytes=48 * 2**20)

    lines = pl.pallas_call(
        start_kernel,
        out_shape=sent,
        in_specs=[VM, VM],
        out_specs=VM,
        scratch_shapes=[
            pltpu.VMEM((PAIRS * PR, 128), F32),
            pltpu.VMEM((PAIRS * PR, 128), F32),
            pltpu.VMEM((PARTS * S, 128), F32),
        ],
        name="lines",
        compiler_params=params,
    )(f, c)
    near, cells = exchange(lines, tab, 0)
    hidden, pre_grad, grad_one, lines = pl.pallas_call(
        middle_kernel,
        out_shape=(wide, wide, sums, sent),
        in_specs=[VM] * 7 + [SM],
        out_specs=(VM,) * 4,
        scratch_shapes=CONV_SCRATCH
        + [
            pltpu.VMEM((NP * R, 128), F32),
            pltpu.VMEM((PARTS * S, 128), F32),
            pltpu.VMEM((NP * R, 128), BF),
        ],
        name="middle",
        compiler_params=params,
    )(f, c, first_kernel, second_kernel, near, cells, corner_row, tab)
    near, cells = exchange(lines, tab, 1)
    output, field_grad, grads = pl.pallas_call(
        last_kernel,
        out_shape=(wide, wide, sums),
        in_specs=[VM] * 9 + [SM, VM],
        out_specs=(VM,) * 3,
        scratch_shapes=CONV_SCRATCH + [pltpu.VMEM((NP * R, 128), BF)],
        name="last",
        compiler_params=params,
    )(hidden, pre_grad, f, c, first_kernel, second_kernel, near, cells, corner_row, tab, grad_one)
    grads = total(grads, 2)
    grad_scale = 1.0 / math.sqrt(2 * 192 * S * S)
    shape_out = (1, TL, S, S * C)
    return (
        output.reshape(shape_out),
        field_grad.reshape(shape_out),
        grads[:, :C].reshape(3, 3, C, C) * grad_scale,
        grads[:, C:].reshape(3, 3, C, C) * grad_scale,
    )


def solution(mesh):
    split = P("batch", "tile", None, None)
    return jax.shard_map(
        body,
        mesh=mesh,
        in_specs=(split, split, P(), P(), P(), P(), P()),
        out_specs=(split, split, P(), P()),
        check_vma=False,
    )
```

```python
import functools
import math

import jax
import jax.numpy as jnp
from jax import lax
from jax.experimental import pallas as pl
from jax.experimental.pallas import tpu as pltpu
from jax.sharding import PartitionSpec as P

TL = 3
S = 32
C = 64
NP = 16
R = TL * S
EDGES = TL * 4
LINES = EDGES * S
HALF = S // 2
SHARE = 9 * C // 8
PAIRS = NP + 2
PR = 128
MESH = pl.DeviceIdType.MESH
F32 = jnp.float32
BF = jnp.bfloat16
VM = pl.BlockSpec(memory_space=pltpu.VMEM)
SM = pl.BlockSpec(memory_space=pltpu.SMEM)


def rows_at(t):
    return t * 40 + 8


def low_lanes(rows):
    return lax.broadcasted_iota(jnp.int32, (rows, 128), 1) < C


def swap(v):
    return pltpu.roll(v, C, 1)


def put_lines(lines, first, second, place, out):
    low16, low32 = low_lanes(16), low_lanes(32)
    step = place(1, 0) - place(0, 0)
    for t in range(TL):
        for e, i in ((0, S - 1), (2, 0)):
            where = pl.ds(place(0, t) + i, NP, stride=step)
            a, b = first[where, :], second[where, :]
            base = (t * 4 + e) * S
            lines[pl.ds(base, NP, stride=2), :] = jnp.where(low16, a, swap(b))
            lines[pl.ds(base + 1, NP, stride=2), :] = jnp.where(low16, swap(a), b)
        for e, pair in ((1, 0), (3, NP - 1)):
            where = pl.ds(place(pair, t), S)
            a, b = first[where, :], second[where, :]
            line = jnp.where(low32, a, swap(b)) if e == 1 else jnp.where(low32, swap(a), b)
            lines[pl.ds((t * 4 + e) * S, S), :] = line
        for corner, (e, s) in enumerate(((2, 0), (2, S - 1), (0, 0), (0, S - 1))):
            lines[pl.ds(LINES + t * 4 + corner, 1), :] = lines[pl.ds((t * 4 + e) * S + s, 1), :]
    lines[pl.ds(LINES + EDGES, HALF - EDGES), :] = jnp.zeros((HALF - EDGES, 128), F32)
    for j in range(EDGES):
        for h in range(2):
            out[h * EDGES + j] = lines[pl.ds(j * S + h * HALF, HALF), :].astype(BF)
    out[2 * EDGES] = lines[pl.ds(LINES, HALF), :].astype(BF)


def fill_pad(pad, src):
    for p in (0, PAIRS - 1):
        pad[pl.ds(p * PR, PR), :] = jnp.zeros((PR, 128), F32)
    for p in range(NP):
        for t in range(TL):
            base = (p + 1) * PR + rows_at(t)
            pad[pl.ds(base - 8, 8), :] = jnp.zeros((8, 128), F32)
            pad[pl.ds(base, S), :] = src[t * S : (t + 1) * S, p * 128 : (p + 1) * 128].astype(F32)
        pad[pl.ds((p + 1) * PR + 120, 8), :] = jnp.zeros((8, 128), F32)


def pad_place(pair, t):
    return (pair + 1) * PR + rows_at(t)


def flat_place(pair, t):
    return pair * R + t * S


def make_shifts(xp, pad):
    for a in range(3):
        for p in range(PAIRS):
            for t in range(TL):
                xp[a, p, t * S : (t + 1) * S, :] = pad[pl.ds(p * PR + rows_at(t) - 1 + a, S), :].astype(BF)


def build_forward(w_out, w):
    w_out[...] = jnp.zeros_like(w_out)
    for a in range(3):
        for c in range(3):
            block = w[a, c].astype(BF)
            for n in range(4):
                m = n + 1 + c
                w_out[a, m * C : (m + 1) * C, n * C : (n + 1) * C] = block


def build_backward(w_out, w_rim, w_corner, w):
    w_out[...] = jnp.zeros_like(w_out)
    w_rim[...] = jnp.zeros_like(w_rim)
    w_corner[...] = jnp.zeros_like(w_corner)
    for a in range(3):
        for c in range(3):
            block = w[a, c].T.astype(BF)
            for n in range(4):
                m = n + 3 - c
                w_out[2 - a, m * C : (m + 1) * C, n * C : (n + 1) * C] = block
            spots = []
            if a == 2:
                spots.append((0, c))
            if c == 0:
                spots.append((1, a))
            if a == 0:
                spots.append((2, c))
            if c == 2:
                spots.append((3, a))
            for e, tap in spots:
                w_rim[tap * 128 + C : tap * 128 + 128, e * C : (e + 1) * C] = block
            if a != 1 and c != 1:
                corner = (a // 2) * 2 + c // 2
                w_corner[C:128, corner * C : (corner + 1) * C] = block


def conv(xp, w):
    total = None
    for a in range(3):
        left = jnp.concatenate(
            [
                jnp.concatenate([xp[a, 2 * q + s] for q in range(NP // 2)], axis=0)
                for s in range(4)
            ],
            axis=1,
        )
        part = jnp.dot(left, w[a], preferred_element_type=F32)
        total = part if total is None else total + part
    return total


def columns(xp, a):
    return jnp.concatenate(
        [jnp.concatenate([xp[a, d + p] for p in range(NP)], axis=0) for d in range(3)], axis=1
    )


def first_part(xp, q, a):
    out = lax.dot_general(q, columns(xp, a), (((0,), (0,)), ((), ())), preferred_element_type=F32)
    turned = jnp.concatenate([out[:, d * 128 : (d + 1) * 128].T for d in range(3)], axis=0)
    return turned[64:256] + swap(turned[128:320])


def second_part(qp, h, a):
    out = lax.dot_general(h, columns(qp, 2 - a), (((0,), (0,)), ((), ())), preferred_element_type=F32)
    even, odd = out[:C], out[C:]
    return jnp.concatenate(
        [
            even[:, 128:256] + swap(odd[:, 256:384]),
            swap(even[:, 128:256]) + odd[:, 128:256],
            even[:, :128] + swap(odd[:, 128:256]),
        ],
        axis=0,
    )


def second_rims(grad, lines, wide, corners_ref, corner_row, codes, me):
    upper = jnp.logical_not(low_lanes(C))
    kept = [lines[pl.ds(j * S, S), :].astype(BF) for j in range(EDGES)]
    ours = [line.astype(BF) for line in reverse(kept, codes)]
    zero = jnp.zeros((S, 128), BF)
    left = jnp.concatenate(
        [
            jnp.concatenate([jnp.where(codes[j] % 4 == e, ours[j], zero) for j in range(EDGES)], axis=0)
            for e in range(4)
        ],
        axis=1,
    )
    out = lax.dot_general(left, wide[...], (((0,), (0,)), ((), ())), preferred_element_type=F32)
    pixels = lines[pl.ds(LINES, 16), :].astype(BF)
    pick = picked(corner_row, me)
    kind = lax.broadcasted_iota(jnp.int32, (16, 1024), 1) % 4
    for e in range(4):
        for c in range(3):
            a, b = ((2, c), (c, 0), (0, c), (c, 2))[e]
            at = pl.ds((a * 3 + b) * C, C)
            part = out[e * 128 : e * 128 + C, c * 128 : (c + 1) * 128]
            grad[at, :] = grad[at, :] + jnp.where(upper, part, 0.0)
        chosen = jnp.where(pick & (kind == e), 1.0, 0.0).astype(BF)
        met = jnp.dot(chosen, corners_ref[...], preferred_element_type=F32).astype(BF)
        part = lax.dot_general(pixels, met, (((0,), (0,)), ((), ())), preferred_element_type=F32)
        at = pl.ds(((e // 2) * 6 + (e % 2) * 2) * C, C)
        grad[at, :] = grad[at, :] + jnp.where(upper, part[:C], 0.0)


def reverse(kept, codes):
    flip = (
        lax.broadcasted_iota(jnp.int32, (S, S), 0) + lax.broadcasted_iota(jnp.int32, (S, S), 1)
        == S - 1
    )
    flip = jnp.where(flip, 1.0, 0.0).astype(BF)
    flipped = jnp.dot(flip, jnp.concatenate(kept, axis=1), preferred_element_type=F32)
    return [
        jnp.where(codes[j] >= 4, flipped[:, j * 128 : (j + 1) * 128], kept[j].astype(F32))
        for j in range(EDGES)
    ]


def orient(lines_ref, codes, w_rim, turned, wide):
    lines = lines_ref[...].astype(F32)
    low = low_lanes(S)
    spot = lax.broadcasted_iota(jnp.int32, (LINES, 128), 0) % S
    after = jnp.where(spot == S - 1, 0.0, pltpu.roll(lines, LINES - 1, 0)).astype(BF)
    before = jnp.where(spot == 0, 0.0, pltpu.roll(lines, 1, 0)).astype(BF)
    wide[...] = jnp.concatenate([after, lines_ref[...], before], axis=1)
    rims = jnp.dot(wide[...], w_rim[...], preferred_element_type=F32)
    kept = []
    for j in range(EDGES):
        e = codes[j] % 4
        at = slice(j * S, (j + 1) * S)
        pair = jnp.where(e >= 2, rims[at, 128:], rims[at, :128])
        rim = jnp.where(e % 2 == 1, pair, swap(pair))
        kept.append(jnp.where(low, lines[at], rim).astype(BF))
    for j, line in enumerate(reverse(kept, codes)):
        turned[pl.ds(j * S, S), :] = line


def halo_in(pad, turned, cells):
    low16 = low_lanes(16)
    cells_swapped = swap(cells[...])
    for t in range(TL):
        for e, row in ((0, rows_at(t) + S), (2, rows_at(t) - 1)):
            base = (t * 4 + e) * S
            even = turned[pl.ds(base, NP, stride=2), :]
            odd = turned[pl.ds(base + 1, NP, stride=2), :]
            pad[pl.ds(PR + row, NP, stride=PR), :] = jnp.where(low16, even, swap(odd))
        pad[pl.ds(rows_at(t), S), :] = swap(turned[pl.ds((t * 4 + 1) * S, S), :])
        pad[pl.ds((PAIRS - 1) * PR + rows_at(t), S), :] = turned[pl.ds((t * 4 + 3) * S, S), :]
        for corner, (row, p) in enumerate(((-1, 0), (-1, 1), (S, 0), (S, 1))):
            at = t * 4 + corner
            value = (cells[...] if p else cells_swapped)[at : at + 1]
            pad[pl.ds(p * (PAIRS - 1) * PR + rows_at(t) + row, 1), :] = value


def picked(corner_row, me):
    slot = lax.broadcasted_iota(jnp.int32, (16, 1024), 0)
    return (corner_row[...] == me * EDGES + slot) & (slot < EDGES)


def corner_sums(corners_ref, corner_row, me, w_corner):
    every = jnp.dot(corners_ref[...], w_corner[...], preferred_element_type=F32)
    kind = lax.broadcasted_iota(jnp.int32, (1024, 128), 0) % 4
    pair = jnp.where(kind >= 2, every[:, 128:], every[:, :128])
    other = swap(pair)
    low = low_lanes(1024)
    both = jnp.where((kind % 2 == 1) == low, other, pair).astype(BF)
    pick = picked(corner_row, me)
    return jnp.dot(jnp.where(pick, 1.0, 0.0).astype(BF), both, preferred_element_type=F32)


def rims_in(back, turned, sums):
    low16, low32, low1 = low_lanes(16), low_lanes(S), low_lanes(16)
    for t in range(TL):
        for e, i in ((0, S - 1), (2, 0)):
            base = (t * 4 + e) * S
            even = turned[pl.ds(base, NP, stride=2), :]
            odd = turned[pl.ds(base + 1, NP, stride=2), :]
            at = pl.ds(t * S + i, NP, stride=R)
            back[at, :] = back[at, :] + jnp.where(low16, swap(even), odd)
        at = pl.ds(t * S, S)
        line = swap(turned[pl.ds((t * 4 + 1) * S, S), :])
        back[at, :] = back[at, :] + jnp.where(low32, line, 0.0)
        at = pl.ds((NP - 1) * R + t * S, S)
        back[at, :] = back[at, :] + jnp.where(low32, 0.0, turned[pl.ds((t * 4 + 3) * S, S), :])
    lows, highs = jnp.where(low1, sums, 0.0), jnp.where(low1, 0.0, sums)
    for t in range(TL):
        for corner, (i, p) in enumerate(((0, 0), (0, 1), (S - 1, 0), (S - 1, 1))):
            at = pl.ds(p * (NP - 1) * R + t * S + i, 1)
            s = t * 4 + corner
            back[at, :] = back[at, :] + (highs if p else lows)[s : s + 1]


def both_convs(
    x_ref, q_ref, wf_ref, wb_ref, lines_ref, corners_ref, corner_row, tab, places,
    pad, xp, qp, w_conv, w_rim, w_corner, turned, wide, cells_all, cells, main, back,
):
    me = lax.axis_index("tile")
    codes = [tab[me * EDGES + j] // 2**21 for j in range(EDGES)]
    build_backward(w_conv, w_rim, w_corner, wb_ref)
    fill_pad(pad, q_ref)
    make_shifts(qp, pad)
    out = conv(qp, w_conv)
    for q in range(NP // 2):
        for half in range(2):
            back[pl.ds((2 * q + half) * R, R), :] = out[q * R : (q + 1) * R, half * 128 : (half + 1) * 128]
    orient(lines_ref, codes, w_rim, turned, wide)
    sums = corner_sums(corners_ref, corner_row, me, w_corner)
    rims_in(back, turned, sums)
    cells_all[...] = corners_ref[...].astype(F32)
    for s in range(EDGES):
        v = places[me * EDGES + s]
        tile = v // 4
        device = tile // 3
        row = device * 16 + (tile - device * 3) * 4 + v % 4
        cells[pl.ds(s, 1), :] = cells_all[pl.ds(row, 1), :]
    cells[pl.ds(EDGES, 4), :] = jnp.zeros((4, 128), F32)
    fill_pad(pad, x_ref)
    halo_in(pad, turned, cells)
    make_shifts(xp, pad)
    build_forward(w_conv, wf_ref)
    main[...] = conv(xp, w_conv)


CONV_SCRATCH = [
    pltpu.VMEM((PAIRS * PR, 128), F32),
    pltpu.VMEM((3, PAIRS, R, 128), BF),
    pltpu.VMEM((3, PAIRS, R, 128), BF),
    pltpu.VMEM((3, 512, 256), BF),
    pltpu.VMEM((384, 256), BF),
    pltpu.VMEM((128, 256), BF),
    pltpu.VMEM((LINES, 128), F32),
    pltpu.VMEM((LINES, 384), BF),
    pltpu.VMEM((1024, 128), F32),
    pltpu.VMEM((16, 128), F32),
    pltpu.VMEM((NP // 2 * R, 256), F32),
    pltpu.VMEM((NP * R, 128), F32),
]


def start_kernel(f_ref, c_ref, out, pad_a, pad_b, lines):
    fill_pad(pad_a, f_ref)
    fill_pad(pad_b, c_ref)
    put_lines(lines, pad_a, pad_b, pad_place, out)


def middle_kernel(
    f_ref, c_ref, w1_ref, w2_ref, lines_ref, corners_ref, corner_row, tab, places,
    hidden, pre_grad, grad, out,
    pad, xp, qp, w_conv, w_rim, w_corner, turned, wide, cells_all, cells, main, back, hid, lines, grads, hids,
):
    both_convs(
        f_ref, c_ref, w1_ref, w2_ref, lines_ref, corners_ref, corner_row, tab, places,
        pad, xp, qp, w_conv, w_rim, w_corner, turned, wide, cells_all, cells, main, back,
    )
    for p in range(NP):
        pre = main[pl.ds((p // 2) * R, R), (p % 2) * 128 : (p % 2) * 128 + 128]
        at = pl.ds(p * R, R)
        s = 1.0 / (1.0 + jnp.exp(-pre))
        h = (pre * s).astype(BF)
        g = (back[at, :] * s * (1.0 + pre * (1.0 - s))).astype(BF)
        hidden[:, p * 128 : (p + 1) * 128] = h
        pre_grad[:, p * 128 : (p + 1) * 128] = g
        hid[at, :] = h.astype(F32)
        back[at, :] = g.astype(F32)
        grads[at, :] = g
        hids[at, :] = h
    put_lines(lines, hid, back, flat_place, out)
    low = low_lanes(192)
    for a in range(3):
        grad[pl.ds(a * 192, 192), :] = jnp.where(
            low, first_part(xp, grads[...], a), second_part(qp, hids[...], a)
        )
    me = lax.axis_index("tile")
    codes = [tab[me * EDGES + j] // 2**21 for j in range(EDGES)]
    second_rims(grad, lines, wide, corners_ref, corner_row, codes, me)


def last_kernel(
    h_ref, g_ref, f_ref, c_ref, w1_ref, w2_ref, lines_ref, corners_ref, corner_row, tab, places, grads_ref,
    output, field_grad, grad_one, grad_two,
    pad, xp, qp, w_conv, w_rim, w_corner, turned, wide, cells_all, cells, main, back,
):
    both_convs(
        h_ref, g_ref, w2_ref, w1_ref, lines_ref, corners_ref, corner_row, tab, places,
        pad, xp, qp, w_conv, w_rim, w_corner, turned, wide, cells_all, cells, main, back,
    )
    for p in range(NP):
        at, lanes = pl.ds(p * R, R), slice(p * 128, (p + 1) * 128)
        made = main[pl.ds((p // 2) * R, R), (p % 2) * 128 : (p % 2) * 128 + 128]
        output[:, lanes] = (f_ref[:, lanes].astype(F32) + made).astype(BF)
        field_grad[:, lanes] = (c_ref[:, lanes].astype(F32) + back[at, :]).astype(BF)
    scale = 1.0 / math.sqrt(2 * 192 * S * S)
    grad_one[...] = grads_ref[:, :C] * scale
    grad_two[...] = grads_ref[:, C:] * scale


def exchange_kernel(with_total, x_ref, tab, *refs):
    t = lax.axis_index("tile")
    b = lax.axis_index("batch")
    z, y, x, core = t // 16, (t // 4) % 4, (t // 2) % 2, t % 2

    def index(z, y, x, core):
        return z * 16 + y * 4 + x * 2 + core

    if with_total:
        grads, out_lines, out_corners, out_grads, *refs = refs
        summed, parts, by_y, by_z, *refs = refs
    else:
        out_lines, out_corners, *refs = refs
    held_a, held_b, chosen, got_a, got_b, crossing, crossed, cells, sent, come = refs
    held, got = (held_a, held_b), (got_a, got_b)

    along_z = [(index((z + k) % 4, y, x, core), b) for k in range(1, 4)]
    along_y = [(index(z, (y + k) % 4, x, core), b) for k in range(1, 4)]
    sibling = (index(z, y, x, 1 - core), b)
    across = (index(z, y, 1 - x, core), b)
    group = x * 4 + b * 2 + core
    near = []
    for k in range(1, 8):
        g = (group + k) % 8
        near.append((index(z, y, g // 4, g % 2), (g // 2) % 2))
    partners = along_z + along_y + (near if with_total else [sibling, across])
    barrier = pltpu.get_barrier_semaphore()
    for other in partners:
        pl.semaphore_signal(barrier, inc=1, device_id=other, device_id_type=MESH)
    pl.semaphore_wait(barrier, len(partners))

    copies = []

    def remote(src, dst, other):
        n = len(copies)
        copy = pltpu.make_async_remote_copy(
            src_ref=src, dst_ref=dst, send_sem=sent.at[n], recv_sem=come.at[n],
            device_id=other, device_id_type=MESH,
        )
        copy.start()
        copies.append(copy)
        return copy

    def piece(ref, g):
        return ref.at[pl.ds(pl.multiple_of(g * SHARE, 8), SHARE)]

    chains = ((z, y, along_z, along_y), (y, z, along_y, along_z))
    first, over = [], []
    for h, (p, _, others, _) in enumerate(chains):
        mine = x_ref.at[pl.ds(h * EDGES, EDGES)]
        place = held[h].at[pl.ds((p * 2 + core) * EDGES, EDGES)]
        first.append([remote(mine, place, other) for other in others])
        over.append([remote(mine, place, sibling)])
        held[h][pl.ds((p * 2 + core) * EDGES, EDGES)] = x_ref[pl.ds(h * EDGES, EDGES)]
    cell = ((core * 4 + y) * 4 + z) * 2
    cells[cell + x] = x_ref[2 * EDGES]
    cell_x = remote(x_ref.at[2 * EDGES], cells.at[cell + x], across)
    if with_total:
        scatter = [
            remote(piece(grads, (group + k) % 8), parts.at[group], near[k - 1]) for k in range(1, 8)
        ]
        parts[group] = grads[pl.ds(pl.multiple_of(group * SHARE, 8), SHARE), :]
    for k in range(3):
        for h, (p, _, _, _) in enumerate(chains):
            first[h][k].wait_recv()
            here = held[h].at[pl.ds((((p + 3 - k) % 4) * 2 + core) * EDGES, EDGES)]
            over[h].append(remote(here, here, sibling))
    cell_x.wait_recv()
    here = cells.at[pl.ds(cell, 2)]
    cell_z = [remote(here, here, other) for other in along_z]

    second = []
    for h, (p, q, _, others) in enumerate(chains):
        for copy in over[h]:
            copy.wait_recv()
        second.append([])
        for k in range(4):
            to = (q + k) % 4
            base = (index(z, to, 0, core) if h == 0 else index(to, y, 0, core)) * EDGES

            def take(j, _, h=h, k=k, base=base):
                for side in range(2):
                    line = held[h][(tab[base + side * 2 * EDGES + j] >> (8 * h)) & 255]
                    chosen[h, k, side * EDGES + j] = line
                return 0

            lax.fori_loop(0, EDGES, take, 0)
            place = got[h].at[pl.ds(q * 2 * EDGES, 2 * EDGES)]
            if k:
                second[h].append(remote(chosen.at[h, k], place, others[k - 1]))
            else:
                got[h][pl.ds(q * 2 * EDGES, 2 * EDGES)] = chosen[h, 0]
    if with_total:
        for copy in scatter:
            copy.wait_recv()
        total = parts[0]
        for g in range(1, 8):
            total = total + parts[g]
        by_y[y] = total
        add_y = [remote(by_y.at[y], by_y.at[y], other) for other in along_y]
    for copy in cell_z:
        copy.wait_recv()
    here = cells.at[pl.ds((core * 4 + y) * 8, 8)]
    cell_y = [remote(here, here, other) for other in along_y]

    if with_total:
        for copy in add_y:
            copy.wait_recv()
        by_z[z] = ((by_y[0] + by_y[1]) + by_y[2]) + by_y[3]
        add_z = [remote(by_z.at[z], by_z.at[z], other) for other in along_z]

    third = []
    base = index(z, y, 1 - x, core) * EDGES
    for h in range(2):
        for copy in second[h]:
            copy.wait_recv()

        def pass_on(j, _, h=h):
            crossing[h, j] = got[h][((tab[base + j] >> (16 + 2 * h)) & 3) * (2 * EDGES) + (1 - x) * EDGES + j]
            return 0

        lax.fori_loop(0, EDGES, pass_on, 0)
        third.append(remote(crossing.at[h], crossed.at[h], across))
    if with_total:
        for copy in add_z:
            copy.wait_recv()
        total = ((by_z[0] + by_z[1]) + by_z[2]) + by_z[3]
        summed[...] = total
        out_grads[pl.ds(pl.multiple_of(group * SHARE, 8), SHARE), :] = total
        gather = [remote(summed, piece(out_grads, group), other) for other in near]
    for copy in cell_y:
        copy.wait_recv()
    here = cells.at[pl.ds(core * 32, 32)]
    last = remote(here, here, sibling)

    for h in range(2):
        third[h].wait_recv()

        def give(j, _, h=h):
            entry = tab[t * EDGES + j]
            straight = got[h][((entry >> (16 + 2 * h)) & 3) * (2 * EDGES) + x * EDGES + j]
            near = ((entry >> 20) & 1) == x
            at = pl.ds(pl.multiple_of(j * S + h * HALF, HALF), HALF)
            out_lines[at, :] = jnp.where(near, straight, crossed[h, j])
            return 0

        lax.fori_loop(0, EDGES, give, 0)
    last.wait_recv()
    for d in range(64):
        out_corners[d * HALF : (d + 1) * HALF, :] = cells[
            (((d % 2) * 4 + (d // 4) % 4) * 4 + d // 16) * 2 + (d // 2) % 2
        ]
    if with_total:
        for copy in gather:
            copy.wait_recv()
    for copy in copies:
        copy.wait_send()


def exchange(lines, tab, ident, grads=None):
    n = 6 + 2 + 1 + 6 + 3 + 6 + 3 + 2 + 1
    outs = [jax.ShapeDtypeStruct((LINES, 128), BF), jax.ShapeDtypeStruct((1024, 128), BF)]
    scratch = []
    if grads is not None:
        n += 7 + 3 + 3 + 7
        outs.append(jax.ShapeDtypeStruct((8 * SHARE, 128), F32))
        scratch = [pltpu.VMEM((k, SHARE, 128), F32) for k in (8, 4, 4)]
        scratch = [pltpu.VMEM((SHARE, 128), F32)] + scratch
    return pl.pallas_call(
        functools.partial(exchange_kernel, grads is not None),
        out_shape=tuple(outs),
        in_specs=[VM, SM] + [VM] * len(outs[2:]),
        out_specs=(VM,) * len(outs),
        scratch_shapes=scratch
        + [
            pltpu.VMEM((8 * EDGES, HALF, 128), BF),
            pltpu.VMEM((8 * EDGES, HALF, 128), BF),
            pltpu.VMEM((2, 4, 2 * EDGES, HALF, 128), BF),
            pltpu.VMEM((8 * EDGES, HALF, 128), BF),
            pltpu.VMEM((8 * EDGES, HALF, 128), BF),
            pltpu.VMEM((2, EDGES, HALF, 128), BF),
            pltpu.VMEM((2, EDGES, HALF, 128), BF),
            pltpu.VMEM((64, HALF, 128), BF),
            pltpu.SemaphoreType.DMA((n,)),
            pltpu.SemaphoreType.DMA((n,)),
        ],
        name="exchange_and_total" if scratch else "exchange",
        compiler_params=pltpu.CompilerParams(
            collective_id=ident, has_side_effects=True, vmem_limit_bytes=40 * 2**20
        ),
    )(lines, tab, *([] if grads is None else [grads]))


def tables(adjacency, seam_codes):
    source, tile = adjacency // TL, adjacency % TL
    line = tile * 4 + seam_codes % 4
    z, y, x, core = source // 16, (source // 4) % 4, (source // 2) % 2, source % 2
    by_z, by_y = (z * 2 + core) * EDGES + line, (y * 2 + core) * EDGES + line
    return by_z + by_y * 2**8 + y * 2**16 + z * 2**18 + x * 2**20 + seam_codes * 2**21


def body(fields, cotangent, first_kernel, second_kernel, adjacency, seam_codes, corner_map):
    f = fields.reshape(R, S * C)
    c = cotangent.reshape(R, S * C)
    tab = tables(adjacency, seam_codes).reshape(768)
    places = corner_map.reshape(768)
    corner_row = jnp.pad(corner_map.reshape(64, EDGES), ((0, 0), (0, 4)), constant_values=-1)
    corner_row = corner_row.reshape(1, 1024)
    wide = jax.ShapeDtypeStruct((R, S * C), BF)
    sent = jax.ShapeDtypeStruct((2 * EDGES + 1, HALF, 128), BF)
    sums = jax.ShapeDtypeStruct((576, 128), F32)
    params = pltpu.CompilerParams(vmem_limit_bytes=48 * 2**20)

    lines = pl.pallas_call(
        start_kernel,
        out_shape=sent,
        in_specs=[VM, VM],
        out_specs=VM,
        scratch_shapes=[
            pltpu.VMEM((PAIRS * PR, 128), F32),
            pltpu.VMEM((PAIRS * PR, 128), F32),
            pltpu.VMEM((LINES + HALF, 128), F32),
        ],
        name="lines",
        compiler_params=params,
    )(f, c)
    near, cells = exchange(lines, tab, 0)
    hidden, pre_grad, grads, lines = pl.pallas_call(
        middle_kernel,
        out_shape=(wide, wide, sums, sent),
        in_specs=[VM] * 7 + [SM, SM],
        out_specs=(VM,) * 4,
        scratch_shapes=CONV_SCRATCH
        + [
            pltpu.VMEM((NP * R, 128), F32),
            pltpu.VMEM((LINES + HALF, 128), F32),
            pltpu.VMEM((NP * R, 128), BF),
            pltpu.VMEM((NP * R, 128), BF),
        ],
        name="middle",
        compiler_params=params,
    )(f, c, first_kernel, second_kernel, near, cells, corner_row, tab, places)
    near, cells, grads = exchange(lines, tab, 1, grads)
    kernel_sums = jax.ShapeDtypeStruct((9 * C, C), F32)
    output, field_grad, grad_one, grad_two = pl.pallas_call(
        last_kernel,
        out_shape=(wide, wide, kernel_sums, kernel_sums),
        in_specs=[VM] * 9 + [SM, SM, VM],
        out_specs=(VM,) * 4,
        scratch_shapes=CONV_SCRATCH,
        name="last",
        compiler_params=params,
    )(hidden, pre_grad, f, c, first_kernel, second_kernel, near, cells, corner_row, tab, places, grads)
    shape_out = (1, TL, S, S * C)
    return (
        output.reshape(shape_out),
        field_grad.reshape(shape_out),
        grad_one.reshape(3, 3, C, C),
        grad_two.reshape(3, 3, C, C),
    )


def solution(mesh):
    split = P("batch", "tile", None, None)
    return jax.shard_map(
        body,
        mesh=mesh,
        in_specs=(split, split, P(), P(), P(), P(), P()),
        out_specs=(split, split, P(), P()),
        check_vma=False,
    )
```

```python
import math

import jax
import jax.numpy as jnp
from jax import lax
from jax.experimental import pallas as pl
from jax.experimental.pallas import tpu as pltpu
from jax.sharding import PartitionSpec as P

TL = 3
S = 32
C = 64
NP = 16
R = TL * S
EDGES = TL * 4
LINES = EDGES * S
HALF = S // 2
SHARE = 9 * C // 8
PAIRS = NP + 2
PR = 128
MESH = pl.DeviceIdType.MESH
F32 = jnp.float32
BF = jnp.bfloat16
VM = pl.BlockSpec(memory_space=pltpu.VMEM)


def rows_at(t):
    return t * 40 + 8


def low_lanes(rows):
    return lax.broadcasted_iota(jnp.int32, (rows, 128), 1) < C


def swap(v):
    return pltpu.roll(v, C, 1)


def put_lines(lines, first, second, place, out):
    low16, low32 = low_lanes(16), low_lanes(32)
    step = place(1, 0) - place(0, 0)
    for t in range(TL):
        for e, i in ((0, S - 1), (2, 0)):
            where = pl.ds(place(0, t) + i, NP, stride=step)
            a, b = first[where, :], second[where, :]
            base = (t * 4 + e) * S
            lines[pl.ds(base, NP, stride=2), :] = jnp.where(low16, a, swap(b))
            lines[pl.ds(base + 1, NP, stride=2), :] = jnp.where(low16, swap(a), b)
        for e, pair in ((1, 0), (3, NP - 1)):
            where = pl.ds(place(pair, t), S)
            a, b = first[where, :], second[where, :]
            line = jnp.where(low32, a, swap(b)) if e == 1 else jnp.where(low32, swap(a), b)
            lines[pl.ds((t * 4 + e) * S, S), :] = line
        for corner, (e, s) in enumerate(((2, 0), (2, S - 1), (0, 0), (0, S - 1))):
            lines[pl.ds(LINES + t * 4 + corner, 1), :] = lines[pl.ds((t * 4 + e) * S + s, 1), :]
    lines[pl.ds(LINES + EDGES, HALF - EDGES), :] = jnp.zeros((HALF - EDGES, 128), F32)
    for j in range(EDGES):
        for h in range(2):
            out[h * EDGES + j] = lines[pl.ds(j * S + h * HALF, HALF), :].astype(BF)
    out[2 * EDGES] = lines[pl.ds(LINES, HALF), :].astype(BF)


def fill_pad(pad, src):
    for p in (0, PAIRS - 1):
        pad[pl.ds(p * PR, PR), :] = jnp.zeros((PR, 128), F32)
    for p in range(NP):
        for t in range(TL):
            base = (p + 1) * PR + rows_at(t)
            pad[pl.ds(base - 8, 8), :] = jnp.zeros((8, 128), F32)
            pad[pl.ds(base, S), :] = src[t * S : (t + 1) * S, p * 128 : (p + 1) * 128].astype(F32)
        pad[pl.ds((p + 1) * PR + 120, 8), :] = jnp.zeros((8, 128), F32)


def pad_place(pair, t):
    return (pair + 1) * PR + rows_at(t)


def flat_place(pair, t):
    return pair * R + t * S


def make_shifts(xp, pad):
    for a in range(3):
        for p in range(PAIRS):
            for t in range(TL):
                xp[a, p, t * S : (t + 1) * S, :] = pad[pl.ds(p * PR + rows_at(t) - 1 + a, S), :].astype(BF)


def build_forward(w_out, w):
    w_out[...] = jnp.zeros_like(w_out)
    for a in range(3):
        for c in range(3):
            block = w[a, c].astype(BF)
            for n in range(4):
                m = n + 1 + c
                w_out[a, m * C : (m + 1) * C, n * C : (n + 1) * C] = block


def build_backward(w_out, w_rim, w_corner, w):
    w_out[...] = jnp.zeros_like(w_out)
    w_rim[...] = jnp.zeros_like(w_rim)
    w_corner[...] = jnp.zeros_like(w_corner)
    for a in range(3):
        for c in range(3):
            block = w[a, c].T.astype(BF)
            for n in range(4):
                m = n + 3 - c
                w_out[2 - a, m * C : (m + 1) * C, n * C : (n + 1) * C] = block
            spots = []
            if a == 2:
                spots.append((0, c))
            if c == 0:
                spots.append((1, a))
            if a == 0:
                spots.append((2, c))
            if c == 2:
                spots.append((3, a))
            for e, tap in spots:
                w_rim[tap * 128 + C : tap * 128 + 128, e * C : (e + 1) * C] = block
            if a != 1 and c != 1:
                corner = (a // 2) * 2 + c // 2
                for half in range(2):
                    w_corner[C:128, corner * 128 + half * C : corner * 128 + (half + 1) * C] = block


def conv(xp, w):
    total = None
    for a in range(3):
        left = jnp.concatenate(
            [
                jnp.concatenate([xp[a, 2 * q + s] for q in range(NP // 2)], axis=0)
                for s in range(4)
            ],
            axis=1,
        )
        part = jnp.dot(left, w[a], preferred_element_type=F32)
        total = part if total is None else total + part
    return total


def columns(xp, a):
    return jnp.concatenate(
        [jnp.concatenate([xp[a, d + p] for p in range(NP)], axis=0) for d in range(3)], axis=1
    )


def first_part(xp, q, a):
    out = lax.dot_general(q, columns(xp, a), (((0,), (0,)), ((), ())), preferred_element_type=F32)
    turned = jnp.concatenate([out[:, d * 128 : (d + 1) * 128].T for d in range(3)], axis=0)
    return turned[64:256] + swap(turned[128:320])


def second_part(qp, h, a):
    out = lax.dot_general(h, columns(qp, 2 - a), (((0,), (0,)), ((), ())), preferred_element_type=F32)
    even, odd = out[:C], out[C:]
    return jnp.concatenate(
        [
            even[:, 128:256] + swap(odd[:, 256:384]),
            swap(even[:, 128:256]) + odd[:, 128:256],
            even[:, :128] + swap(odd[:, 128:256]),
        ],
        axis=0,
    )


def second_rims(grad, lines, wide, corners_ref, corner_rows, codes, me):
    upper = jnp.logical_not(low_lanes(C))
    kept = [lines[pl.ds(j * S, S), :].astype(BF) for j in range(EDGES)]
    ours = [line.astype(BF) for line in reverse(kept, codes)]
    zero = jnp.zeros((S, 128), BF)
    left = jnp.concatenate(
        [
            jnp.concatenate([jnp.where(codes[j] % 4 == e, ours[j], zero) for j in range(EDGES)], axis=0)
            for e in range(4)
        ],
        axis=1,
    )
    out = lax.dot_general(left, wide[...], (((0,), (0,)), ((), ())), preferred_element_type=F32)
    pixels = lines[pl.ds(LINES, 16), :].astype(BF)
    for e in range(4):
        for c in range(3):
            a, b = ((2, c), (c, 0), (0, c), (c, 2))[e]
            at = pl.ds((a * 3 + b) * C, C)
            part = out[e * 128 : e * 128 + C, c * 128 : (c + 1) * 128]
            grad[at, :] = grad[at, :] + jnp.where(upper, part, 0.0)
        met = jnp.dot(
            picked(corner_rows, me, e), corners_ref[pl.ds(e * 256, 256), :], preferred_element_type=F32
        ).astype(BF)
        part = lax.dot_general(pixels, met, (((0,), (0,)), ((), ())), preferred_element_type=F32)
        at = pl.ds(((e // 2) * 6 + (e % 2) * 2) * C, C)
        grad[at, :] = grad[at, :] + jnp.where(upper, part[:C], 0.0)


def reverse(kept, codes):
    flip = (
        lax.broadcasted_iota(jnp.int32, (S, S), 0) + lax.broadcasted_iota(jnp.int32, (S, S), 1)
        == S - 1
    )
    flip = jnp.where(flip, 1.0, 0.0).astype(BF)
    flipped = jnp.dot(flip, jnp.concatenate(kept, axis=1), preferred_element_type=F32)
    return [
        jnp.where(codes[j] >= 4, flipped[:, j * 128 : (j + 1) * 128], kept[j].astype(F32))
        for j in range(EDGES)
    ]


def orient(lines_ref, codes, w_rim, turned, wide):
    lines = lines_ref[...].astype(F32)
    low = low_lanes(S)
    spot = lax.broadcasted_iota(jnp.int32, (LINES, 128), 0) % S
    after = jnp.where(spot == S - 1, 0.0, pltpu.roll(lines, LINES - 1, 0)).astype(BF)
    before = jnp.where(spot == 0, 0.0, pltpu.roll(lines, 1, 0)).astype(BF)
    wide[...] = jnp.concatenate([after, lines_ref[...], before], axis=1)
    rims = jnp.dot(wide[...], w_rim[...], preferred_element_type=F32)
    kept = []
    for j in range(EDGES):
        e = codes[j] % 4
        at = slice(j * S, (j + 1) * S)
        pair = jnp.where(e >= 2, rims[at, 128:], rims[at, :128])
        rim = jnp.where(e % 2 == 1, pair, swap(pair))
        kept.append(jnp.where(low, lines[at], rim).astype(BF))
    for j, line in enumerate(reverse(kept, codes)):
        turned[pl.ds(j * S, S), :] = line


def halo_in(pad, turned, cells):
    low16 = low_lanes(16)
    cells_swapped = swap(cells[...])
    for t in range(TL):
        for e, row in ((0, rows_at(t) + S), (2, rows_at(t) - 1)):
            base = (t * 4 + e) * S
            even = turned[pl.ds(base, NP, stride=2), :]
            odd = turned[pl.ds(base + 1, NP, stride=2), :]
            pad[pl.ds(PR + row, NP, stride=PR), :] = jnp.where(low16, even, swap(odd))
        pad[pl.ds(rows_at(t), S), :] = swap(turned[pl.ds((t * 4 + 1) * S, S), :])
        pad[pl.ds((PAIRS - 1) * PR + rows_at(t), S), :] = turned[pl.ds((t * 4 + 3) * S, S), :]
        for corner, (row, p) in enumerate(((-1, 0), (-1, 1), (S, 0), (S, 1))):
            at = t * 4 + corner
            value = (cells[...] if p else cells_swapped)[at : at + 1]
            pad[pl.ds(p * (PAIRS - 1) * PR + rows_at(t) + row, 1), :] = value


def picked(corner_rows, me, kind):
    slot = lax.broadcasted_iota(jnp.int32, (16, 256), 0)
    pick = (corner_rows[kind : kind + 1, :] == me * EDGES + slot) & (slot < EDGES)
    return jnp.where(pick, 1.0, 0.0).astype(BF)


def corner_sums(corners_ref, corner_rows, me, w_corner):
    total = None
    for kind in range(4):
        rim = jnp.dot(
            corners_ref[pl.ds(kind * 256, 256), :],
            w_corner[:, kind * 128 : (kind + 1) * 128],
            preferred_element_type=F32,
        ).astype(BF)
        part = jnp.dot(picked(corner_rows, me, kind), rim, preferred_element_type=F32)
        total = part if total is None else total + part
    return total


def rims_in(back, turned, sums):
    low16, low32, low1 = low_lanes(16), low_lanes(S), low_lanes(16)
    for t in range(TL):
        for e, i in ((0, S - 1), (2, 0)):
            base = (t * 4 + e) * S
            even = turned[pl.ds(base, NP, stride=2), :]
            odd = turned[pl.ds(base + 1, NP, stride=2), :]
            at = pl.ds(t * S + i, NP, stride=R)
            back[at, :] = back[at, :] + jnp.where(low16, swap(even), odd)
        at = pl.ds(t * S, S)
        line = swap(turned[pl.ds((t * 4 + 1) * S, S), :])
        back[at, :] = back[at, :] + jnp.where(low32, line, 0.0)
        at = pl.ds((NP - 1) * R + t * S, S)
        back[at, :] = back[at, :] + jnp.where(low32, 0.0, turned[pl.ds((t * 4 + 3) * S, S), :])
    lows, highs = jnp.where(low1, sums, 0.0), jnp.where(low1, 0.0, sums)
    for t in range(TL):
        for corner, (i, p) in enumerate(((0, 0), (0, 1), (S - 1, 0), (S - 1, 1))):
            at = pl.ds(p * (NP - 1) * R + t * S + i, 1)
            s = t * 4 + corner
            back[at, :] = back[at, :] + (highs if p else lows)[s : s + 1]


def cells_of(corners_ref, places, me):
    slot = lax.broadcasted_iota(jnp.int32, (16, 1024), 0)
    row = jnp.full((16, 1024), -1, jnp.int32)
    for s in range(EDGES):
        v = places[s % 4, me * TL + s // 4]
        row = jnp.where(slot == s, (v & 3) * 256 + (v >> 2), row)
    pick = jnp.where(lax.broadcasted_iota(jnp.int32, (16, 1024), 1) == row, 1.0, 0.0).astype(BF)
    return jnp.dot(pick, corners_ref[...], preferred_element_type=F32)


def codes_of(seams, me):
    return [seams[j % 4, me * TL + j // 4] for j in range(EDGES)]


def load_rows(corner_rows, rows):
    corner_rows[...] = jnp.full((8, 256), -1, jnp.int32)
    corner_rows[0:4, 0:192] = rows[...]


def put_back(back, out):
    for q in range(NP // 2):
        for half in range(2):
            back[pl.ds((2 * q + half) * R, R), :] = out[q * R : (q + 1) * R, half * 128 : (half + 1) * 128]


def first_kernel_body(
    f_hbm, c_hbm, w1_hbm, w2_hbm, adjacency_hbm, seams_hbm, places_hbm,
    hidden_hbm, back_hbm, w_rim_two, w_corner_two, near_two, corners_two, out_grads,
    f_ref, c_ref, w1_ref, w2_ref, adjacency, seams, places, rows, loads, stores, corner_rows,
    hidden, back_two, index,
    pad_f, pad_c, xp, qp, w_back, w_forth, w_rim, w_corner, turned, wide, cells, main, back,
    hid, lines, grads, hids, grad, sent_one, sent_two, near, corners, *refs,
):
    me = lax.axis_index("tile")
    inputs = [
        pltpu.make_async_copy(src, dst, loads.at[n])
        for n, (src, dst) in enumerate(
            (
                (f_hbm, f_ref), (c_hbm, c_ref), (w2_hbm, w2_ref), (w1_hbm, w1_ref),
                (adjacency_hbm, adjacency), (seams_hbm, seams), (places_hbm, places), (places_hbm, rows),
            )
        )
    ]
    for copy in inputs:
        copy.start()
    mesh = Mesh()
    mesh.greet()
    n = len(ROUND)
    one, two, rest = refs[:n], refs[n : 2 * n], refs[2 * n :]
    summed, parts, by_y, by_z, sent, come = rest
    net = Net(sent, come)
    inputs[0].wait()
    fill_pad(pad_f, f_ref)
    inputs[1].wait()
    fill_pad(pad_c, c_ref)
    put_lines(lines, pad_f, pad_c, pad_place, sent_one)
    mesh.meet()
    first = exchange_steps(mesh, net, index, sent_one, near, corners, one)
    next(first)
    for copy in inputs[4:]:
        copy.wait()
    find_index(mesh, adjacency, seams, index)
    load_rows(corner_rows, rows)
    make_shifts(qp, pad_c)
    inputs[2].wait()
    build_backward(w_back, w_rim, w_corner, w2_ref)
    next(first)
    put_back(back, conv(qp, w_back))
    next(first)
    inputs[3].wait()
    build_forward(w_forth, w1_ref)
    next(first)
    next(first)

    codes = codes_of(seams, me)
    orient(near, codes, w_rim, turned, wide)
    cells[...] = cells_of(corners, places, me)
    halo_in(pad_f, turned, cells)
    make_shifts(xp, pad_f)
    rims_in(back, turned, corner_sums(corners, corner_rows, me, w_corner))
    main[...] = conv(xp, w_forth)
    for p in range(NP):
        pre = main[pl.ds((p // 2) * R, R), (p % 2) * 128 : (p % 2) * 128 + 128]
        at = pl.ds(p * R, R)
        s = 1.0 / (1.0 + jnp.exp(-pre))
        h = (pre * s).astype(BF)
        g = (back[at, :] * s * (1.0 + pre * (1.0 - s))).astype(BF)
        hidden[:, p * 128 : (p + 1) * 128] = h
        hid[at, :] = h.astype(F32)
        back[at, :] = g.astype(F32)
        grads[at, :] = g
        hids[at, :] = h
    put_lines(lines, hid, back, flat_place, sent_two)
    second = exchange_steps(mesh, net, index, sent_two, near_two, corners_two, two)
    next(second)
    outputs = [
        pltpu.make_async_copy(hidden, hidden_hbm, stores.at[0]),
        pltpu.make_async_copy(back_two, back_hbm, stores.at[1]),
    ]
    outputs[0].start()

    low = low_lanes(192)
    for a in range(3):
        grad[pl.ds(a * 192, 192), :] = jnp.where(
            low, first_part(xp, grads[...], a), second_part(qp, hids[...], a)
        )
    second_rims(grad, lines, wide, corners, corner_rows, codes, me)
    adding = total_steps(mesh, net, grad, out_grads, summed, parts, by_y, by_z)
    next(adding)
    next(second)
    for p in range(NP):
        for t in range(TL):
            pad_c[pl.ds(pad_place(p, t), S), :] = back[pl.ds(flat_place(p, t), S), :]
    build_backward(w_back, w_rim_two, w_corner_two, w1_ref)
    next(second)
    make_shifts(qp, pad_c)
    next(adding)
    put_back(back_two, conv(qp, w_back))
    outputs[1].start()
    next(second)
    next(adding)
    next(adding)
    next(second)
    next(adding)
    net.finish()
    for copy in outputs:
        copy.wait()


def last_kernel_body(
    h_hbm, back_hbm, f_ref, c_ref, w2_ref, w_rim, w_corner, near, corners, seams_hbm, places_hbm, grads,
    output, field_grad, grad_one, grad_two,
    h_ref, back, seams, places, rows, loads, corner_rows, pad, xp, w_forth, turned, wide, cells, main,
):
    me = lax.axis_index("tile")
    inputs = [
        pltpu.make_async_copy(src, dst, loads.at[n])
        for n, (src, dst) in enumerate(
            (
                (seams_hbm, seams), (places_hbm, places), (places_hbm, rows), (h_hbm, h_ref),
                (back_hbm, back),
            )
        )
    ]
    for copy in inputs:
        copy.start()
    build_forward(w_forth, w2_ref)
    for copy in inputs:
        copy.wait()
    load_rows(corner_rows, rows)
    orient(near, codes_of(seams, me), w_rim, turned, wide)
    cells[...] = cells_of(corners, places, me)
    fill_pad(pad, h_ref)
    halo_in(pad, turned, cells)
    make_shifts(xp, pad)
    main[...] = conv(xp, w_forth)
    rims_in(back, turned, corner_sums(corners, corner_rows, me, w_corner))
    for p in range(NP):
        at, lanes = pl.ds(p * R, R), slice(p * 128, (p + 1) * 128)
        made = main[pl.ds((p // 2) * R, R), (p % 2) * 128 : (p % 2) * 128 + 128]
        output[:, lanes] = (f_ref[:, lanes].astype(F32) + made).astype(BF)
        field_grad[:, lanes] = (c_ref[:, lanes].astype(F32) + back[at, :]).astype(BF)
    scale = 1.0 / math.sqrt(2 * 192 * S * S)
    grad_one[...] = grads[:, :C] * scale
    grad_two[...] = grads[:, C:] * scale


class Mesh:
    def __init__(self):
        self.t = t = lax.axis_index("tile")
        self.b = b = lax.axis_index("batch")
        self.z, self.y, self.x, self.core = z, y, x, core = t // 16, (t // 4) % 4, (t // 2) % 2, t % 2
        self.along_z = [(self.index((z + k) % 4, y, x, core), b) for k in range(1, 4)]
        self.along_y = [(self.index(z, (y + k) % 4, x, core), b) for k in range(1, 4)]
        self.sibling = (self.index(z, y, x, 1 - core), b)
        self.across = (self.index(z, y, 1 - x, core), b)
        self.group = x * 4 + b * 2 + core
        self.near = []
        for k in range(1, 8):
            g = (self.group + k) % 8
            self.near.append((self.index(z, y, g // 4, g % 2), (g // 2) % 2))

    def index(self, z, y, x, core):
        return z * 16 + y * 4 + x * 2 + core

    def greet(self):
        for other in self.along_z + self.along_y + self.near:
            pl.semaphore_signal(
                pltpu.get_barrier_semaphore(), inc=1, device_id=other, device_id_type=MESH
            )

    def meet(self):
        pl.semaphore_wait(pltpu.get_barrier_semaphore(), 13)


class Net:
    def __init__(self, sent, come):
        self.sent, self.come, self.copies = sent, come, []

    def send(self, src, dst, other):
        n = len(self.copies)
        copy = pltpu.make_async_remote_copy(
            src_ref=src, dst_ref=dst, send_sem=self.sent.at[n], recv_sem=self.come.at[n],
            device_id=other, device_id_type=MESH,
        )
        copy.start()
        self.copies.append(copy)
        return copy

    def finish(self):
        for copy in self.copies:
            copy.wait_send()


def find_index(mesh, adjacency, seams, index):
    z, y, x, core = mesh.z, mesh.y, mesh.x, mesh.core

    def decode(device, j):
        tile, code = adjacency[j % 4, device * TL + j // 4], seams[j % 4, device * TL + j // 4]
        source = (tile * 171) >> 9
        return source, (tile - source * 3) * 4 + (code & 3)

    for h in range(2):
        for k in range(4):
            for side in range(2):
                device = (
                    mesh.index(z, (y + k) % 4, side, core) if h == 0 else mesh.index((z + k) % 4, y, side, core)
                )
                for j in range(EDGES):
                    source, line = decode(device, j)
                    p = (source >> 4) if h == 0 else ((source >> 2) & 3)
                    index[(h * 4 + k) * 24 + side * 12 + j] = (p * 2 + (source & 1)) * EDGES + line
    for j in range(EDGES):
        for n, device in enumerate((mesh.index(z, y, 1 - x, core), mesh.t)):
            source, _ = decode(device, j)
            index[192 + n * 24 + j] = ((source >> 2) & 3) * 24
            index[192 + n * 24 + 12 + j] = (source >> 4) * 24
            if n:
                index[240 + j] = (source >> 1) & 1


def exchange_steps(mesh, net, index, x_ref, out_lines, out_corners, refs):
    held_a, held_b, chosen, got_a, got_b, crossing, crossed, cells, apart, ordered = refs
    held, got = (held_a, held_b), (got_a, got_b)
    t, z, y, x, core = mesh.t, mesh.z, mesh.y, mesh.x, mesh.core
    remote, sibling, across = net.send, mesh.sibling, mesh.across
    along_z, along_y = mesh.along_z, mesh.along_y

    chains = ((z, y, along_z, along_y), (y, z, along_y, along_z))
    first, over = [], []
    for h, (p, _, others, _) in enumerate(chains):
        mine = x_ref.at[pl.ds(h * EDGES, EDGES)]
        place = held[h].at[pl.ds((p * 2 + core) * EDGES, EDGES)]
        first.append([remote(mine, place, other) for other in others])
        over.append([remote(mine, place, sibling)])
        held[h][pl.ds((p * 2 + core) * EDGES, EDGES)] = x_ref[pl.ds(h * EDGES, EDGES)]
    cell = ((core * 4 + y) * 4 + z) * 2
    cells[cell + x] = x_ref[2 * EDGES]
    cell_x = remote(x_ref.at[2 * EDGES], cells.at[cell + x], across)
    yield
    for k in range(3):
        for h, (p, _, _, _) in enumerate(chains):
            first[h][k].wait_recv()
            here = held[h].at[pl.ds((((p + 3 - k) % 4) * 2 + core) * EDGES, EDGES)]
            over[h].append(remote(here, here, sibling))
    cell_x.wait_recv()
    here = cells.at[pl.ds(cell, 2)]
    cell_z = [remote(here, here, other) for other in along_z]
    yield

    second = []
    for h, (p, q, _, others) in enumerate(chains):
        for copy in over[h]:
            copy.wait_recv()
        second.append([])
        for k in (1, 2, 3, 0):
            for j in range(2 * EDGES):
                chosen[h, k, j] = held[h][index[(h * 4 + k) * 24 + j]]
            place = got[h].at[pl.ds(q * 2 * EDGES, 2 * EDGES)]
            if k:
                second[h].append(remote(chosen.at[h, k], place, others[k - 1]))
            else:
                got[h][pl.ds(q * 2 * EDGES, 2 * EDGES)] = chosen[h, 0]
    for copy in cell_z:
        copy.wait_recv()
    here = cells.at[pl.ds((core * 4 + y) * 8, 8)]
    cell_y = [remote(here, here, other) for other in along_y]
    yield

    third = []
    for h in range(2):
        for copy in second[h]:
            copy.wait_recv()
        for j in range(EDGES):
            crossing[h, j] = got[h][index[192 + h * 12 + j] + (1 - x) * EDGES + j]
        third.append(remote(crossing.at[h], crossed.at[h], across))
    for copy in cell_y:
        copy.wait_recv()
    here = cells.at[pl.ds(core * 32, 32)]
    last = remote(here, here, sibling)
    yield

    for h in range(2):
        third[h].wait_recv()
        for j in range(EDGES):
            straight = got[h][index[216 + h * 12 + j] + x * EDGES + j]
            near = index[240 + j] == x
            at = slice(j * S + h * HALF, j * S + (h + 1) * HALF)
            out_lines[at, :] = jnp.where(near, straight, crossed[h, j])
    last.wait_recv()
    for d in range(64):
        apart[d * HALF : (d + 1) * HALF, :] = cells[
            (((d % 2) * 4 + (d // 4) % 4) * 4 + d // 16) * 2 + (d // 2) % 2
        ].astype(F32)
    for kind in range(4):
        for tile in range(TL):
            ordered[pl.ds(kind * 256 + tile, 64, stride=TL), :] = apart[
                pl.ds(tile * 4 + kind, 64, stride=HALF), :
            ]
        ordered[pl.ds(kind * 256 + 192, 64), :] = jnp.zeros((64, 128), F32)
    out_corners[...] = ordered[...].astype(BF)
    yield


def total_steps(mesh, net, grads, out_grads, summed, parts, by_y, by_z):
    z, y, group, remote = mesh.z, mesh.y, mesh.group, net.send

    def piece(ref, g):
        return ref.at[pl.ds(pl.multiple_of(g * SHARE, 8), SHARE)]

    scatter = [
        remote(piece(grads, (group + k) % 8), parts.at[group], mesh.near[k - 1]) for k in range(1, 8)
    ]
    parts[group] = grads[pl.ds(pl.multiple_of(group * SHARE, 8), SHARE), :]
    yield
    for copy in scatter:
        copy.wait_recv()
    total = parts[0]
    for g in range(1, 8):
        total = total + parts[g]
    by_y[y] = total
    add_y = [remote(by_y.at[y], by_y.at[y], other) for other in mesh.along_y]
    yield
    for copy in add_y:
        copy.wait_recv()
    by_z[z] = ((by_y[0] + by_y[1]) + by_y[2]) + by_y[3]
    add_z = [remote(by_z.at[z], by_z.at[z], other) for other in mesh.along_z]
    yield
    for copy in add_z:
        copy.wait_recv()
    total = ((by_z[0] + by_z[1]) + by_z[2]) + by_z[3]
    summed[...] = total
    out_grads[pl.ds(pl.multiple_of(group * SHARE, 8), SHARE), :] = total
    gather = [remote(summed, piece(out_grads, group), other) for other in mesh.near]
    yield
    for copy in gather:
        copy.wait_recv()
    yield


ROUND = [
    pltpu.VMEM((8 * EDGES, HALF, 128), BF),
    pltpu.VMEM((8 * EDGES, HALF, 128), BF),
    pltpu.VMEM((2, 4, 2 * EDGES, HALF, 128), BF),
    pltpu.VMEM((8 * EDGES, HALF, 128), BF),
    pltpu.VMEM((8 * EDGES, HALF, 128), BF),
    pltpu.VMEM((2, EDGES, HALF, 128), BF),
    pltpu.VMEM((2, EDGES, HALF, 128), BF),
    pltpu.VMEM((64, HALF, 128), BF),
    pltpu.VMEM((1024, 128), F32),
    pltpu.VMEM((1024, 128), F32),
]
COPIES = 2 * (6 + 2 + 1 + 6 + 3 + 6 + 3 + 2 + 1) + 7 + 3 + 3 + 7


def body(fields, cotangent, first_kernel, second_kernel, adjacency, seam_codes, corner_map):
    f = fields.reshape(R, S * C)
    c = cotangent.reshape(R, S * C)
    tables = (adjacency.T, seam_codes.T, corner_map.T)
    pad, shifts = pltpu.VMEM((PAIRS * PR, 128), F32), pltpu.VMEM((3, PAIRS, R, 128), BF)
    w_conv, w_rim, w_corner = (pltpu.VMEM(shape, BF) for shape in ((3, 512, 256), (384, 256), (128, 512)))
    flat, flat_low = pltpu.VMEM((NP * R, 128), F32), pltpu.VMEM((NP * R, 128), BF)
    turned, shifted, sixteen = (
        pltpu.VMEM((LINES, 128), F32), pltpu.VMEM((LINES, 384), BF), pltpu.VMEM((16, 128), F32),
    )
    quads, kernel = pltpu.VMEM((NP // 2 * R, 256), F32), pltpu.VMEM((3, 3, C, C), F32)
    tile, sums = pltpu.VMEM((R, S * C), BF), pltpu.VMEM((9 * C, 128), F32)
    blocks = pltpu.VMEM((2 * EDGES + 1, HALF, 128), BF)
    near, corners = pltpu.VMEM((LINES, 128), BF), pltpu.VMEM((1024, 128), BF)

    hbm = pl.BlockSpec(memory_space=pltpu.HBM)
    small, small_rows = pltpu.SMEM((4, 192), jnp.int32), pltpu.VMEM((4, 192), jnp.int32)
    corner_rows = pltpu.VMEM((8, 256), jnp.int32)

    def shape(ref):
        return jax.ShapeDtypeStruct(ref.shape, ref.dtype)

    hidden, back, rim, corner, near_two, cells_two, grads = pl.pallas_call(
        first_kernel_body,
        out_shape=tuple(shape(r) for r in (tile, flat, w_rim, w_corner, near, corners, sums)),
        in_specs=[hbm] * 7,
        out_specs=(hbm, hbm) + (VM,) * 5,
        scratch_shapes=[tile, tile, kernel, kernel, small, small, small, small_rows]
        + [pltpu.SemaphoreType.DMA((8,)), pltpu.SemaphoreType.DMA((2,)), corner_rows, tile, flat]
        + [pltpu.SMEM((252,), jnp.int32)]
        + [pad, pad, shifts, shifts, w_conv, w_conv, w_rim, w_corner, turned, shifted, sixteen]
        + [quads, flat, flat, pltpu.VMEM((LINES + HALF, 128), F32), flat_low, flat_low, sums]
        + [blocks, blocks, near, corners]
        + ROUND * 2
        + [pltpu.VMEM((SHARE, 128), F32)]
        + [pltpu.VMEM((k, SHARE, 128), F32) for k in (8, 4, 4)]
        + [pltpu.SemaphoreType.DMA((COPIES,))] * 2,
        name="first",
        compiler_params=pltpu.CompilerParams(
            collective_id=0, has_side_effects=True, vmem_limit_bytes=54 * 2**20
        ),
    )(f, c, first_kernel, second_kernel, *tables)
    kernel_sums = jax.ShapeDtypeStruct((9 * C, C), F32)
    output, field_grad, grad_one, grad_two = pl.pallas_call(
        last_kernel_body,
        out_shape=(shape(tile), shape(tile), kernel_sums, kernel_sums),
        in_specs=[hbm] * 2 + [VM] * 7 + [hbm] * 2 + [VM],
        out_specs=(VM,) * 4,
        scratch_shapes=[tile, flat, small, small, small_rows, pltpu.SemaphoreType.DMA((5,)), corner_rows]
        + [pad, shifts, w_conv, turned, shifted, sixteen, quads],
        name="last",
        compiler_params=pltpu.CompilerParams(vmem_limit_bytes=58 * 2**20),
    )(hidden, back, f, c, second_kernel, rim, corner, near_two, cells_two, *tables[1:], grads)
    shape_out = (1, TL, S, S * C)
    return (
        output.reshape(shape_out),
        field_grad.reshape(shape_out),
        grad_one.reshape(3, 3, C, C),
        grad_two.reshape(3, 3, C, C),
    )


def solution(mesh):
    split = P("batch", "tile", None, None)
    return jax.shard_map(
        body,
        mesh=mesh,
        in_specs=(split, split, P(), P(), P(), P(), P()),
        out_specs=(split, split, P(), P()),
        check_vma=False,
    )
```

```python
import math

import jax
import jax.numpy as jnp
from jax import lax
from jax.experimental import pallas as pl
from jax.experimental.pallas import tpu as pltpu
from jax.sharding import PartitionSpec as P

TL = 3
S = 32
C = 64
NP = 16
R = TL * S
EDGES = TL * 4
LINES = EDGES * S
HALF = S // 2
SHARE = 9 * C // 8
PAIRS = NP + 2
PR = 128
MESH = pl.DeviceIdType.MESH
F32 = jnp.float32
BF = jnp.bfloat16


def rows_at(t):
    return t * 40 + 8


def low_lanes(rows):
    return lax.broadcasted_iota(jnp.int32, (rows, 128), 1) < C


def swap(v):
    return pltpu.roll(v, C, 1)


def put_lines(lines, first, second, place, out):
    low16, low32 = low_lanes(16), low_lanes(32)
    step = place(1, 0) - place(0, 0)
    for t in range(TL):
        for e, i in ((0, S - 1), (2, 0)):
            where = pl.ds(place(0, t) + i, NP, stride=step)
            a, b = first[where, :], second[where, :]
            base = (t * 4 + e) * S
            lines[pl.ds(base, NP, stride=2), :] = jnp.where(low16, a, swap(b))
            lines[pl.ds(base + 1, NP, stride=2), :] = jnp.where(low16, swap(a), b)
        for e, pair in ((1, 0), (3, NP - 1)):
            where = pl.ds(place(pair, t), S)
            a, b = first[where, :], second[where, :]
            line = jnp.where(low32, a, swap(b)) if e == 1 else jnp.where(low32, swap(a), b)
            lines[pl.ds((t * 4 + e) * S, S), :] = line
        for corner, (e, s) in enumerate(((2, 0), (2, S - 1), (0, 0), (0, S - 1))):
            lines[pl.ds(LINES + t * 4 + corner, 1), :] = lines[pl.ds((t * 4 + e) * S + s, 1), :]
    lines[pl.ds(LINES + EDGES, HALF - EDGES), :] = jnp.zeros((HALF - EDGES, 128), F32)
    for j in range(EDGES):
        for h in range(2):
            out[h * EDGES + j] = lines[pl.ds(j * S + h * HALF, HALF), :].astype(BF)
    out[2 * EDGES] = lines[pl.ds(LINES, HALF), :].astype(BF)


def fill_pad(pad, src):
    for p in (0, PAIRS - 1):
        pad[pl.ds(p * PR, PR), :] = jnp.zeros((PR, 128), F32)
    for p in range(NP):
        for t in range(TL):
            base = (p + 1) * PR + rows_at(t)
            pad[pl.ds(base - 8, 8), :] = jnp.zeros((8, 128), F32)
            pad[pl.ds(base, S), :] = src[t * S : (t + 1) * S, p * 128 : (p + 1) * 128].astype(F32)
        pad[pl.ds((p + 1) * PR + 120, 8), :] = jnp.zeros((8, 128), F32)


def fill_flat(pad, flat, zero):
    if zero:
        pad[...] = jnp.zeros_like(pad)
    for p in range(NP):
        for t in range(TL):
            pad[pl.ds(pad_place(p, t), S), :] = flat[pl.ds(flat_place(p, t), S), :]


def patch_shifts(xp, pad):
    for t in range(TL):
        for p in (0, PAIRS - 1):
            for a in range(3):
                xp[a, p, t * S : (t + 1) * S, :] = pad[pl.ds(p * PR + rows_at(t) - 1 + a, S), :].astype(BF)
        for p in range(1, PAIRS - 1):
            first = p * PR + rows_at(t)
            xp[0, p, t * S : t * S + HALF, :] = pad[pl.ds(first - 1, HALF), :].astype(BF)
            xp[2, p, t * S + HALF : (t + 1) * S, :] = pad[pl.ds(first + HALF + 1, HALF), :].astype(BF)


def pad_place(pair, t):
    return (pair + 1) * PR + rows_at(t)


def flat_place(pair, t):
    return pair * R + t * S


def make_shifts(xp, pad):
    for a in range(3):
        for p in range(PAIRS):
            for t in range(TL):
                xp[a, p, t * S : (t + 1) * S, :] = pad[pl.ds(p * PR + rows_at(t) - 1 + a, S), :].astype(BF)


def edge_taps(a, c):
    return [
        spot for spot in ((0, c), (1, a), (2, c), (3, a)) if (a == 2, c == 0, a == 0, c == 2)[spot[0]]
    ]


def build_forward(w_out, w_edge, w_cell, w):
    w_out[...] = jnp.zeros_like(w_out)
    w_cell[...] = jnp.zeros_like(w_cell)
    for a in range(3):
        for c in range(3):
            block = w[a, c].astype(BF)
            for n in range(4):
                m = n + 1 + c
                w_out[a, m * C : (m + 1) * C, n * C : (n + 1) * C] = block
            for e, tap in edge_taps(a, c):
                w_edge[(2 - tap) * 128 : (2 - tap) * 128 + C, 256 + e * C : 256 + (e + 1) * C] = block
                w_edge[tap * 128 : tap * 128 + C, 512 + e * C : 512 + (e + 1) * C] = block
            if a != 1 and c != 1:
                at = ((a // 2) * 2 + c // 2) * 128
                w_cell[:C, at : at + C] = block
                w_cell[:C, at + C : at + 128] = block


def build_backward(w_out, w_edge, w_corner, w):
    w_out[...] = jnp.zeros_like(w_out)
    w_corner[...] = jnp.zeros_like(w_corner)
    for a in range(3):
        for c in range(3):
            block = w[a, c].T.astype(BF)
            for n in range(4):
                m = n + 3 - c
                w_out[2 - a, m * C : (m + 1) * C, n * C : (n + 1) * C] = block
            for e, tap in edge_taps(a, c):
                w_edge[tap * 128 + C : tap * 128 + 128, e * C : (e + 1) * C] = block
            if a != 1 and c != 1:
                at = ((a // 2) * 2 + c // 2) * 128
                w_corner[C:128, at : at + C] = block
                w_corner[C:128, at + C : at + 128] = block


def conv(xp, w):
    total = None
    for a in range(3):
        left = jnp.concatenate(
            [
                jnp.concatenate([xp[a, 2 * q + s] for q in range(NP // 2)], axis=0)
                for s in range(4)
            ],
            axis=1,
        )
        part = jnp.dot(left, w[a], preferred_element_type=F32)
        total = part if total is None else total + part
    return total


def columns(xp, a):
    return jnp.concatenate(
        [jnp.concatenate([xp[a, d + p] for p in range(NP)], axis=0) for d in range(3)], axis=1
    )


def first_part(xp, q, a):
    out = lax.dot_general(q, columns(xp, a), (((0,), (0,)), ((), ())), preferred_element_type=F32)
    turned = jnp.concatenate([out[:, d * 128 : (d + 1) * 128].T for d in range(3)], axis=0)
    return turned[64:256] + swap(turned[128:320])


def second_part(qp, h, a):
    out = lax.dot_general(h, columns(qp, 2 - a), (((0,), (0,)), ((), ())), preferred_element_type=F32)
    even, odd = out[:C], out[C:]
    return jnp.concatenate(
        [
            even[:, 128:256] + swap(odd[:, 256:384]),
            swap(even[:, 128:256]) + odd[:, 128:256],
            even[:, :128] + swap(odd[:, 128:256]),
        ],
        axis=0,
    )


def second_rims(grad, lines, wide, corners_ref, corner_rows, codes, me):
    upper = jnp.logical_not(low_lanes(C))
    kept = [lines[pl.ds(j * S, S), :].astype(BF) for j in range(EDGES)]
    ours = [line.astype(BF) for line in reverse(kept, codes)]
    zero = jnp.zeros((S, 128), BF)
    left = jnp.concatenate(
        [
            jnp.concatenate([jnp.where(codes[j] % 4 == e, ours[j], zero) for j in range(EDGES)], axis=0)
            for e in range(4)
        ],
        axis=1,
    )
    out = lax.dot_general(left, wide[...], (((0,), (0,)), ((), ())), preferred_element_type=F32)
    pixels = lines[pl.ds(LINES, 16), :].astype(BF)
    for e in range(4):
        for c in range(3):
            a, b = ((2, c), (c, 0), (0, c), (c, 2))[e]
            at = pl.ds((a * 3 + b) * C, C)
            part = out[e * 128 : e * 128 + C, c * 128 : (c + 1) * 128]
            grad[at, :] = grad[at, :] + jnp.where(upper, part, 0.0)
        met = jnp.dot(
            picked(corner_rows, me, e), corners_ref[pl.ds(e * 256, 256), :], preferred_element_type=F32
        ).astype(BF)
        part = lax.dot_general(pixels, met, (((0,), (0,)), ((), ())), preferred_element_type=F32)
        at = pl.ds(((e // 2) * 6 + (e % 2) * 2) * C, C)
        grad[at, :] = grad[at, :] + jnp.where(upper, part[:C], 0.0)


def reverse(kept, codes, precision=None):
    flip = (
        lax.broadcasted_iota(jnp.int32, (S, S), 0) + lax.broadcasted_iota(jnp.int32, (S, S), 1)
        == S - 1
    )
    flip = jnp.where(flip, 1.0, 0.0).astype(kept[0].dtype)
    flipped = jnp.dot(
        flip, jnp.concatenate(kept, axis=1), preferred_element_type=F32, precision=precision
    )
    return [
        jnp.where(codes[j] >= 4, flipped[:, j * 128 : (j + 1) * 128], kept[j].astype(F32))
        for j in range(EDGES)
    ]


def edge_terms(lines_ref, codes, w_edge, turned, wide, terms):
    lines = lines_ref[...].astype(F32)
    low = low_lanes(S)
    spot = lax.broadcasted_iota(jnp.int32, (LINES, 128), 0) % S
    after = jnp.where(spot == S - 1, 0.0, pltpu.roll(lines, LINES - 1, 0)).astype(BF)
    before = jnp.where(spot == 0, 0.0, pltpu.roll(lines, 1, 0)).astype(BF)
    wide[...] = jnp.concatenate([after, lines_ref[...], before], axis=1)
    terms[...] = jnp.dot(wide[...], w_edge[...], preferred_element_type=F32)
    kept = []
    for j in range(EDGES):
        e, at, tile = codes[j] & 3, pl.ds(j * S, S), (j % 4) // 2 * 128
        pair = jnp.where(e >= 2, terms[at, 128:256], terms[at, :128])
        rim = jnp.where((e & 1) == 1, pair, swap(pair))
        halo = jnp.where(
            codes[j] >= 4, terms[at, 512 + tile : 640 + tile], terms[at, 256 + tile : 384 + tile]
        )
        kept.append(jnp.where(low, swap(halo) if j % 2 else halo, rim.astype(BF).astype(F32)))
    for j, line in enumerate(reverse(kept, codes, lax.Precision.HIGHEST)):
        turned[pl.ds(j * S, S), :] = line


def raw_lines(lines_ref, codes, turned):
    kept = [lines_ref[pl.ds(j * S, S), :] for j in range(EDGES)]
    for j, line in enumerate(reverse(kept, codes)):
        turned[pl.ds(j * S, S), :] = line


def halo_in(pad, turned, cells):
    low16 = low_lanes(16)
    cells_swapped = swap(cells[...])
    for t in range(TL):
        for e, row in ((0, rows_at(t) + S), (2, rows_at(t) - 1)):
            base = (t * 4 + e) * S
            even = turned[pl.ds(base, NP, stride=2), :]
            odd = turned[pl.ds(base + 1, NP, stride=2), :]
            pad[pl.ds(PR + row, NP, stride=PR), :] = jnp.where(low16, even, swap(odd))
        pad[pl.ds(rows_at(t), S), :] = swap(turned[pl.ds((t * 4 + 1) * S, S), :])
        pad[pl.ds((PAIRS - 1) * PR + rows_at(t), S), :] = turned[pl.ds((t * 4 + 3) * S, S), :]
        for corner, (row, p) in enumerate(((-1, 0), (-1, 1), (S, 0), (S, 1))):
            at = t * 4 + corner
            value = (cells[...] if p else cells_swapped)[at : at + 1]
            pad[pl.ds(p * (PAIRS - 1) * PR + rows_at(t) + row, 1), :] = value


def picked(corner_rows, me, kind):
    slot = lax.broadcasted_iota(jnp.int32, (16, 256), 0)
    pick = (corner_rows[kind : kind + 1, :] == me * EDGES + slot) & (slot < EDGES)
    return jnp.where(pick, 1.0, 0.0).astype(BF)


def corner_sums(corners_ref, corner_rows, me, w_corner):
    total = None
    for kind in range(4):
        rim = jnp.dot(
            corners_ref[pl.ds(kind * 256, 256), :],
            w_corner[:, kind * 128 : (kind + 1) * 128],
            preferred_element_type=F32,
        ).astype(BF)
        part = jnp.dot(picked(corner_rows, me, kind), rim, preferred_element_type=F32)
        total = part if total is None else total + part
    return total


def cell_terms(cells, w_cell):
    every = jnp.dot(cells[...].astype(BF), w_cell[...], preferred_element_type=F32)
    kind = lax.broadcasted_iota(jnp.int32, (16, 128), 0) % 4
    total = jnp.zeros((16, 128), F32)
    for k in range(4):
        total = jnp.where(kind == k, every[:, k * 128 : (k + 1) * 128], total)
    return total


def add_edges(flat, turned, cells, upper):
    low16, low32 = low_lanes(16), low_lanes(S)

    def at_low(v):
        return swap(v) if upper else v

    def at_high(v):
        return v if upper else swap(v)

    for t in range(TL):
        for e, i in ((0, S - 1), (2, 0)):
            base = (t * 4 + e) * S
            even = turned[pl.ds(base, NP, stride=2), :]
            odd = turned[pl.ds(base + 1, NP, stride=2), :]
            at = pl.ds(t * S + i, NP, stride=R)
            flat[at, :] = flat[at, :] + jnp.where(low16, at_low(even), at_high(odd))
        at = pl.ds(t * S, S)
        line = at_low(turned[pl.ds((t * 4 + 1) * S, S), :])
        flat[at, :] = flat[at, :] + jnp.where(low32, line, 0.0)
        at = pl.ds((NP - 1) * R + t * S, S)
        line = at_high(turned[pl.ds((t * 4 + 3) * S, S), :])
        flat[at, :] = flat[at, :] + jnp.where(low32, 0.0, line)
    lows, highs = jnp.where(low16, cells, 0.0), jnp.where(low16, 0.0, cells)
    for t in range(TL):
        for corner, (i, p) in enumerate(((0, 0), (0, 1), (S - 1, 0), (S - 1, 1))):
            at = pl.ds(p * (NP - 1) * R + t * S + i, 1)
            s = t * 4 + corner
            flat[at, :] = flat[at, :] + (highs if p else lows)[s : s + 1]


def cells_of(corners_ref, places, me):
    slot = lax.broadcasted_iota(jnp.int32, (16, 1024), 0)
    row = jnp.full((16, 1024), -1, jnp.int32)
    for s in range(EDGES):
        v = places[s % 4, me * TL + s // 4]
        row = jnp.where(slot == s, (v & 3) * 256 + (v >> 2), row)
    pick = jnp.where(lax.broadcasted_iota(jnp.int32, (16, 1024), 1) == row, 1.0, 0.0).astype(BF)
    return jnp.dot(pick, corners_ref[...], preferred_element_type=F32)


def codes_of(seams, me):
    return [seams[j % 4, me * TL + j // 4] for j in range(EDGES)]


def load_rows(corner_rows, rows):
    corner_rows[...] = jnp.full((8, 256), -1, jnp.int32)
    corner_rows[0:4, 0:192] = rows[...]


def put_back(back, out):
    for q in range(NP // 2):
        for half in range(2):
            back[pl.ds((2 * q + half) * R, R), :] = out[q * R : (q + 1) * R, half * 128 : (half + 1) * 128]


def whole_kernel(
    f_hbm, c_hbm, w1_hbm, w2_hbm, adjacency_hbm, seams_hbm, places_hbm,
    output_hbm, field_grad_hbm, grad_one_hbm, grad_two_hbm,
    f_ref, c_ref, w1_ref, w2_ref, adjacency, seams, places, rows, loads, stores, corner_rows, index,
    output, field_grad, grad_one, grad_two,
    pad_f, pad_c, xp, qp, w_forth, w_back, w_forth_two, w_back_two, w_edge, w_edge_two,
    w_corner, w_cell, w_corner_two, w_cell_two,
    turned, raw, wide, wide_two, terms, cells, main, back, hid, lines, grads, hids, grad,
    sent_one, sent_two, near, near_two, corners, corners_two, out_grads, *refs,
):
    me = lax.axis_index("tile")
    inputs = [
        pltpu.make_async_copy(src, dst, loads.at[n])
        for n, (src, dst) in enumerate(
            (
                (f_hbm, f_ref), (c_hbm, c_ref), (w2_hbm, w2_ref), (w1_hbm, w1_ref),
                (adjacency_hbm, adjacency), (seams_hbm, seams), (places_hbm, places), (places_hbm, rows),
            )
        )
    ]
    for copy in inputs:
        copy.start()
    mesh = Mesh()
    mesh.greet()
    n = len(ROUND)
    one, two, rest = refs[:n], refs[n : 2 * n], refs[2 * n :]
    summed, parts, by_y, by_z, sent, come = rest
    net = Net(sent, come)
    inputs[0].wait()
    fill_pad(pad_f, f_ref)
    inputs[1].wait()
    fill_pad(pad_c, c_ref)
    put_lines(lines, pad_f, pad_c, pad_place, sent_one)
    mesh.meet()
    first = exchange_steps(mesh, net, index, sent_one, near, corners, one)
    next(first)
    for copy in inputs[4:]:
        copy.wait()
    find_index(mesh, adjacency, seams, index)
    load_rows(corner_rows, rows)
    make_shifts(qp, pad_c)
    make_shifts(xp, pad_f)
    next(first)
    inputs[2].wait()
    inputs[3].wait()
    w_edge[...] = jnp.zeros_like(w_edge)
    build_backward(w_back, w_edge, w_corner, w2_ref)
    next(first)
    put_back(back, conv(qp, w_back))
    build_forward(w_forth, w_edge, w_cell, w1_ref)
    put_back(main, conv(xp, w_forth))
    next(first)
    w_edge_two[...] = jnp.zeros_like(w_edge_two)
    build_backward(w_back_two, w_edge_two, w_corner_two, w1_ref)
    build_forward(w_forth_two, w_edge_two, w_cell_two, w2_ref)
    next(first)

    codes = codes_of(seams, me)
    edge_terms(near, codes, w_edge, turned, wide, terms)
    cells[...] = cells_of(corners, places, me)
    add_edges(main, turned, cell_terms(cells, w_cell), False)
    add_edges(back, turned, corner_sums(corners, corner_rows, me, w_corner), True)
    for p in range(NP):
        at = pl.ds(p * R, R)
        pre = main[at, :]
        s = 1.0 / (1.0 + jnp.exp(-pre))
        h = (pre * s).astype(BF)
        g = (back[at, :] * s * (1.0 + pre * (1.0 - s))).astype(BF)
        hid[at, :] = h.astype(F32)
        back[at, :] = g.astype(F32)
        grads[at, :] = g
        hids[at, :] = h
    put_lines(lines, hid, back, flat_place, sent_two)
    second = exchange_steps(mesh, net, index, sent_two, near_two, corners_two, two)
    next(second)

    raw_lines(near, codes, raw)
    halo_in(pad_f, raw, cells)
    patch_shifts(xp, pad_f)
    low = low_lanes(192)
    for a in range(3):
        grad[pl.ds(a * 192, 192), :] = jnp.where(
            low, first_part(xp, grads[...], a), second_part(qp, hids[...], a)
        )
    second_rims(grad, lines, wide, corners, corner_rows, codes, me)
    adding = total_steps(mesh, net, grad, out_grads, summed, parts, by_y, by_z)
    next(adding)
    next(second)
    fill_flat(pad_f, hid, True)
    next(second)
    make_shifts(xp, pad_f)
    put_back(main, conv(xp, w_forth_two))
    next(adding)
    fill_flat(pad_c, back, False)
    make_shifts(qp, pad_c)
    put_back(back, conv(qp, w_back_two))
    next(adding)
    next(second)
    next(adding)
    next(second)

    edge_terms(near_two, codes, w_edge_two, turned, wide_two, terms)
    cells[...] = cells_of(corners_two, places, me)
    add_edges(main, turned, cell_terms(cells, w_cell_two), False)
    add_edges(back, turned, corner_sums(corners_two, corner_rows, me, w_corner_two), True)
    for p in range(NP):
        at, lanes = pl.ds(p * R, R), slice(p * 128, (p + 1) * 128)
        output[:, lanes] = (f_ref[:, lanes].astype(F32) + main[at, :]).astype(BF)
        field_grad[:, lanes] = (c_ref[:, lanes].astype(F32) + back[at, :]).astype(BF)
    results = [
        pltpu.make_async_copy(src, dst, stores.at[n])
        for n, (src, dst) in enumerate(
            (
                (output, output_hbm), (field_grad, field_grad_hbm),
                (grad_one, grad_one_hbm), (grad_two, grad_two_hbm),
            )
        )
    ]
    results[0].start()
    results[1].start()
    next(adding)
    scale = 1.0 / math.sqrt(2 * 192 * S * S)
    grad_one[...] = out_grads[:, :C] * scale
    grad_two[...] = out_grads[:, C:] * scale
    results[2].start()
    results[3].start()
    net.finish()
    for copy in results:
        copy.wait()


def hand_over(*refs):
    ins, outs, held, come, gone = refs[:4], refs[4:8], refs[8:12], refs[12], refs[13]
    arrive = [pltpu.make_async_copy(a, b, come.at[n]) for n, (a, b) in enumerate(zip(ins, held))]
    leave = [pltpu.make_async_copy(a, b, gone.at[n]) for n, (a, b) in enumerate(zip(held, outs))]
    for copy in arrive:
        copy.start()
    for n in range(4):
        arrive[n].wait()
        leave[n].start()
    for copy in leave:
        copy.wait()


class Mesh:
    def __init__(self):
        self.t = t = lax.axis_index("tile")
        self.b = b = lax.axis_index("batch")
        self.z, self.y, self.x, self.core = z, y, x, core = t // 16, (t // 4) % 4, (t // 2) % 2, t % 2
        self.along_z = [(self.index((z + k) % 4, y, x, core), b) for k in range(1, 4)]
        self.along_y = [(self.index(z, (y + k) % 4, x, core), b) for k in range(1, 4)]
        self.sibling = (self.index(z, y, x, 1 - core), b)
        self.across = (self.index(z, y, 1 - x, core), b)
        self.group = x * 4 + b * 2 + core
        self.near = []
        for k in range(1, 8):
            g = (self.group + k) % 8
            self.near.append((self.index(z, y, g // 4, g % 2), (g // 2) % 2))

    def index(self, z, y, x, core):
        return z * 16 + y * 4 + x * 2 + core

    def greet(self):
        for other in self.along_z + self.along_y + self.near:
            pl.semaphore_signal(
                pltpu.get_barrier_semaphore(), inc=1, device_id=other, device_id_type=MESH
            )

    def meet(self):
        pl.semaphore_wait(pltpu.get_barrier_semaphore(), 13)


class Net:
    def __init__(self, sent, come):
        self.sent, self.come, self.copies = sent, come, []

    def send(self, src, dst, other):
        n = len(self.copies)
        copy = pltpu.make_async_remote_copy(
            src_ref=src, dst_ref=dst, send_sem=self.sent.at[n], recv_sem=self.come.at[n],
            device_id=other, device_id_type=MESH,
        )
        copy.start()
        self.copies.append(copy)
        return copy

    def finish(self):
        for copy in self.copies:
            copy.wait_send()


def find_index(mesh, adjacency, seams, index):
    z, y, x, core = mesh.z, mesh.y, mesh.x, mesh.core

    def decode(device, j):
        tile, code = adjacency[j % 4, device * TL + j // 4], seams[j % 4, device * TL + j // 4]
        source = (tile * 171) >> 9
        return source, (tile - source * 3) * 4 + (code & 3)

    for h in range(2):
        for k in range(4):
            for side in range(2):
                device = (
                    mesh.index(z, (y + k) % 4, side, core) if h == 0 else mesh.index((z + k) % 4, y, side, core)
                )
                for j in range(EDGES):
                    source, line = decode(device, j)
                    p = (source >> 4) if h == 0 else ((source >> 2) & 3)
                    index[(h * 4 + k) * 24 + side * 12 + j] = (p * 2 + (source & 1)) * EDGES + line
    for j in range(EDGES):
        for n, device in enumerate((mesh.index(z, y, 1 - x, core), mesh.t)):
            source, _ = decode(device, j)
            index[192 + n * 24 + j] = ((source >> 2) & 3) * 24
            index[192 + n * 24 + 12 + j] = (source >> 4) * 24
            if n:
                index[240 + j] = (source >> 1) & 1


def exchange_steps(mesh, net, index, x_ref, out_lines, out_corners, refs):
    held_a, held_b, chosen, got_a, got_b, crossing, crossed, cells, apart, ordered = refs
    held, got = (held_a, held_b), (got_a, got_b)
    t, z, y, x, core = mesh.t, mesh.z, mesh.y, mesh.x, mesh.core
    remote, sibling, across = net.send, mesh.sibling, mesh.across
    along_z, along_y = mesh.along_z, mesh.along_y

    chains = ((z, y, along_z, along_y), (y, z, along_y, along_z))
    first, over = [], []
    for h, (p, _, others, _) in enumerate(chains):
        mine = x_ref.at[pl.ds(h * EDGES, EDGES)]
        place = held[h].at[pl.ds((p * 2 + core) * EDGES, EDGES)]
        first.append([remote(mine, place, other) for other in others])
        over.append([remote(mine, place, sibling)])
        held[h][pl.ds((p * 2 + core) * EDGES, EDGES)] = x_ref[pl.ds(h * EDGES, EDGES)]
    cell = ((core * 4 + y) * 4 + z) * 2
    cells[cell + x] = x_ref[2 * EDGES]
    cell_x = remote(x_ref.at[2 * EDGES], cells.at[cell + x], across)
    yield
    for k in range(3):
        for h, (p, _, _, _) in enumerate(chains):
            first[h][k].wait_recv()
            here = held[h].at[pl.ds((((p + 3 - k) % 4) * 2 + core) * EDGES, EDGES)]
            over[h].append(remote(here, here, sibling))
    cell_x.wait_recv()
    here = cells.at[pl.ds(cell, 2)]
    cell_z = [remote(here, here, other) for other in along_z]
    yield

    second = []
    for h, (p, q, _, others) in enumerate(chains):
        for copy in over[h]:
            copy.wait_recv()
        second.append([])
        for k in (1, 2, 3, 0):
            for j in range(2 * EDGES):
                chosen[h, k, j] = held[h][index[(h * 4 + k) * 24 + j]]
            place = got[h].at[pl.ds(q * 2 * EDGES, 2 * EDGES)]
            if k:
                second[h].append(remote(chosen.at[h, k], place, others[k - 1]))
            else:
                got[h][pl.ds(q * 2 * EDGES, 2 * EDGES)] = chosen[h, 0]
    for copy in cell_z:
        copy.wait_recv()
    here = cells.at[pl.ds((core * 4 + y) * 8, 8)]
    cell_y = [remote(here, here, other) for other in along_y]
    yield

    third = []
    for h in range(2):
        for copy in second[h]:
            copy.wait_recv()
        for j in range(EDGES):
            crossing[h, j] = got[h][index[192 + h * 12 + j] + (1 - x) * EDGES + j]
        third.append(remote(crossing.at[h], crossed.at[h], across))
    for copy in cell_y:
        copy.wait_recv()
    here = cells.at[pl.ds(core * 32, 32)]
    last = remote(here, here, sibling)
    yield

    for h in range(2):
        third[h].wait_recv()
        for j in range(EDGES):
            straight = got[h][index[216 + h * 12 + j] + x * EDGES + j]
            near = index[240 + j] == x
            at = slice(j * S + h * HALF, j * S + (h + 1) * HALF)
            out_lines[at, :] = jnp.where(near, straight, crossed[h, j])
    last.wait_recv()
    for d in range(64):
        apart[d * HALF : (d + 1) * HALF, :] = cells[
            (((d % 2) * 4 + (d // 4) % 4) * 4 + d // 16) * 2 + (d // 2) % 2
        ].astype(F32)
    for kind in range(4):
        for tile in range(TL):
            ordered[pl.ds(kind * 256 + tile, 64, stride=TL), :] = apart[
                pl.ds(tile * 4 + kind, 64, stride=HALF), :
            ]
        ordered[pl.ds(kind * 256 + 192, 64), :] = jnp.zeros((64, 128), F32)
    out_corners[...] = ordered[...].astype(BF)
    yield


def total_steps(mesh, net, grads, out_grads, summed, parts, by_y, by_z):
    z, y, group, remote = mesh.z, mesh.y, mesh.group, net.send

    def piece(ref, g):
        return ref.at[pl.ds(pl.multiple_of(g * SHARE, 8), SHARE)]

    scatter = [
        remote(piece(grads, (group + k) % 8), parts.at[group], mesh.near[k - 1]) for k in range(1, 8)
    ]
    parts[group] = grads[pl.ds(pl.multiple_of(group * SHARE, 8), SHARE), :]
    yield
    for copy in scatter:
        copy.wait_recv()
    total = parts[0]
    for g in range(1, 8):
        total = total + parts[g]
    by_y[y] = total
    add_y = [remote(by_y.at[y], by_y.at[y], other) for other in mesh.along_y]
    yield
    for copy in add_y:
        copy.wait_recv()
    by_z[z] = ((by_y[0] + by_y[1]) + by_y[2]) + by_y[3]
    add_z = [remote(by_z.at[z], by_z.at[z], other) for other in mesh.along_z]
    yield
    for copy in add_z:
        copy.wait_recv()
    total = ((by_z[0] + by_z[1]) + by_z[2]) + by_z[3]
    summed[...] = total
    out_grads[pl.ds(pl.multiple_of(group * SHARE, 8), SHARE), :] = total
    gather = [remote(summed, piece(out_grads, group), other) for other in mesh.near]
    yield
    for copy in gather:
        copy.wait_recv()
    yield


ROUND = [
    pltpu.VMEM((8 * EDGES, HALF, 128), BF),
    pltpu.VMEM((8 * EDGES, HALF, 128), BF),
    pltpu.VMEM((2, 4, 2 * EDGES, HALF, 128), BF),
    pltpu.VMEM((8 * EDGES, HALF, 128), BF),
    pltpu.VMEM((8 * EDGES, HALF, 128), BF),
    pltpu.VMEM((2, EDGES, HALF, 128), BF),
    pltpu.VMEM((2, EDGES, HALF, 128), BF),
    pltpu.VMEM((64, HALF, 128), BF),
    pltpu.VMEM((1024, 128), F32),
    pltpu.VMEM((1024, 128), F32),
]
COPIES = 2 * (6 + 2 + 1 + 6 + 3 + 6 + 3 + 2 + 1) + 7 + 3 + 3 + 7


def body(fields, cotangent, first_kernel, second_kernel, adjacency, seam_codes, corner_map):
    f = fields.reshape(R, S * C)
    c = cotangent.reshape(R, S * C)
    tables = (adjacency.T, seam_codes.T, corner_map.T)
    pad, shifts = pltpu.VMEM((PAIRS * PR, 128), F32), pltpu.VMEM((3, PAIRS, R, 128), BF)
    w_conv, w_edge = pltpu.VMEM((3, 512, 256), BF), pltpu.VMEM((384, 768), BF)
    w_corner = pltpu.VMEM((128, 512), BF)
    flat, flat_low = pltpu.VMEM((NP * R, 128), F32), pltpu.VMEM((NP * R, 128), BF)
    turned, shifted = pltpu.VMEM((LINES, 128), F32), pltpu.VMEM((LINES, 384), BF)
    terms, sixteen = pltpu.VMEM((LINES, 768), F32), pltpu.VMEM((16, 128), F32)
    kernel, kernel_sum = pltpu.VMEM((3, 3, C, C), F32), pltpu.VMEM((9 * C, C), F32)
    tile, sums = pltpu.VMEM((R, S * C), BF), pltpu.VMEM((9 * C, 128), F32)
    blocks = pltpu.VMEM((2 * EDGES + 1, HALF, 128), BF)
    near, corners = pltpu.VMEM((LINES, 128), BF), pltpu.VMEM((1024, 128), BF)
    hbm = pl.BlockSpec(memory_space=pltpu.HBM)
    small = pltpu.SMEM((4, 192), jnp.int32)
    sem = pltpu.SemaphoreType.DMA
    shapes = tuple(jax.ShapeDtypeStruct(r.shape, r.dtype) for r in (tile, tile, kernel_sum, kernel_sum))
    results = pl.pallas_call(
        whole_kernel,
        out_shape=shapes,
        in_specs=[hbm] * 7,
        out_specs=(hbm,) * 4,
        scratch_shapes=[tile, tile, kernel, kernel, small, small, small]
        + [pltpu.VMEM((4, 192), jnp.int32), sem((8,)), sem((4,)), pltpu.VMEM((8, 256), jnp.int32)]
        + [pltpu.SMEM((252,), jnp.int32), tile, tile, kernel_sum, kernel_sum]
        + [pad, pad, shifts, shifts, w_conv, w_conv, w_conv, w_conv, w_edge, w_edge]
        + [w_corner] * 4
        + [turned, turned, shifted, shifted, terms, sixteen, flat, flat, flat]
        + [pltpu.VMEM((LINES + HALF, 128), F32), flat_low, flat_low, sums]
        + [blocks, blocks, near, near, corners, corners, sums]
        + ROUND * 2
        + [pltpu.VMEM((SHARE, 128), F32)]
        + [pltpu.VMEM((k, SHARE, 128), F32) for k in (8, 4, 4)]
        + [sem((COPIES,))] * 2,
        name="whole",
        compiler_params=pltpu.CompilerParams(
            collective_id=0, has_side_effects=True, vmem_limit_bytes=54 * 2**20
        ),
    )(f, c, first_kernel, second_kernel, *tables)
    output, field_grad, grad_one, grad_two = pl.pallas_call(
        hand_over,
        out_shape=shapes,
        in_specs=[hbm] * 4,
        out_specs=(hbm,) * 4,
        scratch_shapes=[tile, tile, kernel_sum, kernel_sum, sem((4,)), sem((4,))],
        name="hand_over",
        compiler_params=pltpu.CompilerParams(vmem_limit_bytes=58 * 2**20),
    )(*results)
    shape_out = (1, TL, S, S * C)
    return (
        output.reshape(shape_out),
        field_grad.reshape(shape_out),
        grad_one.reshape(3, 3, C, C),
        grad_two.reshape(3, 3, C, C),
    )


def solution(mesh):
    split = P("batch", "tile", None, None)
    return jax.shard_map(
        body,
        mesh=mesh,
        in_specs=(split, split, P(), P(), P(), P(), P()),
        out_specs=(split, split, P(), P()),
        check_vma=False,
    )
```

```python
import math

import jax
import jax.numpy as jnp
from jax import lax
from jax.experimental import pallas as pl
from jax.experimental.pallas import tpu as pltpu
from jax.sharding import PartitionSpec as P

TL = 3
S = 32
C = 64
NP = 16
R = TL * S
EDGES = TL * 4
LINES = EDGES * S
HALF = S // 2
SHARE = 9 * C // 8
PAIRS = NP + 2
PR = 128
MESH = pl.DeviceIdType.MESH
F32 = jnp.float32
BF = jnp.bfloat16


def rows_at(t):
    return t * 40 + 8


def low_lanes(rows):
    return lax.broadcasted_iota(jnp.int32, (rows, 128), 1) < C


def swap(v):
    return pltpu.roll(v, C, 1)


def put_lines(lines, first, second, place, out):
    low16, low32 = low_lanes(16), low_lanes(32)
    step = place(1, 0) - place(0, 0)
    for t in range(TL):
        for e, i in ((0, S - 1), (2, 0)):
            where = pl.ds(place(0, t) + i, NP, stride=step)
            a, b = first[where, :], second[where, :]
            base = (t * 4 + e) * S
            lines[pl.ds(base, NP, stride=2), :] = jnp.where(low16, a, swap(b))
            lines[pl.ds(base + 1, NP, stride=2), :] = jnp.where(low16, swap(a), b)
        for e, pair in ((1, 0), (3, NP - 1)):
            where = pl.ds(place(pair, t), S)
            a, b = first[where, :], second[where, :]
            line = jnp.where(low32, a, swap(b)) if e == 1 else jnp.where(low32, swap(a), b)
            lines[pl.ds((t * 4 + e) * S, S), :] = line
        for corner, (e, s) in enumerate(((2, 0), (2, S - 1), (0, 0), (0, S - 1))):
            lines[pl.ds(LINES + t * 4 + corner, 1), :] = lines[pl.ds((t * 4 + e) * S + s, 1), :]
    lines[pl.ds(LINES + EDGES, HALF - EDGES), :] = jnp.zeros((HALF - EDGES, 128), F32)
    for j in range(EDGES):
        for h in range(2):
            out[h * EDGES + j] = lines[pl.ds(j * S + h * HALF, HALF), :].astype(BF)
    out[2 * EDGES] = lines[pl.ds(LINES, HALF), :].astype(BF)


def fill_pad(pad, src):
    for p in (0, PAIRS - 1):
        pad[pl.ds(p * PR, PR), :] = jnp.zeros((PR, 128), F32)
    for p in range(NP):
        for t in range(TL):
            base = (p + 1) * PR + rows_at(t)
            pad[pl.ds(base - 8, 8), :] = jnp.zeros((8, 128), F32)
            pad[pl.ds(base, S), :] = src[t * S : (t + 1) * S, p * 128 : (p + 1) * 128].astype(F32)
        pad[pl.ds((p + 1) * PR + 120, 8), :] = jnp.zeros((8, 128), F32)


def fill_flat(pad, flat, zero):
    if zero:
        pad[...] = jnp.zeros_like(pad)
    for p in range(NP):
        for t in range(TL):
            pad[pl.ds(pad_place(p, t), S), :] = flat[pl.ds(flat_place(p, t), S), :]


def patch_shifts(xp, pad):
    for t in range(TL):
        for p in (0, PAIRS - 1):
            for a in range(3):
                xp[a, p, t * S : (t + 1) * S, :] = pad[pl.ds(p * PR + rows_at(t) - 1 + a, S), :].astype(BF)
        for p in range(1, PAIRS - 1):
            first = p * PR + rows_at(t)
            xp[0, p, t * S : t * S + HALF, :] = pad[pl.ds(first - 1, HALF), :].astype(BF)
            xp[2, p, t * S + HALF : (t + 1) * S, :] = pad[pl.ds(first + HALF + 1, HALF), :].astype(BF)


def pad_place(pair, t):
    return (pair + 1) * PR + rows_at(t)


def flat_place(pair, t):
    return pair * R + t * S


def make_shifts(xp, pad):
    for a in range(3):
        for p in range(PAIRS):
            for t in range(TL):
                xp[a, p, t * S : (t + 1) * S, :] = pad[pl.ds(p * PR + rows_at(t) - 1 + a, S), :].astype(BF)


def edge_taps(a, c):
    return [
        spot for spot in ((0, c), (1, a), (2, c), (3, a)) if (a == 2, c == 0, a == 0, c == 2)[spot[0]]
    ]


def build_forward(w_out, w_edge, w_cell, w):
    w_out[...] = jnp.zeros_like(w_out)
    w_cell[...] = jnp.zeros_like(w_cell)
    for a in range(3):
        for c in range(3):
            block = w[a, c].astype(BF)
            for n in range(4):
                m = n + 1 + c
                w_out[a, m * C : (m + 1) * C, n * C : (n + 1) * C] = block
            for e, tap in edge_taps(a, c):
                w_edge[(2 - tap) * 128 : (2 - tap) * 128 + C, 256 + e * C : 256 + (e + 1) * C] = block
                w_edge[tap * 128 : tap * 128 + C, 512 + e * C : 512 + (e + 1) * C] = block
            if a != 1 and c != 1:
                at = ((a // 2) * 2 + c // 2) * 128
                w_cell[:C, at : at + C] = block
                w_cell[:C, at + C : at + 128] = block


def build_backward(w_out, w_edge, w_corner, w):
    w_out[...] = jnp.zeros_like(w_out)
    w_corner[...] = jnp.zeros_like(w_corner)
    for a in range(3):
        for c in range(3):
            block = w[a, c].T.astype(BF)
            for n in range(4):
                m = n + 3 - c
                w_out[2 - a, m * C : (m + 1) * C, n * C : (n + 1) * C] = block
            for e, tap in edge_taps(a, c):
                w_edge[tap * 128 + C : tap * 128 + 128, e * C : (e + 1) * C] = block
            if a != 1 and c != 1:
                at = ((a // 2) * 2 + c // 2) * 128
                w_corner[C:128, at : at + C] = block
                w_corner[C:128, at + C : at + 128] = block


def conv(xp, w):
    total = None
    for a in range(3):
        left = jnp.concatenate(
            [
                jnp.concatenate([xp[a, 2 * q + s] for q in range(NP // 2)], axis=0)
                for s in range(4)
            ],
            axis=1,
        )
        part = jnp.dot(left, w[a], preferred_element_type=F32)
        total = part if total is None else total + part
    return total


def columns(xp, a):
    return jnp.concatenate(
        [jnp.concatenate([xp[a, d + p] for p in range(NP)], axis=0) for d in range(3)], axis=1
    )


def first_part(xp, q, a):
    out = lax.dot_general(q, columns(xp, a), (((0,), (0,)), ((), ())), preferred_element_type=F32)
    turned = jnp.concatenate([out[:, d * 128 : (d + 1) * 128].T for d in range(3)], axis=0)
    return turned[64:256] + swap(turned[128:320])


def second_part(qp, h, a):
    out = lax.dot_general(h, columns(qp, 2 - a), (((0,), (0,)), ((), ())), preferred_element_type=F32)
    even, odd = out[:C], out[C:]
    return jnp.concatenate(
        [
            even[:, 128:256] + swap(odd[:, 256:384]),
            swap(even[:, 128:256]) + odd[:, 128:256],
            even[:, :128] + swap(odd[:, 128:256]),
        ],
        axis=0,
    )


def second_rims(grad, lines, wide, corners_ref, corner_rows, codes, me):
    upper = jnp.logical_not(low_lanes(C))
    kept = [lines[pl.ds(j * S, S), :].astype(BF) for j in range(EDGES)]
    ours = [line.astype(BF) for line in reverse(kept, codes)]
    zero = jnp.zeros((S, 128), BF)
    left = jnp.concatenate(
        [
            jnp.concatenate([jnp.where(codes[j] % 4 == e, ours[j], zero) for j in range(EDGES)], axis=0)
            for e in range(4)
        ],
        axis=1,
    )
    out = lax.dot_general(left, wide[...], (((0,), (0,)), ((), ())), preferred_element_type=F32)
    pixels = lines[pl.ds(LINES, 16), :].astype(BF)
    for e in range(4):
        for c in range(3):
            a, b = ((2, c), (c, 0), (0, c), (c, 2))[e]
            at = pl.ds((a * 3 + b) * C, C)
            part = out[e * 128 : e * 128 + C, c * 128 : (c + 1) * 128]
            grad[at, :] = grad[at, :] + jnp.where(upper, part, 0.0)
        met = jnp.dot(
            picked(corner_rows, me, e), corners_ref[pl.ds(e * 256, 256), :], preferred_element_type=F32
        ).astype(BF)
        part = lax.dot_general(pixels, met, (((0,), (0,)), ((), ())), preferred_element_type=F32)
        at = pl.ds(((e // 2) * 6 + (e % 2) * 2) * C, C)
        grad[at, :] = grad[at, :] + jnp.where(upper, part[:C], 0.0)


def reverse(kept, codes, precision=None):
    flip = (
        lax.broadcasted_iota(jnp.int32, (S, S), 0) + lax.broadcasted_iota(jnp.int32, (S, S), 1)
        == S - 1
    )
    flip = jnp.where(flip, 1.0, 0.0).astype(kept[0].dtype)
    flipped = jnp.dot(
        flip, jnp.concatenate(kept, axis=1), preferred_element_type=F32, precision=precision
    )
    return [
        jnp.where(codes[j] >= 4, flipped[:, j * 128 : (j + 1) * 128], kept[j].astype(F32))
        for j in range(EDGES)
    ]


def edge_terms(lines_ref, codes, w_edge, turned, wide, terms):
    lines = lines_ref[...].astype(F32)
    low = low_lanes(S)
    spot = lax.broadcasted_iota(jnp.int32, (LINES, 128), 0) % S
    after = jnp.where(spot == S - 1, 0.0, pltpu.roll(lines, LINES - 1, 0)).astype(BF)
    before = jnp.where(spot == 0, 0.0, pltpu.roll(lines, 1, 0)).astype(BF)
    wide[...] = jnp.concatenate([after, lines_ref[...], before], axis=1)
    terms[...] = jnp.dot(wide[...], w_edge[...], preferred_element_type=F32)
    kept = []
    for j in range(EDGES):
        e, at, tile = codes[j] & 3, pl.ds(j * S, S), (j % 4) // 2 * 128
        pair = jnp.where(e >= 2, terms[at, 128:256], terms[at, :128])
        rim = jnp.where((e & 1) == 1, pair, swap(pair))
        halo = jnp.where(
            codes[j] >= 4, terms[at, 512 + tile : 640 + tile], terms[at, 256 + tile : 384 + tile]
        )
        kept.append(jnp.where(low, swap(halo) if j % 2 else halo, rim.astype(BF).astype(F32)))
    for j, line in enumerate(reverse(kept, codes, lax.Precision.HIGHEST)):
        turned[pl.ds(j * S, S), :] = line


def raw_lines(lines_ref, codes, turned):
    kept = [lines_ref[pl.ds(j * S, S), :] for j in range(EDGES)]
    for j, line in enumerate(reverse(kept, codes)):
        turned[pl.ds(j * S, S), :] = line


def halo_in(pad, turned, cells):
    low16 = low_lanes(16)
    cells_swapped = swap(cells[...])
    for t in range(TL):
        for e, row in ((0, rows_at(t) + S), (2, rows_at(t) - 1)):
            base = (t * 4 + e) * S
            even = turned[pl.ds(base, NP, stride=2), :]
            odd = turned[pl.ds(base + 1, NP, stride=2), :]
            pad[pl.ds(PR + row, NP, stride=PR), :] = jnp.where(low16, even, swap(odd))
        pad[pl.ds(rows_at(t), S), :] = swap(turned[pl.ds((t * 4 + 1) * S, S), :])
        pad[pl.ds((PAIRS - 1) * PR + rows_at(t), S), :] = turned[pl.ds((t * 4 + 3) * S, S), :]
        for corner, (row, p) in enumerate(((-1, 0), (-1, 1), (S, 0), (S, 1))):
            at = t * 4 + corner
            value = (cells[...] if p else cells_swapped)[at : at + 1]
            pad[pl.ds(p * (PAIRS - 1) * PR + rows_at(t) + row, 1), :] = value


def picked(corner_rows, me, kind):
    slot = lax.broadcasted_iota(jnp.int32, (16, 256), 0)
    pick = (corner_rows[kind : kind + 1, :] == me * EDGES + slot) & (slot < EDGES)
    return jnp.where(pick, 1.0, 0.0).astype(BF)


def corner_sums(corners_ref, corner_rows, me, w_corner):
    total = None
    for kind in range(4):
        rim = jnp.dot(
            corners_ref[pl.ds(kind * 256, 256), :],
            w_corner[:, kind * 128 : (kind + 1) * 128],
            preferred_element_type=F32,
        ).astype(BF)
        part = jnp.dot(picked(corner_rows, me, kind), rim, preferred_element_type=F32)
        total = part if total is None else total + part
    return total


def cell_terms(cells, w_cell):
    every = jnp.dot(cells[...].astype(BF), w_cell[...], preferred_element_type=F32)
    kind = lax.broadcasted_iota(jnp.int32, (16, 128), 0) % 4
    total = jnp.zeros((16, 128), F32)
    for k in range(4):
        total = jnp.where(kind == k, every[:, k * 128 : (k + 1) * 128], total)
    return total


def add_edges(flat, turned, upper):
    low16, low32 = low_lanes(16), low_lanes(S)

    def at_low(v):
        return swap(v) if upper else v

    def at_high(v):
        return v if upper else swap(v)

    for t in range(TL):
        for e, i in ((0, S - 1), (2, 0)):
            base = (t * 4 + e) * S
            even = turned[pl.ds(base, NP, stride=2), :]
            odd = turned[pl.ds(base + 1, NP, stride=2), :]
            at = pl.ds(t * S + i, NP, stride=R)
            flat[at, :] = flat[at, :] + jnp.where(low16, at_low(even), at_high(odd))
        at = pl.ds(t * S, S)
        line = at_low(turned[pl.ds((t * 4 + 1) * S, S), :])
        flat[at, :] = flat[at, :] + jnp.where(low32, line, 0.0)
        at = pl.ds((NP - 1) * R + t * S, S)
        line = at_high(turned[pl.ds((t * 4 + 3) * S, S), :])
        flat[at, :] = flat[at, :] + jnp.where(low32, 0.0, line)


def add_cells(flat, cells):
    low16 = low_lanes(16)
    lows, highs = jnp.where(low16, cells, 0.0), jnp.where(low16, 0.0, cells)
    for t in range(TL):
        for corner, (i, p) in enumerate(((0, 0), (0, 1), (S - 1, 0), (S - 1, 1))):
            at = pl.ds(p * (NP - 1) * R + t * S + i, 1)
            s = t * 4 + corner
            flat[at, :] = flat[at, :] + (highs if p else lows)[s : s + 1]


def cells_of(corners_ref, places, me):
    slot = lax.broadcasted_iota(jnp.int32, (16, 1024), 0)
    row = jnp.full((16, 1024), -1, jnp.int32)
    for s in range(EDGES):
        v = places[s % 4, me * TL + s // 4]
        row = jnp.where(slot == s, (v & 3) * 256 + (v >> 2), row)
    pick = jnp.where(lax.broadcasted_iota(jnp.int32, (16, 1024), 1) == row, 1.0, 0.0).astype(BF)
    return jnp.dot(pick, corners_ref[...], preferred_element_type=F32)


def codes_of(seams, me):
    return [seams[j % 4, me * TL + j // 4] for j in range(EDGES)]


def load_rows(corner_rows, rows):
    corner_rows[...] = jnp.full((8, 256), -1, jnp.int32)
    corner_rows[0:4, 0:192] = rows[...]


def put_back(back, out):
    for q in range(NP // 2):
        for half in range(2):
            back[pl.ds((2 * q + half) * R, R), :] = out[q * R : (q + 1) * R, half * 128 : (half + 1) * 128]


def whole_kernel(
    f_hbm, c_hbm, w1_hbm, w2_hbm, adjacency_hbm, seams_hbm, places_hbm,
    output_hbm, field_grad_hbm, grad_one_hbm, grad_two_hbm,
    f_ref, c_ref, w1_ref, w2_ref, adjacency, seams, places, rows, loads, stores, corner_rows, index,
    output, field_grad, grad_one, grad_two,
    pad_f, pad_c, xp, qp, w_forth, w_back, w_forth_two, w_back_two, w_edge, w_edge_two,
    w_corner, w_cell, w_corner_two, w_cell_two,
    turned, raw, wide, wide_two, terms, cells, main, back, hid, lines, grads, hids, grad,
    sent_one, sent_two, near, near_two, corners, corners_two, out_grads, *refs,
):
    me = lax.axis_index("tile")
    inputs = [
        pltpu.make_async_copy(src, dst, loads.at[n])
        for n, (src, dst) in enumerate(
            (
                (f_hbm, f_ref), (c_hbm, c_ref), (w2_hbm, w2_ref), (w1_hbm, w1_ref),
                (adjacency_hbm, adjacency), (seams_hbm, seams), (places_hbm, places), (places_hbm, rows),
            )
        )
    ]
    for copy in inputs:
        copy.start()
    mesh = Mesh()
    mesh.greet()
    n = len(ROUND)
    one, two, rest = refs[:n], refs[n : 2 * n], refs[2 * n :]
    summed, parts, by_y, by_z, sent, come = rest
    net = Net(sent, come)
    inputs[0].wait()
    fill_pad(pad_f, f_ref)
    inputs[1].wait()
    fill_pad(pad_c, c_ref)
    put_lines(lines, pad_f, pad_c, pad_place, sent_one)
    mesh.meet()
    first = exchange_steps(mesh, net, index, sent_one, near, corners, one)
    next(first)
    for copy in inputs[4:]:
        copy.wait()
    find_index(mesh, adjacency, seams, index)
    load_rows(corner_rows, rows)
    make_shifts(qp, pad_c)
    next(first)
    inputs[2].wait()
    inputs[3].wait()
    make_shifts(xp, pad_f)
    w_edge[...] = jnp.zeros_like(w_edge)
    build_backward(w_back, w_edge, w_corner, w2_ref)
    next(first)
    next(first)
    put_back(back, conv(qp, w_back))
    build_forward(w_forth, w_edge, w_cell, w1_ref)
    put_back(main, conv(xp, w_forth))
    w_edge_two[...] = jnp.zeros_like(w_edge_two)
    build_backward(w_back_two, w_edge_two, w_corner_two, w1_ref)
    build_forward(w_forth_two, w_edge_two, w_cell_two, w2_ref)
    next(first)
    cells[...] = cells_of(corners, places, me)
    add_cells(main, cell_terms(cells, w_cell))
    add_cells(back, corner_sums(corners, corner_rows, me, w_corner))
    next(first)

    codes = codes_of(seams, me)
    edge_terms(near, codes, w_edge, turned, wide, terms)
    add_edges(main, turned, False)
    add_edges(back, turned, True)
    for p in range(NP):
        at = pl.ds(p * R, R)
        pre = main[at, :]
        s = 1.0 / (1.0 + jnp.exp(-pre))
        h = (pre * s).astype(BF)
        g = (back[at, :] * s * (1.0 + pre * (1.0 - s))).astype(BF)
        hid[at, :] = h.astype(F32)
        back[at, :] = g.astype(F32)
        grads[at, :] = g
        hids[at, :] = h
    put_lines(lines, hid, back, flat_place, sent_two)
    second = exchange_steps(mesh, net, index, sent_two, near_two, corners_two, two)
    next(second)

    raw_lines(near, codes, raw)
    halo_in(pad_f, raw, cells)
    patch_shifts(xp, pad_f)
    low = low_lanes(192)
    for a in range(3):
        grad[pl.ds(a * 192, 192), :] = jnp.where(
            low, first_part(xp, grads[...], a), second_part(qp, hids[...], a)
        )
    second_rims(grad, lines, wide, corners, corner_rows, codes, me)
    adding = total_steps(mesh, net, grad, out_grads, summed, parts, by_y, by_z)
    next(adding)
    next(second)
    fill_flat(pad_f, hid, True)
    make_shifts(xp, pad_f)
    next(second)
    next(adding)
    next(second)
    put_back(main, conv(xp, w_forth_two))
    fill_flat(pad_c, back, False)
    make_shifts(qp, pad_c)
    next(adding)
    put_back(back, conv(qp, w_back_two))
    next(second)
    cells[...] = cells_of(corners_two, places, me)
    add_cells(main, cell_terms(cells, w_cell_two))
    add_cells(back, corner_sums(corners_two, corner_rows, me, w_corner_two))
    next(adding)
    next(second)

    edge_terms(near_two, codes, w_edge_two, turned, wide_two, terms)
    add_edges(main, turned, False)
    add_edges(back, turned, True)
    for p in range(NP):
        at, lanes = pl.ds(p * R, R), slice(p * 128, (p + 1) * 128)
        output[:, lanes] = (f_ref[:, lanes].astype(F32) + main[at, :]).astype(BF)
        field_grad[:, lanes] = (c_ref[:, lanes].astype(F32) + back[at, :]).astype(BF)
    results = [
        pltpu.make_async_copy(src, dst, stores.at[n])
        for n, (src, dst) in enumerate(
            (
                (output, output_hbm), (field_grad, field_grad_hbm),
                (grad_one, grad_one_hbm), (grad_two, grad_two_hbm),
            )
        )
    ]
    results[0].start()
    results[1].start()
    next(adding)
    scale = 1.0 / math.sqrt(2 * 192 * S * S)
    grad_one[...] = out_grads[:, :C] * scale
    grad_two[...] = out_grads[:, C:] * scale
    results[2].start()
    results[3].start()
    net.finish()
    for copy in results:
        copy.wait()


def hand_over(*refs):
    ins, outs, held, come, gone = refs[:4], refs[4:8], refs[8:12], refs[12], refs[13]
    arrive = [pltpu.make_async_copy(a, b, come.at[n]) for n, (a, b) in enumerate(zip(ins, held))]
    leave = [pltpu.make_async_copy(a, b, gone.at[n]) for n, (a, b) in enumerate(zip(held, outs))]
    for copy in arrive:
        copy.start()
    for n in range(4):
        arrive[n].wait()
        leave[n].start()
    for copy in leave:
        copy.wait()


class Mesh:
    def __init__(self):
        self.t = t = lax.axis_index("tile")
        self.b = b = lax.axis_index("batch")
        self.z, self.y, self.x, self.core = z, y, x, core = t // 16, (t // 4) % 4, (t // 2) % 2, t % 2
        self.along_z = [(self.index((z + k) % 4, y, x, core), b) for k in range(1, 4)]
        self.along_y = [(self.index(z, (y + k) % 4, x, core), b) for k in range(1, 4)]
        self.sibling = (self.index(z, y, x, 1 - core), b)
        self.across = (self.index(z, y, 1 - x, core), b)
        self.group = x * 4 + b * 2 + core
        self.near = []
        for k in range(1, 8):
            g = (self.group + k) % 8
            self.near.append((self.index(z, y, g // 4, g % 2), (g // 2) % 2))

    def index(self, z, y, x, core):
        return z * 16 + y * 4 + x * 2 + core

    def greet(self):
        for other in self.along_z + self.along_y + self.near:
            pl.semaphore_signal(
                pltpu.get_barrier_semaphore(), inc=1, device_id=other, device_id_type=MESH
            )

    def meet(self):
        pl.semaphore_wait(pltpu.get_barrier_semaphore(), 13)


class Net:
    def __init__(self, sent, come):
        self.sent, self.come, self.copies = sent, come, []

    def send(self, src, dst, other):
        n = len(self.copies)
        copy = pltpu.make_async_remote_copy(
            src_ref=src, dst_ref=dst, send_sem=self.sent.at[n], recv_sem=self.come.at[n],
            device_id=other, device_id_type=MESH,
        )
        copy.start()
        self.copies.append(copy)
        return copy

    def finish(self):
        for copy in self.copies:
            copy.wait_send()


def find_index(mesh, adjacency, seams, index):
    z, y, x, core = mesh.z, mesh.y, mesh.x, mesh.core

    def decode(device, j):
        tile, code = adjacency[j % 4, device * TL + j // 4], seams[j % 4, device * TL + j // 4]
        source = (tile * 171) >> 9
        return source, (tile - source * 3) * 4 + (code & 3)

    for h in range(2):
        for k in range(4):
            device = mesh.index(z, (y + k) % 4, x, core) if h == 0 else mesh.index((z + k) % 4, y, x, core)
            for j in range(EDGES):
                source, line = decode(device, j)
                p = (source >> 4) if h == 0 else ((source >> 2) & 3)
                index[(h * 4 + k) * 12 + j] = (p * 4 + (source & 3)) * EDGES + line
                if k == 0:
                    q = ((source >> 2) & 3) if h == 0 else (source >> 4)
                    index[96 + h * 12 + j] = q * EDGES + j


def exchange_steps(mesh, net, index, x_ref, out_lines, out_corners, refs):
    held_a, held_b, chosen, got_a, got_b, cells, apart, ordered = refs
    held, got = (held_a, held_b), (got_a, got_b)
    z, y, x, core = mesh.z, mesh.y, mesh.x, mesh.core
    remote, sibling, across = net.send, mesh.sibling, mesh.across
    along_z, along_y = mesh.along_z, mesh.along_y
    chains = ((z, y, along_z, along_y), (y, z, along_y, along_z))

    def place(h, p, side):
        return held[h].at[pl.ds((p * 4 + side * 2 + core) * EDGES, EDGES)]

    first, over, passed, turn = [], [], [], []
    cell = ((core * 4 + y) * 4 + z) * 2
    for h, (p, _, _, _) in enumerate(chains):
        turn.append(remote(x_ref.at[pl.ds(h * EDGES, EDGES)], place(h, p, x), across))
    cell_x = remote(x_ref.at[2 * EDGES], cells.at[cell + x], across)
    for h, (p, _, others, _) in enumerate(chains):
        mine = x_ref.at[pl.ds(h * EDGES, EDGES)]
        first.append([remote(mine, place(h, p, x), other) for other in others])
    for h, (p, _, _, _) in enumerate(chains):
        over.append([remote(x_ref.at[pl.ds(h * EDGES, EDGES)], place(h, p, x), sibling)])
        held[h][pl.ds((p * 4 + x * 2 + core) * EDGES, EDGES)] = x_ref[pl.ds(h * EDGES, EDGES)]
    cells[cell + x] = x_ref[2 * EDGES]
    yield

    for h, (p, _, others, _) in enumerate(chains):
        turn[h].wait_recv()
        here = place(h, p, 1 - x)
        passed.append([remote(here, here, other) for other in others])
        over[h].append(remote(here, here, sibling))
    cell_x.wait_recv()
    here = cells.at[pl.ds(cell, 2)]
    cell_z = [remote(here, here, other) for other in along_z]
    for k in (0, 2, 1):
        for h, (p, _, _, _) in enumerate(chains):
            first[h][k].wait_recv()
            here = place(h, (p + 3 - k) % 4, x)
            over[h].append(remote(here, here, sibling))
    yield

    for copy in cell_z:
        copy.wait_recv()
    here = cells.at[pl.ds((core * 4 + y) * 8, 8)]
    cell_y = [remote(here, here, other) for other in along_y]
    for k in (0, 2, 1):
        for h, (p, _, _, _) in enumerate(chains):
            passed[h][k].wait_recv()
            here = place(h, (p + 3 - k) % 4, 1 - x)
            over[h].append(remote(here, here, sibling))
    yield

    second = []
    for h, (p, q, _, others) in enumerate(chains):
        for copy in over[h]:
            copy.wait_recv()
        second.append([])
        for k in (2, 1, 3, 0):
            for j in range(EDGES):
                chosen[h, k, j] = held[h][index[(h * 4 + k) * 12 + j]]
            if k:
                there = got[h].at[pl.ds(q * EDGES, EDGES)]
                second[h].append(remote(chosen.at[h, k], there, others[k - 1]))
            else:
                got[h][pl.ds(q * EDGES, EDGES)] = chosen[h, 0]
    for copy in cell_y:
        copy.wait_recv()
    here = cells.at[pl.ds(core * 32, 32)]
    last = remote(here, here, sibling)
    yield

    last.wait_recv()
    for d in range(64):
        apart[d * HALF : (d + 1) * HALF, :] = cells[
            (((d % 2) * 4 + (d // 4) % 4) * 4 + d // 16) * 2 + (d // 2) % 2
        ].astype(F32)
    for kind in range(4):
        for tile in range(TL):
            ordered[pl.ds(kind * 256 + tile, 64, stride=TL), :] = apart[
                pl.ds(tile * 4 + kind, 64, stride=HALF), :
            ]
        ordered[pl.ds(kind * 256 + 192, 64), :] = jnp.zeros((64, 128), F32)
    out_corners[...] = ordered[...].astype(BF)
    yield

    for h in range(2):
        for copy in second[h]:
            copy.wait_recv()
        for j in range(EDGES):
            out_lines[j * S + h * HALF : j * S + (h + 1) * HALF, :] = got[h][index[96 + h * 12 + j]]
    yield


def total_steps(mesh, net, grads, out_grads, summed, parts, by_y, by_z):
    z, y, group, remote = mesh.z, mesh.y, mesh.group, net.send

    def piece(ref, g):
        return ref.at[pl.ds(pl.multiple_of(g * SHARE, 8), SHARE)]

    scatter = [
        remote(piece(grads, (group + k) % 8), parts.at[group], mesh.near[k - 1]) for k in range(1, 8)
    ]
    parts[group] = grads[pl.ds(pl.multiple_of(group * SHARE, 8), SHARE), :]
    yield
    for copy in scatter:
        copy.wait_recv()
    total = parts[0]
    for g in range(1, 8):
        total = total + parts[g]
    by_y[y] = total
    add_y = [remote(by_y.at[y], by_y.at[y], other) for other in mesh.along_y]
    yield
    for copy in add_y:
        copy.wait_recv()
    by_z[z] = ((by_y[0] + by_y[1]) + by_y[2]) + by_y[3]
    add_z = [remote(by_z.at[z], by_z.at[z], other) for other in mesh.along_z]
    yield
    for copy in add_z:
        copy.wait_recv()
    total = ((by_z[0] + by_z[1]) + by_z[2]) + by_z[3]
    summed[...] = total
    out_grads[pl.ds(pl.multiple_of(group * SHARE, 8), SHARE), :] = total
    gather = [remote(summed, piece(out_grads, group), other) for other in mesh.near]
    yield
    for copy in gather:
        copy.wait_recv()
    yield


ROUND = [
    pltpu.VMEM((16 * EDGES, HALF, 128), BF),
    pltpu.VMEM((16 * EDGES, HALF, 128), BF),
    pltpu.VMEM((2, 4, EDGES, HALF, 128), BF),
    pltpu.VMEM((4 * EDGES, HALF, 128), BF),
    pltpu.VMEM((4 * EDGES, HALF, 128), BF),
    pltpu.VMEM((64, HALF, 128), BF),
    pltpu.VMEM((1024, 128), F32),
    pltpu.VMEM((1024, 128), F32),
]
COPIES = 2 * (2 + 1 + 6 + 2 + 6 + 2 + 3 + 6 + 3 + 6 + 6 + 1) + 7 + 3 + 3 + 7


def body(fields, cotangent, first_kernel, second_kernel, adjacency, seam_codes, corner_map):
    f = fields.reshape(R, S * C)
    c = cotangent.reshape(R, S * C)
    tables = (adjacency.T, seam_codes.T, corner_map.T)
    pad, shifts = pltpu.VMEM((PAIRS * PR, 128), F32), pltpu.VMEM((3, PAIRS, R, 128), BF)
    w_conv, w_edge = pltpu.VMEM((3, 512, 256), BF), pltpu.VMEM((384, 768), BF)
    w_corner = pltpu.VMEM((128, 512), BF)
    flat, flat_low = pltpu.VMEM((NP * R, 128), F32), pltpu.VMEM((NP * R, 128), BF)
    turned, shifted = pltpu.VMEM((LINES, 128), F32), pltpu.VMEM((LINES, 384), BF)
    terms, sixteen = pltpu.VMEM((LINES, 768), F32), pltpu.VMEM((16, 128), F32)
    kernel, kernel_sum = pltpu.VMEM((3, 3, C, C), F32), pltpu.VMEM((9 * C, C), F32)
    tile, sums = pltpu.VMEM((R, S * C), BF), pltpu.VMEM((9 * C, 128), F32)
    blocks = pltpu.VMEM((2 * EDGES + 1, HALF, 128), BF)
    near, corners = pltpu.VMEM((LINES, 128), BF), pltpu.VMEM((1024, 128), BF)
    hbm = pl.BlockSpec(memory_space=pltpu.HBM)
    small = pltpu.SMEM((4, 192), jnp.int32)
    sem = pltpu.SemaphoreType.DMA
    shapes = tuple(jax.ShapeDtypeStruct(r.shape, r.dtype) for r in (tile, tile, kernel_sum, kernel_sum))
    results = pl.pallas_call(
        whole_kernel,
        out_shape=shapes,
        in_specs=[hbm] * 7,
        out_specs=(hbm,) * 4,
        scratch_shapes=[tile, tile, kernel, kernel, small, small, small]
        + [pltpu.VMEM((4, 192), jnp.int32), sem((8,)), sem((4,)), pltpu.VMEM((8, 256), jnp.int32)]
        + [pltpu.SMEM((120,), jnp.int32), tile, tile, kernel_sum, kernel_sum]
        + [pad, pad, shifts, shifts, w_conv, w_conv, w_conv, w_conv, w_edge, w_edge]
        + [w_corner] * 4
        + [turned, turned, shifted, shifted, terms, sixteen, flat, flat, flat]
        + [pltpu.VMEM((LINES + HALF, 128), F32), flat_low, flat_low, sums]
        + [blocks, blocks, near, near, corners, corners, sums]
        + ROUND * 2
        + [pltpu.VMEM((SHARE, 128), F32)]
        + [pltpu.VMEM((k, SHARE, 128), F32) for k in (8, 4, 4)]
        + [sem((COPIES,))] * 2,
        name="whole",
        compiler_params=pltpu.CompilerParams(
            collective_id=0, has_side_effects=True, vmem_limit_bytes=54 * 2**20
        ),
    )(f, c, first_kernel, second_kernel, *tables)
    output, field_grad, grad_one, grad_two = pl.pallas_call(
        hand_over,
        out_shape=shapes,
        in_specs=[hbm] * 4,
        out_specs=(hbm,) * 4,
        scratch_shapes=[tile, tile, kernel_sum, kernel_sum, sem((4,)), sem((4,))],
        name="hand_over",
        compiler_params=pltpu.CompilerParams(vmem_limit_bytes=58 * 2**20),
    )(*results)
    shape_out = (1, TL, S, S * C)
    return (
        output.reshape(shape_out),
        field_grad.reshape(shape_out),
        grad_one.reshape(3, 3, C, C),
        grad_two.reshape(3, 3, C, C),
    )


def solution(mesh):
    split = P("batch", "tile", None, None)
    return jax.shard_map(
        body,
        mesh=mesh,
        in_specs=(split, split, P(), P(), P(), P(), P()),
        out_specs=(split, split, P(), P()),
        check_vma=False,
    )
```

```python
import math

import jax
import jax.numpy as jnp
from jax import lax
from jax.experimental import pallas as pl
from jax.experimental.pallas import tpu as pltpu
from jax.sharding import PartitionSpec as P

TL = 3
S = 32
C = 64
NP = 16
R = TL * S
EDGES = TL * 4
LINES = EDGES * S
HALF = S // 2
SHARE = 9 * C // 8
PAIRS = NP + 2
PR = 128
MESH = pl.DeviceIdType.MESH
F32 = jnp.float32
BF = jnp.bfloat16


def rows_at(t):
    return t * 40 + 8


def low_lanes(rows):
    return lax.broadcasted_iota(jnp.int32, (rows, 128), 1) < C


def swap(v):
    return pltpu.roll(v, C, 1)


def put_lines(lines, first, second, place, out):
    low16, low32 = low_lanes(16), low_lanes(32)
    step = place(1, 0) - place(0, 0)
    for t in range(TL):
        for e, i in ((0, S - 1), (2, 0)):
            where = pl.ds(place(0, t) + i, NP, stride=step)
            a, b = first[where, :], second[where, :]
            base = (t * 4 + e) * S
            lines[pl.ds(base, NP, stride=2), :] = jnp.where(low16, a, swap(b))
            lines[pl.ds(base + 1, NP, stride=2), :] = jnp.where(low16, swap(a), b)
        for e, pair in ((1, 0), (3, NP - 1)):
            where = pl.ds(place(pair, t), S)
            a, b = first[where, :], second[where, :]
            line = jnp.where(low32, a, swap(b)) if e == 1 else jnp.where(low32, swap(a), b)
            lines[pl.ds((t * 4 + e) * S, S), :] = line
        for corner, (e, s) in enumerate(((2, 0), (2, S - 1), (0, 0), (0, S - 1))):
            lines[pl.ds(LINES + t * 4 + corner, 1), :] = lines[pl.ds((t * 4 + e) * S + s, 1), :]
    lines[pl.ds(LINES + EDGES, HALF - EDGES), :] = jnp.zeros((HALF - EDGES, 128), F32)
    for j in range(EDGES):
        for h in range(2):
            out[h * EDGES + j] = lines[pl.ds(j * S + h * HALF, HALF), :].astype(BF)
    out[2 * EDGES] = lines[pl.ds(LINES, HALF), :].astype(BF)


def fill_pad(pad, src):
    for p in (0, PAIRS - 1):
        pad[pl.ds(p * PR, PR), :] = jnp.zeros((PR, 128), F32)
    for p in range(NP):
        for t in range(TL):
            base = (p + 1) * PR + rows_at(t)
            pad[pl.ds(base - 8, 8), :] = jnp.zeros((8, 128), F32)
            pad[pl.ds(base, S), :] = src[t * S : (t + 1) * S, p * 128 : (p + 1) * 128].astype(F32)
        pad[pl.ds((p + 1) * PR + 120, 8), :] = jnp.zeros((8, 128), F32)


def fill_flat(pad, flat, zero):
    if zero:
        pad[...] = jnp.zeros_like(pad)
    for p in range(NP):
        for t in range(TL):
            pad[pl.ds(pad_place(p, t), S), :] = flat[pl.ds(flat_place(p, t), S), :]


def patch_shifts(xp, pad):
    for t in range(TL):
        for p in (0, PAIRS - 1):
            for a in range(3):
                xp[a, p, t * S : (t + 1) * S, :] = pad[pl.ds(p * PR + rows_at(t) - 1 + a, S), :].astype(BF)
        for p in range(1, PAIRS - 1):
            first = p * PR + rows_at(t)
            xp[0, p, t * S : t * S + HALF, :] = pad[pl.ds(first - 1, HALF), :].astype(BF)
            xp[2, p, t * S + HALF : (t + 1) * S, :] = pad[pl.ds(first + HALF + 1, HALF), :].astype(BF)


def pad_place(pair, t):
    return (pair + 1) * PR + rows_at(t)


def flat_place(pair, t):
    return pair * R + t * S


def make_shifts(xp, pad):
    for a in range(3):
        for p in range(PAIRS):
            for t in range(TL):
                xp[a, p, t * S : (t + 1) * S, :] = pad[pl.ds(p * PR + rows_at(t) - 1 + a, S), :].astype(BF)


def edge_taps(a, c):
    return [
        spot for spot in ((0, c), (1, a), (2, c), (3, a)) if (a == 2, c == 0, a == 0, c == 2)[spot[0]]
    ]


def build_forward(w_out, w_edge, w_cell, w):
    w_out[...] = jnp.zeros_like(w_out)
    w_cell[...] = jnp.zeros_like(w_cell)
    for a in range(3):
        for c in range(3):
            block = w[a, c].astype(BF)
            for n in range(4):
                m = n + 1 + c
                w_out[a, m * C : (m + 1) * C, n * C : (n + 1) * C] = block
            for e, tap in edge_taps(a, c):
                w_edge[(2 - tap) * 128 : (2 - tap) * 128 + C, 256 + e * C : 256 + (e + 1) * C] = block
                w_edge[tap * 128 : tap * 128 + C, 512 + e * C : 512 + (e + 1) * C] = block
            if a != 1 and c != 1:
                at = ((a // 2) * 2 + c // 2) * 128
                w_cell[:C, at : at + C] = block
                w_cell[:C, at + C : at + 128] = block


def build_backward(w_out, w_edge, w_corner, w):
    w_out[...] = jnp.zeros_like(w_out)
    w_corner[...] = jnp.zeros_like(w_corner)
    for a in range(3):
        for c in range(3):
            block = w[a, c].T.astype(BF)
            for n in range(4):
                m = n + 3 - c
                w_out[2 - a, m * C : (m + 1) * C, n * C : (n + 1) * C] = block
            for e, tap in edge_taps(a, c):
                w_edge[tap * 128 + C : tap * 128 + 128, e * C : (e + 1) * C] = block
            if a != 1 and c != 1:
                at = ((a // 2) * 2 + c // 2) * 128
                w_corner[C:128, at : at + C] = block
                w_corner[C:128, at + C : at + 128] = block


def conv(xp, w):
    total = None
    for a in range(3):
        left = jnp.concatenate(
            [
                jnp.concatenate([xp[a, 2 * q + s] for q in range(NP // 2)], axis=0)
                for s in range(4)
            ],
            axis=1,
        )
        part = jnp.dot(left, w[a], preferred_element_type=F32)
        total = part if total is None else total + part
    return total


def columns(xp, a):
    return jnp.concatenate(
        [jnp.concatenate([xp[a, d + p] for p in range(NP)], axis=0) for d in range(3)], axis=1
    )


def first_part(xp, q, a):
    out = lax.dot_general(q, columns(xp, a), (((0,), (0,)), ((), ())), preferred_element_type=F32)
    turned = jnp.concatenate([out[:, d * 128 : (d + 1) * 128].T for d in range(3)], axis=0)
    return turned[64:256] + swap(turned[128:320])


def second_part(qp, h, a):
    out = lax.dot_general(h, columns(qp, 2 - a), (((0,), (0,)), ((), ())), preferred_element_type=F32)
    even, odd = out[:C], out[C:]
    return jnp.concatenate(
        [
            even[:, 128:256] + swap(odd[:, 256:384]),
            swap(even[:, 128:256]) + odd[:, 128:256],
            even[:, :128] + swap(odd[:, 128:256]),
        ],
        axis=0,
    )


def second_rims(grad, lines, wide, corners_ref, corner_rows, codes, me):
    upper = jnp.logical_not(low_lanes(C))
    kept = [lines[pl.ds(j * S, S), :].astype(BF) for j in range(EDGES)]
    ours = [line.astype(BF) for line in reverse(kept, codes)]
    zero = jnp.zeros((S, 128), BF)
    left = jnp.concatenate(
        [
            jnp.concatenate([jnp.where(codes[j] % 4 == e, ours[j], zero) for j in range(EDGES)], axis=0)
            for e in range(4)
        ],
        axis=1,
    )
    out = lax.dot_general(left, wide[...], (((0,), (0,)), ((), ())), preferred_element_type=F32)
    pixels = lines[pl.ds(LINES, 16), :].astype(BF)
    for e in range(4):
        for c in range(3):
            a, b = ((2, c), (c, 0), (0, c), (c, 2))[e]
            at = pl.ds((a * 3 + b) * C, C)
            part = out[e * 128 : e * 128 + C, c * 128 : (c + 1) * 128]
            grad[at, :] = grad[at, :] + jnp.where(upper, part, 0.0)
        met = jnp.dot(
            picked(corner_rows, me, e), corners_ref[pl.ds(e * 256, 256), :], preferred_element_type=F32
        ).astype(BF)
        part = lax.dot_general(pixels, met, (((0,), (0,)), ((), ())), preferred_element_type=F32)
        at = pl.ds(((e // 2) * 6 + (e % 2) * 2) * C, C)
        grad[at, :] = grad[at, :] + jnp.where(upper, part[:C], 0.0)


def reverse(kept, codes, precision=None):
    flip = (
        lax.broadcasted_iota(jnp.int32, (S, S), 0) + lax.broadcasted_iota(jnp.int32, (S, S), 1)
        == S - 1
    )
    flip = jnp.where(flip, 1.0, 0.0).astype(kept[0].dtype)
    flipped = jnp.dot(
        flip, jnp.concatenate(kept, axis=1), preferred_element_type=F32, precision=precision
    )
    return [
        jnp.where(codes[j] >= 4, flipped[:, j * 128 : (j + 1) * 128], kept[j].astype(F32))
        for j in range(EDGES)
    ]


def edge_terms(lines_ref, codes, w_edge, turned, wide, terms):
    lines = lines_ref[...].astype(F32)
    low = low_lanes(S)
    spot = lax.broadcasted_iota(jnp.int32, (LINES, 128), 0) % S
    after = jnp.where(spot == S - 1, 0.0, pltpu.roll(lines, LINES - 1, 0)).astype(BF)
    before = jnp.where(spot == 0, 0.0, pltpu.roll(lines, 1, 0)).astype(BF)
    wide[...] = jnp.concatenate([after, lines_ref[...], before], axis=1)
    terms[...] = jnp.dot(wide[...], w_edge[...], preferred_element_type=F32)
    kept = []
    for j in range(EDGES):
        e, at, tile = codes[j] & 3, pl.ds(j * S, S), (j % 4) // 2 * 128
        pair = jnp.where(e >= 2, terms[at, 128:256], terms[at, :128])
        rim = jnp.where((e & 1) == 1, pair, swap(pair))
        halo = jnp.where(
            codes[j] >= 4, terms[at, 512 + tile : 640 + tile], terms[at, 256 + tile : 384 + tile]
        )
        kept.append(jnp.where(low, swap(halo) if j % 2 else halo, rim.astype(BF).astype(F32)))
    for j, line in enumerate(reverse(kept, codes, lax.Precision.HIGHEST)):
        turned[pl.ds(j * S, S), :] = line


def raw_lines(lines_ref, codes, turned):
    kept = [lines_ref[pl.ds(j * S, S), :] for j in range(EDGES)]
    for j, line in enumerate(reverse(kept, codes)):
        turned[pl.ds(j * S, S), :] = line


def halo_in(pad, turned, cells):
    low16 = low_lanes(16)
    cells_swapped = swap(cells[...])
    for t in range(TL):
        for e, row in ((0, rows_at(t) + S), (2, rows_at(t) - 1)):
            base = (t * 4 + e) * S
            even = turned[pl.ds(base, NP, stride=2), :]
            odd = turned[pl.ds(base + 1, NP, stride=2), :]
            pad[pl.ds(PR + row, NP, stride=PR), :] = jnp.where(low16, even, swap(odd))
        pad[pl.ds(rows_at(t), S), :] = swap(turned[pl.ds((t * 4 + 1) * S, S), :])
        pad[pl.ds((PAIRS - 1) * PR + rows_at(t), S), :] = turned[pl.ds((t * 4 + 3) * S, S), :]
        for corner, (row, p) in enumerate(((-1, 0), (-1, 1), (S, 0), (S, 1))):
            at = t * 4 + corner
            value = (cells[...] if p else cells_swapped)[at : at + 1]
            pad[pl.ds(p * (PAIRS - 1) * PR + rows_at(t) + row, 1), :] = value


def picked(corner_rows, me, kind):
    slot = lax.broadcasted_iota(jnp.int32, (16, 256), 0)
    pick = (corner_rows[kind : kind + 1, :] == me * EDGES + slot) & (slot < EDGES)
    return jnp.where(pick, 1.0, 0.0).astype(BF)


def corner_sums(corners_ref, corner_rows, me, w_corner):
    total = None
    for kind in range(4):
        rim = jnp.dot(
            corners_ref[pl.ds(kind * 256, 256), :],
            w_corner[:, kind * 128 : (kind + 1) * 128],
            preferred_element_type=F32,
        ).astype(BF)
        part = jnp.dot(picked(corner_rows, me, kind), rim, preferred_element_type=F32)
        total = part if total is None else total + part
    return total


def cell_terms(cells, w_cell):
    every = jnp.dot(cells[...].astype(BF), w_cell[...], preferred_element_type=F32)
    kind = lax.broadcasted_iota(jnp.int32, (16, 128), 0) % 4
    total = jnp.zeros((16, 128), F32)
    for k in range(4):
        total = jnp.where(kind == k, every[:, k * 128 : (k + 1) * 128], total)
    return total


def add_edges(flat, turned, upper):
    low16, low32 = low_lanes(16), low_lanes(S)

    def at_low(v):
        return swap(v) if upper else v

    def at_high(v):
        return v if upper else swap(v)

    for t in range(TL):
        for e, i in ((0, S - 1), (2, 0)):
            base = (t * 4 + e) * S
            even = turned[pl.ds(base, NP, stride=2), :]
            odd = turned[pl.ds(base + 1, NP, stride=2), :]
            at = pl.ds(t * S + i, NP, stride=R)
            flat[at, :] = flat[at, :] + jnp.where(low16, at_low(even), at_high(odd))
        at = pl.ds(t * S, S)
        line = at_low(turned[pl.ds((t * 4 + 1) * S, S), :])
        flat[at, :] = flat[at, :] + jnp.where(low32, line, 0.0)
        at = pl.ds((NP - 1) * R + t * S, S)
        line = at_high(turned[pl.ds((t * 4 + 3) * S, S), :])
        flat[at, :] = flat[at, :] + jnp.where(low32, 0.0, line)


def add_cells(flat, cells):
    low16 = low_lanes(16)
    lows, highs = jnp.where(low16, cells, 0.0), jnp.where(low16, 0.0, cells)
    for t in range(TL):
        for corner, (i, p) in enumerate(((0, 0), (0, 1), (S - 1, 0), (S - 1, 1))):
            at = pl.ds(p * (NP - 1) * R + t * S + i, 1)
            s = t * 4 + corner
            flat[at, :] = flat[at, :] + (highs if p else lows)[s : s + 1]


def cells_of(corners_ref, places, me):
    slot = lax.broadcasted_iota(jnp.int32, (16, 1024), 0)
    row = jnp.full((16, 1024), -1, jnp.int32)
    for s in range(EDGES):
        v = places[s % 4, me * TL + s // 4]
        row = jnp.where(slot == s, (v & 3) * 256 + (v >> 2), row)
    pick = jnp.where(lax.broadcasted_iota(jnp.int32, (16, 1024), 1) == row, 1.0, 0.0).astype(BF)
    return jnp.dot(pick, corners_ref[...], preferred_element_type=F32)


def codes_of(seams, me):
    return [seams[j % 4, me * TL + j // 4] for j in range(EDGES)]


def load_rows(corner_rows, rows):
    corner_rows[...] = jnp.full((8, 256), -1, jnp.int32)
    corner_rows[0:4, 0:192] = rows[...]


def put_back(back, out):
    for q in range(NP // 2):
        for half in range(2):
            back[pl.ds((2 * q + half) * R, R), :] = out[q * R : (q + 1) * R, half * 128 : (half + 1) * 128]


def whole_kernel(
    f_hbm, c_hbm, w1_hbm, w2_hbm, adjacency_hbm, seams_hbm, places_hbm,
    output_hbm, field_grad_hbm, grad_one_hbm, grad_two_hbm,
    f_ref, c_ref, w1_ref, w2_ref, adjacency, seams, places, rows, loads, stores, corner_rows, index,
    output, field_grad, grad_one, grad_two,
    pad_f, pad_c, xp, qp, w_forth, w_back, w_forth_two, w_back_two, w_edge, w_edge_two,
    w_corner, w_cell, w_corner_two, w_cell_two,
    turned, raw, wide, wide_two, terms, cells, main, back, hid, lines, grads, hids, grad,
    sent_one, sent_two, near, near_two, corners, corners_two, out_grads, *refs,
):
    me = lax.axis_index("tile")
    inputs = [
        pltpu.make_async_copy(src, dst, loads.at[n])
        for n, (src, dst) in enumerate(
            (
                (f_hbm, f_ref), (c_hbm, c_ref), (w2_hbm, w2_ref), (w1_hbm, w1_ref),
                (adjacency_hbm, adjacency), (seams_hbm, seams), (places_hbm, places), (places_hbm, rows),
            )
        )
    ]
    for copy in inputs:
        copy.start()
    mesh = Mesh()
    mesh.greet()
    n = len(ROUND)
    one, two, rest = refs[:n], refs[n : 2 * n], refs[2 * n :]
    summed, parts, by_y, by_z, leaving, sent, come = rest
    net = Net(sent, come)
    inputs[0].wait()
    fill_pad(pad_f, f_ref)
    inputs[1].wait()
    fill_pad(pad_c, c_ref)
    put_lines(lines, pad_f, pad_c, pad_place, sent_one)
    mesh.meet()
    first = exchange_steps(mesh, net, index, sent_one, near, corners, one)
    next(first)
    for copy in inputs[2:]:
        copy.wait()
    make_shifts(qp, pad_c)
    next(first)
    find_index(mesh, adjacency, seams, index)
    load_rows(corner_rows, rows)
    next(first)
    w_edge[...] = jnp.zeros_like(w_edge)
    next(first)
    make_shifts(xp, pad_f)
    build_backward(w_back, w_edge, w_corner, w2_ref)
    put_back(back, conv(qp, w_back))
    build_forward(w_forth, w_edge, w_cell, w1_ref)
    put_back(main, conv(xp, w_forth))
    w_edge_two[...] = jnp.zeros_like(w_edge_two)
    build_backward(w_back_two, w_edge_two, w_corner_two, w1_ref)
    build_forward(w_forth_two, w_edge_two, w_cell_two, w2_ref)
    next(first)
    cells[...] = cells_of(corners, places, me)
    add_cells(main, cell_terms(cells, w_cell))
    add_cells(back, corner_sums(corners, corner_rows, me, w_corner))
    next(first)

    codes = codes_of(seams, me)
    edge_terms(near, codes, w_edge, turned, wide, terms)
    add_edges(main, turned, False)
    add_edges(back, turned, True)
    for p in range(NP):
        at = pl.ds(p * R, R)
        pre = main[at, :]
        s = 1.0 / (1.0 + jnp.exp(-pre))
        h = (pre * s).astype(BF)
        g = (back[at, :] * s * (1.0 + pre * (1.0 - s))).astype(BF)
        hid[at, :] = h.astype(F32)
        back[at, :] = g.astype(F32)
        grads[at, :] = g
        hids[at, :] = h
    put_lines(lines, hid, back, flat_place, sent_two)
    second = exchange_steps(mesh, net, index, sent_two, near_two, corners_two, two)
    sofar = len(net.copies)
    next(second)
    net.drain(sofar)

    raw_lines(near, codes, raw)
    halo_in(pad_f, raw, cells)
    patch_shifts(xp, pad_f)
    low = low_lanes(192)
    for a in range(3):
        grad[pl.ds(a * 192, 192), :] = jnp.where(
            low, first_part(xp, grads[...], a), second_part(qp, hids[...], a)
        )
    second_rims(grad, lines, wide, corners, corner_rows, codes, me)
    adding = total_steps(mesh, net, grad, out_grads, summed, parts, by_y, by_z, leaving)
    next(adding)
    next(second)
    fill_flat(pad_f, hid, True)
    make_shifts(xp, pad_f)
    next(adding)
    next(second)
    put_back(main, conv(xp, w_forth_two))
    next(second)
    next(adding)
    fill_flat(pad_c, back, False)
    make_shifts(qp, pad_c)
    put_back(back, conv(qp, w_back_two))
    sofar = len(net.copies)
    next(adding)
    net.drain(sofar)
    next(second)
    cells[...] = cells_of(corners_two, places, me)
    add_cells(main, cell_terms(cells, w_cell_two))
    add_cells(back, corner_sums(corners_two, corner_rows, me, w_corner_two))
    next(second)

    edge_terms(near_two, codes, w_edge_two, turned, wide_two, terms)
    add_edges(main, turned, False)
    add_edges(back, turned, True)
    for p in range(NP):
        at, lanes = pl.ds(p * R, R), slice(p * 128, (p + 1) * 128)
        output[:, lanes] = (f_ref[:, lanes].astype(F32) + main[at, :]).astype(BF)
        field_grad[:, lanes] = (c_ref[:, lanes].astype(F32) + back[at, :]).astype(BF)
    results = [
        pltpu.make_async_copy(src, dst, stores.at[n])
        for n, (src, dst) in enumerate(
            (
                (output, output_hbm), (field_grad, field_grad_hbm),
                (grad_one, grad_one_hbm), (grad_two, grad_two_hbm),
            )
        )
    ]
    results[0].start()
    results[1].start()
    next(adding)
    scale = 1.0 / math.sqrt(2 * 192 * S * S)
    for g in range(8):
        share = out_grads[g].astype(F32)[:SHARE] * scale
        grad_one[pl.ds(g * SHARE, SHARE), :] = share[:, :C]
        grad_two[pl.ds(g * SHARE, SHARE), :] = share[:, C:]
    results[2].start()
    results[3].start()
    net.drain()
    for copy in results:
        copy.wait()


def hand_over(*refs):
    ins, outs, held, come, gone = refs[:4], refs[4:8], refs[8:12], refs[12], refs[13]
    arrive = [pltpu.make_async_copy(a, b, come.at[n]) for n, (a, b) in enumerate(zip(ins, held))]
    leave = [pltpu.make_async_copy(a, b, gone.at[n]) for n, (a, b) in enumerate(zip(held, outs))]
    for copy in arrive:
        copy.start()
    for n in range(4):
        arrive[n].wait()
        leave[n].start()
    for copy in leave:
        copy.wait()


class Mesh:
    def __init__(self):
        self.t = t = lax.axis_index("tile")
        self.b = b = lax.axis_index("batch")
        self.z, self.y, self.x, self.core = z, y, x, core = t // 16, (t // 4) % 4, (t // 2) % 2, t % 2
        self.along_z = [(self.index((z + k) % 4, y, x, core), b) for k in range(1, 4)]
        self.along_y = [(self.index(z, (y + k) % 4, x, core), b) for k in range(1, 4)]
        self.sibling = (self.index(z, y, x, 1 - core), b)
        self.across = (self.index(z, y, 1 - x, core), b)
        self.group = x * 4 + b * 2 + core
        self.near = []
        for k in range(1, 8):
            g = (self.group + k) % 8
            self.near.append((self.index(z, y, g // 4, g % 2), (g // 2) % 2))

    def index(self, z, y, x, core):
        return z * 16 + y * 4 + x * 2 + core

    def greet(self):
        for other in self.along_z + self.along_y + self.near:
            pl.semaphore_signal(
                pltpu.get_barrier_semaphore(), inc=1, device_id=other, device_id_type=MESH
            )

    def meet(self):
        pl.semaphore_wait(pltpu.get_barrier_semaphore(), 13)


class Net:
    def __init__(self, sent, come):
        self.sent, self.come, self.copies, self.waited = sent, come, [], 0

    def send(self, src, dst, other):
        n = len(self.copies)
        copy = pltpu.make_async_remote_copy(
            src_ref=src, dst_ref=dst, send_sem=self.sent.at[n], recv_sem=self.come.at[n],
            device_id=other, device_id_type=MESH,
        )
        copy.start()
        self.copies.append(copy)
        return copy

    def drain(self, stop=None):
        stop = len(self.copies) if stop is None else stop
        for copy in self.copies[self.waited : stop]:
            copy.wait_send()
        self.waited = stop


def find_index(mesh, adjacency, seams, index):
    z, y, x, core = mesh.z, mesh.y, mesh.x, mesh.core

    def decode(device, j):
        tile, code = adjacency[j % 4, device * TL + j // 4], seams[j % 4, device * TL + j // 4]
        source = (tile * 171) >> 9
        return source, (tile - source * 3) * 4 + (code & 3)

    for h in range(2):
        for k in range(4):
            device = mesh.index(z, (y + k) % 4, x, core) if h == 0 else mesh.index((z + k) % 4, y, x, core)
            for j in range(EDGES):
                source, line = decode(device, j)
                p = (source >> 4) if h == 0 else ((source >> 2) & 3)
                index[(h * 4 + k) * 12 + j] = ((source & 1) * 8 + ((source >> 1) & 1) * 4 + p) * EDGES + line
                if k == 0:
                    q = ((source >> 2) & 3) if h == 0 else (source >> 4)
                    index[96 + h * 12 + j] = q * EDGES + j


def exchange_steps(mesh, net, index, x_ref, out_lines, out_corners, refs):
    held_a, held_b, chosen, got_a, got_b, cells, apart, ordered = refs
    held, got = (held_a, held_b), (got_a, got_b)
    z, y, x, core = mesh.z, mesh.y, mesh.x, mesh.core
    remote, sibling, across = net.send, mesh.sibling, mesh.across
    along_z, along_y = mesh.along_z, mesh.along_y
    chains = ((z, y, along_z, along_y), (y, z, along_y, along_z))

    def place(h, p, side):
        return held[h].at[pl.ds((core * 8 + side * 4 + p) * EDGES, EDGES)]

    def column(h, side):
        return held[h].at[pl.ds((core * 8 + side * 4) * EDGES, 4 * EDGES)]

    first, over, passed, turn = [], [], [], []
    cell = ((core * 4 + y) * 4 + z) * 2
    for h, (p, _, _, _) in enumerate(chains):
        turn.append(remote(x_ref.at[pl.ds(h * EDGES, EDGES)], place(h, p, x), across))
    cell_x = remote(x_ref.at[2 * EDGES], cells.at[cell + x], across)
    for h, (p, _, others, _) in enumerate(chains):
        mine = x_ref.at[pl.ds(h * EDGES, EDGES)]
        first.append([remote(mine, place(h, p, x), other) for other in others])
    for h, (p, _, _, _) in enumerate(chains):
        over.append([])
        held[h][pl.ds((core * 8 + x * 4 + p) * EDGES, EDGES)] = x_ref[pl.ds(h * EDGES, EDGES)]
    cells[cell + x] = x_ref[2 * EDGES]
    yield

    for h, (p, _, others, _) in enumerate(chains):
        turn[h].wait_recv()
        here = place(h, p, 1 - x)
        passed.append([remote(here, here, other) for other in others])
    cell_x.wait_recv()
    here = cells.at[pl.ds(cell, 2)]
    cell_z = [remote(here, here, other) for other in along_z]
    for h in range(2):
        for copy in first[h]:
            copy.wait_recv()
        over[h].append(remote(column(h, x), column(h, x), sibling))
    yield

    for copy in cell_z:
        copy.wait_recv()
    here = cells.at[pl.ds((core * 4 + y) * 8, 8)]
    cell_y = [remote(here, here, other) for other in along_y]
    for h in range(2):
        for copy in passed[h]:
            copy.wait_recv()
        over[h].append(remote(column(h, 1 - x), column(h, 1 - x), sibling))
    yield

    second = []
    for h, (p, q, _, others) in enumerate(chains):
        for copy in over[h]:
            copy.wait_recv()
        second.append([])
        for k in (2, 1, 3, 0):
            for j in range(EDGES):
                chosen[h, k, j] = held[h][index[(h * 4 + k) * 12 + j]]
            if k:
                there = got[h].at[pl.ds(q * EDGES, EDGES)]
                second[h].append(remote(chosen.at[h, k], there, others[k - 1]))
            else:
                got[h][pl.ds(q * EDGES, EDGES)] = chosen[h, 0]
    for copy in cell_y:
        copy.wait_recv()
    here = cells.at[pl.ds(core * 32, 32)]
    last = remote(here, here, sibling)
    yield

    last.wait_recv()
    for d in range(64):
        apart[d * HALF : (d + 1) * HALF, :] = cells[
            (((d % 2) * 4 + (d // 4) % 4) * 4 + d // 16) * 2 + (d // 2) % 2
        ].astype(F32)
    for kind in range(4):
        for tile in range(TL):
            ordered[pl.ds(kind * 256 + tile, 64, stride=TL), :] = apart[
                pl.ds(tile * 4 + kind, 64, stride=HALF), :
            ]
        ordered[pl.ds(kind * 256 + 192, 64), :] = jnp.zeros((64, 128), F32)
    out_corners[...] = ordered[...].astype(BF)
    yield

    for h in range(2):
        for copy in second[h]:
            copy.wait_recv()
        for j in range(EDGES):
            out_lines[j * S + h * HALF : j * S + (h + 1) * HALF, :] = got[h][index[96 + h * 12 + j]]
    yield


def total_steps(mesh, net, grads, out_grads, summed, parts, by_y, by_z, leaving):
    z, y, group, remote = mesh.z, mesh.y, mesh.group, net.send

    def piece(ref, g):
        return ref.at[pl.ds(pl.multiple_of(g * SHARE, 8), SHARE)]

    for g in range(8):
        leaving[g] = jnp.zeros_like(leaving[g])
        leaving[g, :SHARE, :] = grads[pl.ds(g * SHARE, SHARE), :].astype(BF)
    scatter = [
        remote(leaving.at[(group + k) % 8], parts.at[group], mesh.near[k - 1]) for k in range(1, 8)
    ]
    parts[group] = leaving[group]
    yield
    for copy in scatter:
        copy.wait_recv()
    total = parts[0].astype(F32)
    for g in range(1, 8):
        total = total + parts[g].astype(F32)
    by_y[y] = total[:SHARE]
    add_y = [remote(by_y.at[y], by_y.at[y], other) for other in mesh.along_y]
    yield
    for copy in add_y:
        copy.wait_recv()
    by_z[z] = ((by_y[0] + by_y[1]) + by_y[2]) + by_y[3]
    add_z = [remote(by_z.at[z], by_z.at[z], other) for other in mesh.along_z]
    yield
    for copy in add_z:
        copy.wait_recv()
    total = ((by_z[0] + by_z[1]) + by_z[2]) + by_z[3]
    summed[...] = jnp.zeros_like(summed)
    summed[:SHARE, :] = total.astype(BF)
    out_grads[group] = summed[...]
    gather = [remote(summed, out_grads.at[group], other) for other in mesh.near]
    yield
    for copy in gather:
        copy.wait_recv()
    yield


ROUND = [
    pltpu.VMEM((16 * EDGES, HALF, 128), BF),
    pltpu.VMEM((16 * EDGES, HALF, 128), BF),
    pltpu.VMEM((2, 4, EDGES, HALF, 128), BF),
    pltpu.VMEM((4 * EDGES, HALF, 128), BF),
    pltpu.VMEM((4 * EDGES, HALF, 128), BF),
    pltpu.VMEM((64, HALF, 128), BF),
    pltpu.VMEM((1024, 128), F32),
    pltpu.VMEM((1024, 128), F32),
]
COPIES = 2 * (2 + 1 + 6 + 6 + 3 + 2 + 3 + 2 + 6 + 1) + 7 + 3 + 3 + 7


def body(fields, cotangent, first_kernel, second_kernel, adjacency, seam_codes, corner_map):
    f = fields.reshape(R, S * C)
    c = cotangent.reshape(R, S * C)
    tables = (adjacency.T, seam_codes.T, corner_map.T)
    pad, shifts = pltpu.VMEM((PAIRS * PR, 128), F32), pltpu.VMEM((3, PAIRS, R, 128), BF)
    w_conv, w_edge = pltpu.VMEM((3, 512, 256), BF), pltpu.VMEM((384, 768), BF)
    w_corner = pltpu.VMEM((128, 512), BF)
    flat, flat_low = pltpu.VMEM((NP * R, 128), F32), pltpu.VMEM((NP * R, 128), BF)
    turned, shifted = pltpu.VMEM((LINES, 128), F32), pltpu.VMEM((LINES, 384), BF)
    terms, sixteen = pltpu.VMEM((LINES, 768), F32), pltpu.VMEM((16, 128), F32)
    kernel, kernel_sum = pltpu.VMEM((3, 3, C, C), F32), pltpu.VMEM((9 * C, C), F32)
    tile, sums = pltpu.VMEM((R, S * C), BF), pltpu.VMEM((9 * C, 128), F32)
    blocks = pltpu.VMEM((2 * EDGES + 1, HALF, 128), BF)
    near, corners = pltpu.VMEM((LINES, 128), BF), pltpu.VMEM((1024, 128), BF)
    hbm = pl.BlockSpec(memory_space=pltpu.HBM)
    small = pltpu.SMEM((4, 192), jnp.int32)
    sem = pltpu.SemaphoreType.DMA
    shapes = tuple(jax.ShapeDtypeStruct(r.shape, r.dtype) for r in (tile, tile, kernel_sum, kernel_sum))
    results = pl.pallas_call(
        whole_kernel,
        out_shape=shapes,
        in_specs=[hbm] * 7,
        out_specs=(hbm,) * 4,
        scratch_shapes=[tile, tile, kernel, kernel, small, small, small]
        + [pltpu.VMEM((4, 192), jnp.int32), sem((8,)), sem((4,)), pltpu.VMEM((8, 256), jnp.int32)]
        + [pltpu.SMEM((120,), jnp.int32), tile, tile, kernel_sum, kernel_sum]
        + [pad, pad, shifts, shifts, w_conv, w_conv, w_conv, w_conv, w_edge, w_edge]
        + [w_corner] * 4
        + [turned, turned, shifted, shifted, terms, sixteen, flat, flat, flat]
        + [pltpu.VMEM((LINES + HALF, 128), F32), flat_low, flat_low, sums]
        + [blocks, blocks, near, near, corners, corners, pltpu.VMEM((8, SHARE + 8, 128), BF)]
        + ROUND * 2
        + [pltpu.VMEM((SHARE + 8, 128), BF)]
        + [pltpu.VMEM((8, SHARE + 8, 128), BF)]
        + [pltpu.VMEM((k, SHARE, 128), F32) for k in (4, 4)]
        + [pltpu.VMEM((8, SHARE + 8, 128), BF)]
        + [sem((COPIES,))] * 2,
        name="whole",
        compiler_params=pltpu.CompilerParams(
            collective_id=0, has_side_effects=True, vmem_limit_bytes=54 * 2**20
        ),
    )(f, c, first_kernel, second_kernel, *tables)
    output, field_grad, grad_one, grad_two = pl.pallas_call(
        hand_over,
        out_shape=shapes,
        in_specs=[hbm] * 4,
        out_specs=(hbm,) * 4,
        scratch_shapes=[tile, tile, kernel_sum, kernel_sum, sem((4,)), sem((4,))],
        name="hand_over",
        compiler_params=pltpu.CompilerParams(vmem_limit_bytes=58 * 2**20),
    )(*results)
    shape_out = (1, TL, S, S * C)
    return (
        output.reshape(shape_out),
        field_grad.reshape(shape_out),
        grad_one.reshape(3, 3, C, C),
        grad_two.reshape(3, 3, C, C),
    )


def solution(mesh):
    split = P("batch", "tile", None, None)
    return jax.shard_map(
        body,
        mesh=mesh,
        in_specs=(split, split, P(), P(), P(), P(), P()),
        out_specs=(split, split, P(), P()),
        check_vma=False,
    )
```

```python
import math

import jax
import jax.numpy as jnp
from jax import lax
from jax.experimental import pallas as pl
from jax.experimental.pallas import tpu as pltpu
from jax.sharding import PartitionSpec as P

TL = 3
S = 32
C = 64
NP = 16
R = TL * S
EDGES = TL * 4
LINES = EDGES * S
HALF = S // 2
SHARE = 9 * C // 8
PAIRS = NP + 2
PR = 128
MESH = pl.DeviceIdType.MESH
F32 = jnp.float32
BF = jnp.bfloat16


def rows_at(t):
    return t * 40 + 8


def low_lanes(rows):
    return lax.broadcasted_iota(jnp.int32, (rows, 128), 1) < C


def swap(v):
    return pltpu.roll(v, C, 1)


def put_lines(lines, first, second, place, out):
    low16, low32 = low_lanes(16), low_lanes(32)
    step = place(1, 0) - place(0, 0)
    for t in range(TL):
        for e, i in ((0, S - 1), (2, 0)):
            where = pl.ds(place(0, t) + i, NP, stride=step)
            a, b = first[where, :], second[where, :]
            base = (t * 4 + e) * S
            lines[pl.ds(base, NP, stride=2), :] = jnp.where(low16, a, swap(b))
            lines[pl.ds(base + 1, NP, stride=2), :] = jnp.where(low16, swap(a), b)
        for e, pair in ((1, 0), (3, NP - 1)):
            where = pl.ds(place(pair, t), S)
            a, b = first[where, :], second[where, :]
            line = jnp.where(low32, a, swap(b)) if e == 1 else jnp.where(low32, swap(a), b)
            lines[pl.ds((t * 4 + e) * S, S), :] = line
        for corner, (e, s) in enumerate(((2, 0), (2, S - 1), (0, 0), (0, S - 1))):
            lines[pl.ds(LINES + t * 4 + corner, 1), :] = lines[pl.ds((t * 4 + e) * S + s, 1), :]
    lines[pl.ds(LINES + EDGES, HALF - EDGES), :] = jnp.zeros((HALF - EDGES, 128), F32)
    for j in range(EDGES):
        for h in range(2):
            out[h * EDGES + j] = lines[pl.ds(j * S + h * HALF, HALF), :].astype(BF)
    out[2 * EDGES] = lines[pl.ds(LINES, HALF), :].astype(BF)


def fill_pad(pad, src):
    for p in (0, PAIRS - 1):
        pad[pl.ds(p * PR, PR), :] = jnp.zeros((PR, 128), F32)
    for p in range(NP):
        for t in range(TL):
            base = (p + 1) * PR + rows_at(t)
            pad[pl.ds(base - 8, 8), :] = jnp.zeros((8, 128), F32)
            pad[pl.ds(base, S), :] = src[t * S : (t + 1) * S, p * 128 : (p + 1) * 128].astype(F32)
        pad[pl.ds((p + 1) * PR + 120, 8), :] = jnp.zeros((8, 128), F32)


def fill_flat(pad, flat, zero):
    if zero:
        pad[...] = jnp.zeros_like(pad)
    for p in range(NP):
        for t in range(TL):
            pad[pl.ds(pad_place(p, t), S), :] = flat[pl.ds(flat_place(p, t), S), :]


def patch_shifts(xp, pad):
    for t in range(TL):
        for p in (0, PAIRS - 1):
            for a in range(3):
                xp[a, p, t * S : (t + 1) * S, :] = pad[pl.ds(p * PR + rows_at(t) - 1 + a, S), :].astype(BF)
        for p in range(1, PAIRS - 1):
            first = p * PR + rows_at(t)
            xp[0, p, t * S : t * S + HALF, :] = pad[pl.ds(first - 1, HALF), :].astype(BF)
            xp[2, p, t * S + HALF : (t + 1) * S, :] = pad[pl.ds(first + HALF + 1, HALF), :].astype(BF)


def pad_place(pair, t):
    return (pair + 1) * PR + rows_at(t)


def flat_place(pair, t):
    return pair * R + t * S


def make_shifts(xp, pad):
    for a in range(3):
        for p in range(PAIRS):
            for t in range(TL):
                xp[a, p, t * S : (t + 1) * S, :] = pad[pl.ds(p * PR + rows_at(t) - 1 + a, S), :].astype(BF)


def edge_taps(a, c):
    return [
        spot for spot in ((0, c), (1, a), (2, c), (3, a)) if (a == 2, c == 0, a == 0, c == 2)[spot[0]]
    ]


def build_forward(w_out, w_edge, w_cell, w):
    w_out[...] = jnp.zeros_like(w_out)
    w_cell[...] = jnp.zeros_like(w_cell)
    for a in range(3):
        for c in range(3):
            block = w[a, c].astype(BF)
            for n in range(4):
                m = n + 1 + c
                w_out[a, m * C : (m + 1) * C, n * C : (n + 1) * C] = block
            for e, tap in edge_taps(a, c):
                w_edge[(2 - tap) * 128 : (2 - tap) * 128 + C, 256 + e * C : 256 + (e + 1) * C] = block
                w_edge[tap * 128 : tap * 128 + C, 512 + e * C : 512 + (e + 1) * C] = block
            if a != 1 and c != 1:
                at = ((a // 2) * 2 + c // 2) * 128
                w_cell[:C, at : at + C] = block
                w_cell[:C, at + C : at + 128] = block


def build_backward(w_out, w_edge, w_corner, w):
    w_out[...] = jnp.zeros_like(w_out)
    w_corner[...] = jnp.zeros_like(w_corner)
    for a in range(3):
        for c in range(3):
            block = w[a, c].T.astype(BF)
            for n in range(4):
                m = n + 3 - c
                w_out[2 - a, m * C : (m + 1) * C, n * C : (n + 1) * C] = block
            for e, tap in edge_taps(a, c):
                w_edge[tap * 128 + C : tap * 128 + 128, e * C : (e + 1) * C] = block
            if a != 1 and c != 1:
                at = ((a // 2) * 2 + c // 2) * 128
                w_corner[C:128, at : at + C] = block
                w_corner[C:128, at + C : at + 128] = block


def conv(xp, w):
    total = None
    for a in range(3):
        left = jnp.concatenate(
            [
                jnp.concatenate([xp[a, 2 * q + s] for q in range(NP // 2)], axis=0)
                for s in range(4)
            ],
            axis=1,
        )
        part = jnp.dot(left, w[a], preferred_element_type=F32)
        total = part if total is None else total + part
    return total


def columns(xp, a):
    return jnp.concatenate(
        [jnp.concatenate([xp[a, d + p] for p in range(NP)], axis=0) for d in range(3)], axis=1
    )


def first_part(xp, q, a):
    out = lax.dot_general(q, columns(xp, a), (((0,), (0,)), ((), ())), preferred_element_type=F32)
    turned = jnp.concatenate([out[:, d * 128 : (d + 1) * 128].T for d in range(3)], axis=0)
    return turned[64:256] + swap(turned[128:320])


def second_part(qp, h, a):
    out = lax.dot_general(h, columns(qp, 2 - a), (((0,), (0,)), ((), ())), preferred_element_type=F32)
    even, odd = out[:C], out[C:]
    return jnp.concatenate(
        [
            even[:, 128:256] + swap(odd[:, 256:384]),
            swap(even[:, 128:256]) + odd[:, 128:256],
            even[:, :128] + swap(odd[:, 128:256]),
        ],
        axis=0,
    )


def second_rims(grad, lines, wide, corners_ref, corner_rows, codes, me):
    upper = jnp.logical_not(low_lanes(C))
    kept = [lines[pl.ds(j * S, S), :].astype(BF) for j in range(EDGES)]
    ours = [line.astype(BF) for line in reverse(kept, codes)]
    zero = jnp.zeros((S, 128), BF)
    left = jnp.concatenate(
        [
            jnp.concatenate([jnp.where(codes[j] % 4 == e, ours[j], zero) for j in range(EDGES)], axis=0)
            for e in range(4)
        ],
        axis=1,
    )
    out = lax.dot_general(left, wide[...], (((0,), (0,)), ((), ())), preferred_element_type=F32)
    pixels = lines[pl.ds(LINES, 16), :].astype(BF)
    for e in range(4):
        for c in range(3):
            a, b = ((2, c), (c, 0), (0, c), (c, 2))[e]
            at = pl.ds((a * 3 + b) * C, C)
            part = out[e * 128 : e * 128 + C, c * 128 : (c + 1) * 128]
            grad[at, :] = grad[at, :] + jnp.where(upper, part, 0.0)
        met = jnp.dot(
            picked(corner_rows, me, e), corners_ref[pl.ds(e * 256, 256), :], preferred_element_type=F32
        ).astype(BF)
        part = lax.dot_general(pixels, met, (((0,), (0,)), ((), ())), preferred_element_type=F32)
        at = pl.ds(((e // 2) * 6 + (e % 2) * 2) * C, C)
        grad[at, :] = grad[at, :] + jnp.where(upper, part[:C], 0.0)


def reverse(kept, codes, precision=None):
    flip = (
        lax.broadcasted_iota(jnp.int32, (S, S), 0) + lax.broadcasted_iota(jnp.int32, (S, S), 1)
        == S - 1
    )
    flip = jnp.where(flip, 1.0, 0.0).astype(kept[0].dtype)
    flipped = jnp.dot(
        flip, jnp.concatenate(kept, axis=1), preferred_element_type=F32, precision=precision
    )
    return [
        jnp.where(codes[j] >= 4, flipped[:, j * 128 : (j + 1) * 128], kept[j].astype(F32))
        for j in range(EDGES)
    ]


def edge_terms(lines_ref, codes, w_edge, turned, wide, terms):
    lines = lines_ref[...].astype(F32)
    low = low_lanes(S)
    spot = lax.broadcasted_iota(jnp.int32, (LINES, 128), 0) % S
    after = jnp.where(spot == S - 1, 0.0, pltpu.roll(lines, LINES - 1, 0)).astype(BF)
    before = jnp.where(spot == 0, 0.0, pltpu.roll(lines, 1, 0)).astype(BF)
    wide[...] = jnp.concatenate([after, lines_ref[...], before], axis=1)
    terms[...] = jnp.dot(wide[...], w_edge[...], preferred_element_type=F32)
    kept = []
    for j in range(EDGES):
        e, at, tile = codes[j] & 3, pl.ds(j * S, S), (j % 4) // 2 * 128
        pair = jnp.where(e >= 2, terms[at, 128:256], terms[at, :128])
        rim = jnp.where((e & 1) == 1, pair, swap(pair))
        halo = jnp.where(
            codes[j] >= 4, terms[at, 512 + tile : 640 + tile], terms[at, 256 + tile : 384 + tile]
        )
        kept.append(jnp.where(low, swap(halo) if j % 2 else halo, rim.astype(BF).astype(F32)))
    for j, line in enumerate(reverse(kept, codes, lax.Precision.HIGHEST)):
        turned[pl.ds(j * S, S), :] = line


def raw_lines(lines_ref, codes, turned):
    kept = [lines_ref[pl.ds(j * S, S), :] for j in range(EDGES)]
    for j, line in enumerate(reverse(kept, codes)):
        turned[pl.ds(j * S, S), :] = line


def halo_in(pad, turned, cells):
    low16 = low_lanes(16)
    cells_swapped = swap(cells[...])
    for t in range(TL):
        for e, row in ((0, rows_at(t) + S), (2, rows_at(t) - 1)):
            base = (t * 4 + e) * S
            even = turned[pl.ds(base, NP, stride=2), :]
            odd = turned[pl.ds(base + 1, NP, stride=2), :]
            pad[pl.ds(PR + row, NP, stride=PR), :] = jnp.where(low16, even, swap(odd))
        pad[pl.ds(rows_at(t), S), :] = swap(turned[pl.ds((t * 4 + 1) * S, S), :])
        pad[pl.ds((PAIRS - 1) * PR + rows_at(t), S), :] = turned[pl.ds((t * 4 + 3) * S, S), :]
        for corner, (row, p) in enumerate(((-1, 0), (-1, 1), (S, 0), (S, 1))):
            at = t * 4 + corner
            value = (cells[...] if p else cells_swapped)[at : at + 1]
            pad[pl.ds(p * (PAIRS - 1) * PR + rows_at(t) + row, 1), :] = value


def picked(corner_rows, me, kind):
    slot = lax.broadcasted_iota(jnp.int32, (16, 256), 0)
    pick = (corner_rows[kind : kind + 1, :] == me * EDGES + slot) & (slot < EDGES)
    return jnp.where(pick, 1.0, 0.0).astype(BF)


def corner_sums(corners_ref, corner_rows, me, w_corner):
    total = None
    for kind in range(4):
        rim = jnp.dot(
            corners_ref[pl.ds(kind * 256, 256), :],
            w_corner[:, kind * 128 : (kind + 1) * 128],
            preferred_element_type=F32,
        ).astype(BF)
        part = jnp.dot(picked(corner_rows, me, kind), rim, preferred_element_type=F32)
        total = part if total is None else total + part
    return total


def cell_terms(cells, w_cell):
    every = jnp.dot(cells[...].astype(BF), w_cell[...], preferred_element_type=F32)
    kind = lax.broadcasted_iota(jnp.int32, (16, 128), 0) % 4
    total = jnp.zeros((16, 128), F32)
    for k in range(4):
        total = jnp.where(kind == k, every[:, k * 128 : (k + 1) * 128], total)
    return total


def add_edges(flat, turned, upper):
    low16, low32 = low_lanes(16), low_lanes(S)

    def at_low(v):
        return swap(v) if upper else v

    def at_high(v):
        return v if upper else swap(v)

    for t in range(TL):
        for e, i in ((0, S - 1), (2, 0)):
            base = (t * 4 + e) * S
            even = turned[pl.ds(base, NP, stride=2), :]
            odd = turned[pl.ds(base + 1, NP, stride=2), :]
            at = pl.ds(t * S + i, NP, stride=R)
            flat[at, :] = flat[at, :] + jnp.where(low16, at_low(even), at_high(odd))
        at = pl.ds(t * S, S)
        line = at_low(turned[pl.ds((t * 4 + 1) * S, S), :])
        flat[at, :] = flat[at, :] + jnp.where(low32, line, 0.0)
        at = pl.ds((NP - 1) * R + t * S, S)
        line = at_high(turned[pl.ds((t * 4 + 3) * S, S), :])
        flat[at, :] = flat[at, :] + jnp.where(low32, 0.0, line)


def add_cells(flat, cells):
    low16 = low_lanes(16)
    lows, highs = jnp.where(low16, cells, 0.0), jnp.where(low16, 0.0, cells)
    for t in range(TL):
        for corner, (i, p) in enumerate(((0, 0), (0, 1), (S - 1, 0), (S - 1, 1))):
            at = pl.ds(p * (NP - 1) * R + t * S + i, 1)
            s = t * 4 + corner
            flat[at, :] = flat[at, :] + (highs if p else lows)[s : s + 1]


def cells_of(corners_ref, places, me):
    slot = lax.broadcasted_iota(jnp.int32, (16, 1024), 0)
    row = jnp.full((16, 1024), -1, jnp.int32)
    for s in range(EDGES):
        v = places[s % 4, me * TL + s // 4]
        row = jnp.where(slot == s, (v & 3) * 256 + (v >> 2), row)
    pick = jnp.where(lax.broadcasted_iota(jnp.int32, (16, 1024), 1) == row, 1.0, 0.0).astype(BF)
    return jnp.dot(pick, corners_ref[...], preferred_element_type=F32)


def codes_of(seams, me):
    return [seams[j % 4, me * TL + j // 4] for j in range(EDGES)]


def load_rows(corner_rows, rows):
    corner_rows[...] = jnp.full((8, 256), -1, jnp.int32)
    corner_rows[0:4, 0:192] = rows[...]


def put_back(back, out):
    for q in range(NP // 2):
        for half in range(2):
            back[pl.ds((2 * q + half) * R, R), :] = out[q * R : (q + 1) * R, half * 128 : (half + 1) * 128]


def whole_kernel(
    f_hbm, c_hbm, w1_hbm, w2_hbm, adjacency_hbm, seams_hbm, places_hbm,
    output_hbm, field_grad_hbm, grad_one_hbm, grad_two_hbm,
    f_ref, c_ref, w1_ref, w2_ref, adjacency, seams, places, rows, loads, stores, corner_rows, index,
    output, field_grad, grad_one, grad_two,
    pad_f, pad_c, xp, qp, w_forth, w_back, w_forth_two, w_back_two, w_edge, w_edge_two,
    w_corner, w_cell, w_corner_two, w_cell_two,
    turned, raw, wide, wide_two, terms, cells, main, back, hid, lines, grads, hids, grad,
    sent_one, sent_two, near, near_two, corners, corners_two, out_grads, *refs,
):
    me = lax.axis_index("tile")
    inputs = [
        pltpu.make_async_copy(src, dst, loads.at[n])
        for n, (src, dst) in enumerate(
            (
                (f_hbm, f_ref), (c_hbm, c_ref), (w2_hbm, w2_ref), (w1_hbm, w1_ref),
                (adjacency_hbm, adjacency), (seams_hbm, seams), (places_hbm, places), (places_hbm, rows),
            )
        )
    ]
    for copy in inputs:
        copy.start()
    mesh = Mesh()
    mesh.greet()
    n = len(ROUND)
    one, two, rest = refs[:n], refs[n : 2 * n], refs[2 * n :]
    summed, parts, by_y, by_z, leaving, sent, come = rest
    net = Net(sent, come)
    inputs[0].wait()
    fill_pad(pad_f, f_ref)
    inputs[1].wait()
    fill_pad(pad_c, c_ref)
    put_lines(lines, pad_f, pad_c, pad_place, sent_one)
    mesh.meet()
    first = exchange_steps(mesh, net, index, sent_one, near, corners, one)
    next(first)
    for copy in inputs[2:]:
        copy.wait()
    make_shifts(qp, pad_c)
    next(first)
    find_index(mesh, adjacency, seams, index)
    load_rows(corner_rows, rows)
    next(first)
    w_edge[...] = jnp.zeros_like(w_edge)
    next(first)
    make_shifts(xp, pad_f)
    build_backward(w_back, w_edge, w_corner, w2_ref)
    put_back(back, conv(qp, w_back))
    build_forward(w_forth, w_edge, w_cell, w1_ref)
    put_back(main, conv(xp, w_forth))
    w_edge_two[...] = jnp.zeros_like(w_edge_two)
    build_backward(w_back_two, w_edge_two, w_corner_two, w1_ref)
    build_forward(w_forth_two, w_edge_two, w_cell_two, w2_ref)
    next(first)
    cells[...] = cells_of(corners, places, me)
    add_cells(main, cell_terms(cells, w_cell))
    add_cells(back, corner_sums(corners, corner_rows, me, w_corner))
    next(first)

    codes = codes_of(seams, me)
    edge_terms(near, codes, w_edge, turned, wide, terms)
    add_edges(main, turned, False)
    add_edges(back, turned, True)
    for p in range(NP):
        at = pl.ds(p * R, R)
        pre = main[at, :]
        s = 1.0 / (1.0 + jnp.exp(-pre))
        h = (pre * s).astype(BF)
        g = (back[at, :] * s * (1.0 + pre * (1.0 - s))).astype(BF)
        hid[at, :] = h.astype(F32)
        back[at, :] = g.astype(F32)
        grads[at, :] = g
        hids[at, :] = h
    put_lines(lines, hid, back, flat_place, sent_two)
    second = exchange_steps(mesh, net, index, sent_two, near_two, corners_two, two)
    sofar = len(net.copies)
    next(second)
    net.drain(sofar)

    raw_lines(near, codes, raw)
    halo_in(pad_f, raw, cells)
    patch_shifts(xp, pad_f)
    low = low_lanes(192)
    for a in range(3):
        grad[pl.ds(a * 192, 192), :] = jnp.where(
            low, first_part(xp, grads[...], a), second_part(qp, hids[...], a)
        )
    second_rims(grad, lines, wide, corners, corner_rows, codes, me)
    adding = total_steps(mesh, net, grad, out_grads, summed, parts, by_y, by_z, leaving)
    next(adding)
    next(second)
    fill_flat(pad_f, hid, True)
    make_shifts(xp, pad_f)
    next(adding)
    next(second)
    put_back(main, conv(xp, w_forth_two))
    next(adding)
    next(second)
    fill_flat(pad_c, back, False)
    make_shifts(qp, pad_c)
    put_back(back, conv(qp, w_back_two))
    sofar = len(net.copies)
    next(adding)
    net.drain(sofar)
    next(second)
    cells[...] = cells_of(corners_two, places, me)
    add_cells(main, cell_terms(cells, w_cell_two))
    add_cells(back, corner_sums(corners_two, corner_rows, me, w_corner_two))
    next(second)

    edge_terms(near_two, codes, w_edge_two, turned, wide_two, terms)
    add_edges(main, turned, False)
    add_edges(back, turned, True)
    for p in range(NP):
        at, lanes = pl.ds(p * R, R), slice(p * 128, (p + 1) * 128)
        output[:, lanes] = (f_ref[:, lanes].astype(F32) + main[at, :]).astype(BF)
        field_grad[:, lanes] = (c_ref[:, lanes].astype(F32) + back[at, :]).astype(BF)
    results = [
        pltpu.make_async_copy(src, dst, stores.at[n])
        for n, (src, dst) in enumerate(
            (
                (output, output_hbm), (field_grad, field_grad_hbm),
                (grad_one, grad_one_hbm), (grad_two, grad_two_hbm),
            )
        )
    ]
    results[0].start()
    results[1].start()
    next(adding)
    scale = 1.0 / math.sqrt(2 * 192 * S * S)
    for g in range(8):
        share = out_grads[g].astype(F32)[:SHARE] * scale
        grad_one[pl.ds(g * SHARE, SHARE), :] = share[:, :C]
        grad_two[pl.ds(g * SHARE, SHARE), :] = share[:, C:]
    results[2].start()
    results[3].start()
    net.drain()
    for copy in results:
        copy.wait()


def hand_over(*refs):
    ins, outs, held, come, gone = refs[:4], refs[4:8], refs[8:12], refs[12], refs[13]
    arrive = [pltpu.make_async_copy(a, b, come.at[n]) for n, (a, b) in enumerate(zip(ins, held))]
    leave = [pltpu.make_async_copy(a, b, gone.at[n]) for n, (a, b) in enumerate(zip(held, outs))]
    for copy in arrive:
        copy.start()
    for n in range(4):
        arrive[n].wait()
        leave[n].start()
    for copy in leave:
        copy.wait()


class Mesh:
    def __init__(self):
        self.t = t = lax.axis_index("tile")
        self.b = b = lax.axis_index("batch")
        self.z, self.y, self.x, self.core = z, y, x, core = t // 16, (t // 4) % 4, (t // 2) % 2, t % 2
        self.along_z = [(self.index((z + k) % 4, y, x, core), b) for k in range(1, 4)]
        self.along_y = [(self.index(z, (y + k) % 4, x, core), b) for k in range(1, 4)]
        self.sibling = (self.index(z, y, x, 1 - core), b)
        self.across = (self.index(z, y, 1 - x, core), b)
        self.group = x * 4 + b * 2 + core
        self.near = []
        for k in range(1, 8):
            g = (self.group + k) % 8
            self.near.append((self.index(z, y, g // 4, g % 2), (g // 2) % 2))

    def index(self, z, y, x, core):
        return z * 16 + y * 4 + x * 2 + core

    def greet(self):
        for other in self.along_z + self.along_y + self.near:
            pl.semaphore_signal(
                pltpu.get_barrier_semaphore(), inc=1, device_id=other, device_id_type=MESH
            )

    def meet(self):
        pl.semaphore_wait(pltpu.get_barrier_semaphore(), 13)


class Net:
    def __init__(self, sent, come):
        self.sent, self.come, self.copies, self.waited = sent, come, [], 0

    def send(self, src, dst, other):
        n = len(self.copies)
        copy = pltpu.make_async_remote_copy(
            src_ref=src, dst_ref=dst, send_sem=self.sent.at[n], recv_sem=self.come.at[n],
            device_id=other, device_id_type=MESH,
        )
        copy.start()
        self.copies.append(copy)
        return copy

    def drain(self, stop=None):
        stop = len(self.copies) if stop is None else stop
        for copy in self.copies[self.waited : stop]:
            copy.wait_send()
        self.waited = stop


def find_index(mesh, adjacency, seams, index):
    z, y, x, core = mesh.z, mesh.y, mesh.x, mesh.core

    def decode(device, j):
        tile, code = adjacency[j % 4, device * TL + j // 4], seams[j % 4, device * TL + j // 4]
        source = (tile * 171) >> 9
        return source, (tile - source * 3) * 4 + (code & 3)

    for h in range(2):
        for k in range(4):
            device = mesh.index(z, (y + k) % 4, x, core) if h == 0 else mesh.index((z + k) % 4, y, x, core)
            for j in range(EDGES):
                source, line = decode(device, j)
                p = (source >> 4) if h == 0 else ((source >> 2) & 3)
                index[(h * 4 + k) * 12 + j] = ((source & 1) * 8 + ((source >> 1) & 1) * 4 + p) * EDGES + line
                if k == 0:
                    q = ((source >> 2) & 3) if h == 0 else (source >> 4)
                    index[96 + h * 12 + j] = q * EDGES + j


def exchange_steps(mesh, net, index, x_ref, out_lines, out_corners, refs):
    held_a, held_b, chosen, got_a, got_b, cells, apart, ordered = refs
    held, got = (held_a, held_b), (got_a, got_b)
    z, y, x, core = mesh.z, mesh.y, mesh.x, mesh.core
    remote, sibling, across = net.send, mesh.sibling, mesh.across
    along_z, along_y = mesh.along_z, mesh.along_y
    chains = ((z, y, along_z, along_y), (y, z, along_y, along_z))

    def place(h, p, side):
        return held[h].at[pl.ds((core * 8 + side * 4 + p) * EDGES, EDGES)]

    def column(h, side):
        return held[h].at[pl.ds((core * 8 + side * 4) * EDGES, 4 * EDGES)]

    first, over, passed, turn = [], [], [], []
    cell = ((core * 4 + y) * 4 + z) * 2
    for h, (p, _, _, _) in enumerate(chains):
        turn.append(remote(x_ref.at[pl.ds(h * EDGES, EDGES)], place(h, p, x), across))
    cell_x = remote(x_ref.at[2 * EDGES], cells.at[cell + x], across)
    for h, (p, _, others, _) in enumerate(chains):
        mine = x_ref.at[pl.ds(h * EDGES, EDGES)]
        first.append([remote(mine, place(h, p, x), other) for other in others])
    for h, (p, _, _, _) in enumerate(chains):
        over.append([])
        held[h][pl.ds((core * 8 + x * 4 + p) * EDGES, EDGES)] = x_ref[pl.ds(h * EDGES, EDGES)]
    cells[cell + x] = x_ref[2 * EDGES]
    yield

    for h, (p, _, others, _) in enumerate(chains):
        turn[h].wait_recv()
        here = place(h, p, 1 - x)
        passed.append([remote(here, here, other) for other in others])
    cell_x.wait_recv()
    here = cells.at[pl.ds(cell, 2)]
    cell_z = [remote(here, here, other) for other in along_z]
    for h in range(2):
        for copy in first[h]:
            copy.wait_recv()
        over[h].append(remote(column(h, x), column(h, x), sibling))
    yield

    for copy in cell_z:
        copy.wait_recv()
    here = cells.at[pl.ds((core * 4 + y) * 8, 8)]
    cell_y = [remote(here, here, other) for other in along_y]
    for h in range(2):
        for copy in passed[h]:
            copy.wait_recv()
        over[h].append(remote(column(h, 1 - x), column(h, 1 - x), sibling))
    yield

    second = []
    for h, (p, q, _, others) in enumerate(chains):
        for copy in over[h]:
            copy.wait_recv()
        second.append([])
        for k in (2, 1, 3, 0):
            for j in range(EDGES):
                chosen[h, k, j] = held[h][index[(h * 4 + k) * 12 + j]]
            if k:
                there = got[h].at[pl.ds(q * EDGES, EDGES)]
                second[h].append(remote(chosen.at[h, k], there, others[k - 1]))
            else:
                got[h][pl.ds(q * EDGES, EDGES)] = chosen[h, 0]
    for copy in cell_y:
        copy.wait_recv()
    here = cells.at[pl.ds(core * 32, 32)]
    last = remote(here, here, sibling)
    yield

    last.wait_recv()
    for d in range(64):
        apart[d * HALF : (d + 1) * HALF, :] = cells[
            (((d % 2) * 4 + (d // 4) % 4) * 4 + d // 16) * 2 + (d // 2) % 2
        ].astype(F32)
    for kind in range(4):
        for tile in range(TL):
            ordered[pl.ds(kind * 256 + tile, 64, stride=TL), :] = apart[
                pl.ds(tile * 4 + kind, 64, stride=HALF), :
            ]
        ordered[pl.ds(kind * 256 + 192, 64), :] = jnp.zeros((64, 128), F32)
    out_corners[...] = ordered[...].astype(BF)
    yield

    for h in range(2):
        for copy in second[h]:
            copy.wait_recv()
        for j in range(EDGES):
            out_lines[j * S + h * HALF : j * S + (h + 1) * HALF, :] = got[h][index[96 + h * 12 + j]]
    yield


def total_steps(mesh, net, grads, out_grads, summed, parts, by_y, by_z, leaving):
    z, y, group, remote = mesh.z, mesh.y, mesh.group, net.send

    def piece(ref, g):
        return ref.at[pl.ds(pl.multiple_of(g * SHARE, 8), SHARE)]

    for g in range(8):
        leaving[g] = jnp.zeros_like(leaving[g])
        leaving[g, :SHARE, :] = grads[pl.ds(g * SHARE, SHARE), :].astype(BF)
    scatter = [
        remote(leaving.at[(group + k) % 8], parts.at[group], mesh.near[k - 1]) for k in range(1, 8)
    ]
    parts[group] = leaving[group]
    yield
    for copy in scatter:
        copy.wait_recv()
    total = parts[0].astype(F32)
    for g in range(1, 8):
        total = total + parts[g].astype(F32)
    by_y[y] = total[:SHARE]
    add_y = [remote(by_y.at[y], by_y.at[y], other) for other in mesh.along_y]
    yield
    for copy in add_y:
        copy.wait_recv()
    by_z[z] = ((by_y[0] + by_y[1]) + by_y[2]) + by_y[3]
    add_z = [remote(by_z.at[z], by_z.at[z], other) for other in mesh.along_z]
    yield
    for copy in add_z:
        copy.wait_recv()
    total = ((by_z[0] + by_z[1]) + by_z[2]) + by_z[3]
    summed[...] = jnp.zeros_like(summed)
    summed[:SHARE, :] = total.astype(BF)
    out_grads[group] = summed[...]
    gather = [remote(summed, out_grads.at[group], other) for other in mesh.near]
    yield
    for copy in gather:
        copy.wait_recv()
    yield


ROUND = [
    pltpu.VMEM((16 * EDGES, HALF, 128), BF),
    pltpu.VMEM((16 * EDGES, HALF, 128), BF),
    pltpu.VMEM((2, 4, EDGES, HALF, 128), BF),
    pltpu.VMEM((4 * EDGES, HALF, 128), BF),
    pltpu.VMEM((4 * EDGES, HALF, 128), BF),
    pltpu.VMEM((64, HALF, 128), BF),
    pltpu.VMEM((1024, 128), F32),
    pltpu.VMEM((1024, 128), F32),
]
COPIES = 2 * (2 + 1 + 6 + 6 + 3 + 2 + 3 + 2 + 6 + 1) + 7 + 3 + 3 + 7


def body(fields, cotangent, first_kernel, second_kernel, adjacency, seam_codes, corner_map):
    f = fields.reshape(R, S * C)
    c = cotangent.reshape(R, S * C)
    tables = (adjacency.T, seam_codes.T, corner_map.T)
    pad, shifts = pltpu.VMEM((PAIRS * PR, 128), F32), pltpu.VMEM((3, PAIRS, R, 128), BF)
    w_conv, w_edge = pltpu.VMEM((3, 512, 256), BF), pltpu.VMEM((384, 768), BF)
    w_corner = pltpu.VMEM((128, 512), BF)
    flat, flat_low = pltpu.VMEM((NP * R, 128), F32), pltpu.VMEM((NP * R, 128), BF)
    turned, shifted = pltpu.VMEM((LINES, 128), F32), pltpu.VMEM((LINES, 384), BF)
    terms, sixteen = pltpu.VMEM((LINES, 768), F32), pltpu.VMEM((16, 128), F32)
    kernel, kernel_sum = pltpu.VMEM((3, 3, C, C), F32), pltpu.VMEM((9 * C, C), F32)
    tile, sums = pltpu.VMEM((R, S * C), BF), pltpu.VMEM((9 * C, 128), F32)
    blocks = pltpu.VMEM((2 * EDGES + 1, HALF, 128), BF)
    near, corners = pltpu.VMEM((LINES, 128), BF), pltpu.VMEM((1024, 128), BF)
    hbm = pl.BlockSpec(memory_space=pltpu.HBM)
    small = pltpu.SMEM((4, 192), jnp.int32)
    sem = pltpu.SemaphoreType.DMA
    shapes = tuple(jax.ShapeDtypeStruct(r.shape, r.dtype) for r in (tile, tile, kernel_sum, kernel_sum))
    results = pl.pallas_call(
        whole_kernel,
        out_shape=shapes,
        in_specs=[hbm] * 7,
        out_specs=(hbm,) * 4,
        scratch_shapes=[tile, tile, kernel, kernel, small, small, small]
        + [pltpu.VMEM((4, 192), jnp.int32), sem((8,)), sem((4,)), pltpu.VMEM((8, 256), jnp.int32)]
        + [pltpu.SMEM((120,), jnp.int32), tile, tile, kernel_sum, kernel_sum]
        + [pad, pad, shifts, shifts, w_conv, w_conv, w_conv, w_conv, w_edge, w_edge]
        + [w_corner] * 4
        + [turned, turned, shifted, shifted, terms, sixteen, flat, flat, flat]
        + [pltpu.VMEM((LINES + HALF, 128), F32), flat_low, flat_low, sums]
        + [blocks, blocks, near, near, corners, corners, pltpu.VMEM((8, SHARE + 8, 128), BF)]
        + ROUND * 2
        + [pltpu.VMEM((SHARE + 8, 128), BF)]
        + [pltpu.VMEM((8, SHARE + 8, 128), BF)]
        + [pltpu.VMEM((k, SHARE, 128), F32) for k in (4, 4)]
        + [pltpu.VMEM((8, SHARE + 8, 128), BF)]
        + [sem((COPIES,))] * 2,
        name="whole",
        compiler_params=pltpu.CompilerParams(
            collective_id=0, has_side_effects=True, vmem_limit_bytes=54 * 2**20
        ),
    )(f, c, first_kernel, second_kernel, *tables)
    output, field_grad, grad_one, grad_two = pl.pallas_call(
        hand_over,
        out_shape=shapes,
        in_specs=[hbm] * 4,
        out_specs=(hbm,) * 4,
        scratch_shapes=[tile, tile, kernel_sum, kernel_sum, sem((4,)), sem((4,))],
        name="hand_over",
        compiler_params=pltpu.CompilerParams(vmem_limit_bytes=58 * 2**20),
    )(*results)
    shape_out = (1, TL, S, S * C)
    return (
        output.reshape(shape_out),
        field_grad.reshape(shape_out),
        grad_one.reshape(3, 3, C, C),
        grad_two.reshape(3, 3, C, C),
    )


def solution(mesh):
    split = P("batch", "tile", None, None)
    return jax.shard_map(
        body,
        mesh=mesh,
        in_specs=(split, split, P(), P(), P(), P(), P()),
        out_specs=(split, split, P(), P()),
        check_vma=False,
    )
```

```python
import math

import jax
import jax.numpy as jnp
from jax import lax
from jax.experimental import pallas as pl
from jax.experimental.pallas import tpu as pltpu
from jax.sharding import PartitionSpec as P

TL = 3
S = 32
C = 64
NP = 16
R = TL * S
EDGES = TL * 4
LINES = EDGES * S
HALF = S // 2
SHARE = 9 * C // 8
PAIRS = NP + 2
PR = 128
MESH = pl.DeviceIdType.MESH
F32 = jnp.float32
BF = jnp.bfloat16


def rows_at(t):
    return t * 40 + 8


def low_lanes(rows):
    return lax.broadcasted_iota(jnp.int32, (rows, 128), 1) < C


def swap(v):
    return pltpu.roll(v, C, 1)


def put_lines(lines, first, second, place, out):
    low16, low32 = low_lanes(16), low_lanes(32)
    step = place(1, 0) - place(0, 0)
    for t in range(TL):
        for e, i in ((0, S - 1), (2, 0)):
            where = pl.ds(place(0, t) + i, NP, stride=step)
            a, b = first[where, :], second[where, :]
            base = (t * 4 + e) * S
            lines[pl.ds(base, NP, stride=2), :] = jnp.where(low16, a, swap(b))
            lines[pl.ds(base + 1, NP, stride=2), :] = jnp.where(low16, swap(a), b)
        for e, pair in ((1, 0), (3, NP - 1)):
            where = pl.ds(place(pair, t), S)
            a, b = first[where, :], second[where, :]
            line = jnp.where(low32, a, swap(b)) if e == 1 else jnp.where(low32, swap(a), b)
            lines[pl.ds((t * 4 + e) * S, S), :] = line
        for corner, (e, s) in enumerate(((2, 0), (2, S - 1), (0, 0), (0, S - 1))):
            lines[pl.ds(LINES + t * 4 + corner, 1), :] = lines[pl.ds((t * 4 + e) * S + s, 1), :]
    lines[pl.ds(LINES + EDGES, HALF - EDGES), :] = jnp.zeros((HALF - EDGES, 128), F32)
    for j in range(EDGES):
        for h in range(2):
            out[h * EDGES + j] = lines[pl.ds(j * S + h * HALF, HALF), :].astype(BF)
    out[2 * EDGES] = lines[pl.ds(LINES, HALF), :].astype(BF)


def fill_pad(pad, src):
    for p in (0, PAIRS - 1):
        pad[pl.ds(p * PR, PR), :] = jnp.zeros((PR, 128), F32)
    for p in range(NP):
        for t in range(TL):
            base = (p + 1) * PR + rows_at(t)
            pad[pl.ds(base - 8, 8), :] = jnp.zeros((8, 128), F32)
            pad[pl.ds(base, S), :] = src[t * S : (t + 1) * S, p * 128 : (p + 1) * 128].astype(F32)
        pad[pl.ds((p + 1) * PR + 120, 8), :] = jnp.zeros((8, 128), F32)


def fill_flat(pad, flat, zero):
    if zero:
        pad[...] = jnp.zeros_like(pad)
    for p in range(NP):
        for t in range(TL):
            pad[pl.ds(pad_place(p, t), S), :] = flat[pl.ds(flat_place(p, t), S), :]


def patch_shifts(xp, pad):
    for t in range(TL):
        for p in (0, PAIRS - 1):
            for a in range(3):
                xp[a, p, t * S : (t + 1) * S, :] = pad[pl.ds(p * PR + rows_at(t) - 1 + a, S), :].astype(BF)
        for p in range(1, PAIRS - 1):
            first = p * PR + rows_at(t)
            xp[0, p, t * S : t * S + HALF, :] = pad[pl.ds(first - 1, HALF), :].astype(BF)
            xp[2, p, t * S + HALF : (t + 1) * S, :] = pad[pl.ds(first + HALF + 1, HALF), :].astype(BF)


def pad_place(pair, t):
    return (pair + 1) * PR + rows_at(t)


def flat_place(pair, t):
    return pair * R + t * S


def make_shifts(xp, pad):
    for a in range(3):
        for p in range(PAIRS):
            for t in range(TL):
                xp[a, p, t * S : (t + 1) * S, :] = pad[pl.ds(p * PR + rows_at(t) - 1 + a, S), :].astype(BF)


def edge_taps(a, c):
    return [
        spot for spot in ((0, c), (1, a), (2, c), (3, a)) if (a == 2, c == 0, a == 0, c == 2)[spot[0]]
    ]


def build_forward(w_out, w_edge, w_cell, w):
    w_out[...] = jnp.zeros_like(w_out)
    w_cell[...] = jnp.zeros_like(w_cell)
    for a in range(3):
        for c in range(3):
            block = w[a, c].astype(BF)
            for n in range(4):
                m = n + 1 + c
                w_out[a, m * C : (m + 1) * C, n * C : (n + 1) * C] = block
            for e, tap in edge_taps(a, c):
                w_edge[(2 - tap) * 128 : (2 - tap) * 128 + C, 256 + e * C : 256 + (e + 1) * C] = block
                w_edge[tap * 128 : tap * 128 + C, 512 + e * C : 512 + (e + 1) * C] = block
            if a != 1 and c != 1:
                at = ((a // 2) * 2 + c // 2) * 128
                w_cell[:C, at : at + C] = block
                w_cell[:C, at + C : at + 128] = block


def build_backward(w_out, w_edge, w_corner, w):
    w_out[...] = jnp.zeros_like(w_out)
    w_corner[...] = jnp.zeros_like(w_corner)
    for a in range(3):
        for c in range(3):
            block = w[a, c].T.astype(BF)
            for n in range(4):
                m = n + 3 - c
                w_out[2 - a, m * C : (m + 1) * C, n * C : (n + 1) * C] = block
            for e, tap in edge_taps(a, c):
                w_edge[tap * 128 + C : tap * 128 + 128, e * C : (e + 1) * C] = block
            if a != 1 and c != 1:
                at = ((a // 2) * 2 + c // 2) * 128
                w_corner[C:128, at : at + C] = block
                w_corner[C:128, at + C : at + 128] = block


def conv(xp, w):
    total = None
    for a in range(3):
        left = jnp.concatenate(
            [
                jnp.concatenate([xp[a, 2 * q + s] for q in range(NP // 2)], axis=0)
                for s in range(4)
            ],
            axis=1,
        )
        part = jnp.dot(left, w[a], preferred_element_type=F32)
        total = part if total is None else total + part
    return total


def columns(xp, a):
    return jnp.concatenate(
        [jnp.concatenate([xp[a, d + p] for p in range(NP)], axis=0) for d in range(3)], axis=1
    )


def first_part(xp, q, a):
    out = lax.dot_general(q, columns(xp, a), (((0,), (0,)), ((), ())), preferred_element_type=F32)
    turned = jnp.concatenate([out[:, d * 128 : (d + 1) * 128].T for d in range(3)], axis=0)
    return turned[64:256] + swap(turned[128:320])


def second_part(qp, h, a):
    out = lax.dot_general(h, columns(qp, 2 - a), (((0,), (0,)), ((), ())), preferred_element_type=F32)
    even, odd = out[:C], out[C:]
    return jnp.concatenate(
        [
            even[:, 128:256] + swap(odd[:, 256:384]),
            swap(even[:, 128:256]) + odd[:, 128:256],
            even[:, :128] + swap(odd[:, 128:256]),
        ],
        axis=0,
    )


def second_rims(grad, lines, wide, corners_ref, corner_rows, codes, me):
    upper = jnp.logical_not(low_lanes(C))
    kept = [lines[pl.ds(j * S, S), :].astype(BF) for j in range(EDGES)]
    ours = [line.astype(BF) for line in reverse(kept, codes)]
    zero = jnp.zeros((S, 128), BF)
    left = jnp.concatenate(
        [
            jnp.concatenate([jnp.where(codes[j] % 4 == e, ours[j], zero) for j in range(EDGES)], axis=0)
            for e in range(4)
        ],
        axis=1,
    )
    out = lax.dot_general(left, wide[...], (((0,), (0,)), ((), ())), preferred_element_type=F32)
    pixels = lines[pl.ds(LINES, 16), :].astype(BF)
    for e in range(4):
        for c in range(3):
            a, b = ((2, c), (c, 0), (0, c), (c, 2))[e]
            at = pl.ds((a * 3 + b) * C, C)
            part = out[e * 128 : e * 128 + C, c * 128 : (c + 1) * 128]
            grad[at, :] = grad[at, :] + jnp.where(upper, part, 0.0)
        met = jnp.dot(
            picked(corner_rows, me, e), corners_ref[pl.ds(e * 256, 256), :], preferred_element_type=F32
        ).astype(BF)
        part = lax.dot_general(pixels, met, (((0,), (0,)), ((), ())), preferred_element_type=F32)
        at = pl.ds(((e // 2) * 6 + (e % 2) * 2) * C, C)
        grad[at, :] = grad[at, :] + jnp.where(upper, part[:C], 0.0)


def reverse(kept, codes, precision=None):
    flip = (
        lax.broadcasted_iota(jnp.int32, (S, S), 0) + lax.broadcasted_iota(jnp.int32, (S, S), 1)
        == S - 1
    )
    flip = jnp.where(flip, 1.0, 0.0).astype(kept[0].dtype)
    flipped = jnp.dot(
        flip, jnp.concatenate(kept, axis=1), preferred_element_type=F32, precision=precision
    )
    return [
        jnp.where(codes[j] >= 4, flipped[:, j * 128 : (j + 1) * 128], kept[j].astype(F32))
        for j in range(EDGES)
    ]


def edge_terms(lines_ref, codes, w_edge, turned, wide, terms):
    lines = lines_ref[...].astype(F32)
    low = low_lanes(S)
    spot = lax.broadcasted_iota(jnp.int32, (LINES, 128), 0) % S
    after = jnp.where(spot == S - 1, 0.0, pltpu.roll(lines, LINES - 1, 0)).astype(BF)
    before = jnp.where(spot == 0, 0.0, pltpu.roll(lines, 1, 0)).astype(BF)
    wide[...] = jnp.concatenate([after, lines_ref[...], before], axis=1)
    terms[...] = jnp.dot(wide[...], w_edge[...], preferred_element_type=F32)
    kept = []
    for j in range(EDGES):
        e, at, tile = codes[j] & 3, pl.ds(j * S, S), (j % 4) // 2 * 128
        pair = jnp.where(e >= 2, terms[at, 128:256], terms[at, :128])
        rim = jnp.where((e & 1) == 1, pair, swap(pair))
        halo = jnp.where(
            codes[j] >= 4, terms[at, 512 + tile : 640 + tile], terms[at, 256 + tile : 384 + tile]
        )
        kept.append(jnp.where(low, swap(halo) if j % 2 else halo, rim.astype(BF).astype(F32)))
    for j, line in enumerate(reverse(kept, codes, lax.Precision.HIGHEST)):
        turned[pl.ds(j * S, S), :] = line


def raw_lines(lines_ref, codes, turned):
    kept = [lines_ref[pl.ds(j * S, S), :] for j in range(EDGES)]
    for j, line in enumerate(reverse(kept, codes)):
        turned[pl.ds(j * S, S), :] = line


def halo_in(pad, turned, cells):
    low16 = low_lanes(16)
    cells_swapped = swap(cells[...])
    for t in range(TL):
        for e, row in ((0, rows_at(t) + S), (2, rows_at(t) - 1)):
            base = (t * 4 + e) * S
            even = turned[pl.ds(base, NP, stride=2), :]
            odd = turned[pl.ds(base + 1, NP, stride=2), :]
            pad[pl.ds(PR + row, NP, stride=PR), :] = jnp.where(low16, even, swap(odd))
        pad[pl.ds(rows_at(t), S), :] = swap(turned[pl.ds((t * 4 + 1) * S, S), :])
        pad[pl.ds((PAIRS - 1) * PR + rows_at(t), S), :] = turned[pl.ds((t * 4 + 3) * S, S), :]
        for corner, (row, p) in enumerate(((-1, 0), (-1, 1), (S, 0), (S, 1))):
            at = t * 4 + corner
            value = (cells[...] if p else cells_swapped)[at : at + 1]
            pad[pl.ds(p * (PAIRS - 1) * PR + rows_at(t) + row, 1), :] = value


def picked(corner_rows, me, kind):
    slot = lax.broadcasted_iota(jnp.int32, (16, 256), 0)
    pick = (corner_rows[kind : kind + 1, :] == me * EDGES + slot) & (slot < EDGES)
    return jnp.where(pick, 1.0, 0.0).astype(BF)


def corner_sums(corners_ref, corner_rows, me, w_corner):
    total = None
    for kind in range(4):
        rim = jnp.dot(
            corners_ref[pl.ds(kind * 256, 256), :],
            w_corner[:, kind * 128 : (kind + 1) * 128],
            preferred_element_type=F32,
        ).astype(BF)
        part = jnp.dot(picked(corner_rows, me, kind), rim, preferred_element_type=F32)
        total = part if total is None else total + part
    return total


def cell_terms(cells, w_cell):
    every = jnp.dot(cells[...].astype(BF), w_cell[...], preferred_element_type=F32)
    kind = lax.broadcasted_iota(jnp.int32, (16, 128), 0) % 4
    total = jnp.zeros((16, 128), F32)
    for k in range(4):
        total = jnp.where(kind == k, every[:, k * 128 : (k + 1) * 128], total)
    return total


def add_edges(flat, turned, upper):
    low16, low32 = low_lanes(16), low_lanes(S)

    def at_low(v):
        return swap(v) if upper else v

    def at_high(v):
        return v if upper else swap(v)

    for t in range(TL):
        for e, i in ((0, S - 1), (2, 0)):
            base = (t * 4 + e) * S
            even = turned[pl.ds(base, NP, stride=2), :]
            odd = turned[pl.ds(base + 1, NP, stride=2), :]
            at = pl.ds(t * S + i, NP, stride=R)
            flat[at, :] = flat[at, :] + jnp.where(low16, at_low(even), at_high(odd))
        at = pl.ds(t * S, S)
        line = at_low(turned[pl.ds((t * 4 + 1) * S, S), :])
        flat[at, :] = flat[at, :] + jnp.where(low32, line, 0.0)
        at = pl.ds((NP - 1) * R + t * S, S)
        line = at_high(turned[pl.ds((t * 4 + 3) * S, S), :])
        flat[at, :] = flat[at, :] + jnp.where(low32, 0.0, line)


def add_cells(flat, cells):
    low16 = low_lanes(16)
    lows, highs = jnp.where(low16, cells, 0.0), jnp.where(low16, 0.0, cells)
    for t in range(TL):
        for corner, (i, p) in enumerate(((0, 0), (0, 1), (S - 1, 0), (S - 1, 1))):
            at = pl.ds(p * (NP - 1) * R + t * S + i, 1)
            s = t * 4 + corner
            flat[at, :] = flat[at, :] + (highs if p else lows)[s : s + 1]


def cells_of(corners_ref, places, me):
    slot = lax.broadcasted_iota(jnp.int32, (16, 1024), 0)
    row = jnp.full((16, 1024), -1, jnp.int32)
    for s in range(EDGES):
        v = places[s % 4, me * TL + s // 4]
        row = jnp.where(slot == s, (v & 3) * 256 + (v >> 2), row)
    pick = jnp.where(lax.broadcasted_iota(jnp.int32, (16, 1024), 1) == row, 1.0, 0.0).astype(BF)
    return jnp.dot(pick, corners_ref[...], preferred_element_type=F32)


def codes_of(seams, me):
    return [seams[j % 4, me * TL + j // 4] for j in range(EDGES)]


def load_rows(corner_rows, rows):
    corner_rows[...] = jnp.full((8, 256), -1, jnp.int32)
    corner_rows[0:4, 0:192] = rows[...]


def put_back(back, out):
    for q in range(NP // 2):
        for half in range(2):
            back[pl.ds((2 * q + half) * R, R), :] = out[q * R : (q + 1) * R, half * 128 : (half + 1) * 128]


def whole_kernel(
    f_hbm, c_hbm, w1_hbm, w2_hbm, adjacency_hbm, seams_hbm, places_hbm,
    output_hbm, field_grad_hbm, grad_one_hbm, grad_two_hbm,
    f_ref, c_ref, w1_ref, w2_ref, adjacency, seams, places, rows, loads, stores, corner_rows, index,
    output, field_grad, grad_one, grad_two,
    pad_f, pad_c, xp, qp, w_forth, w_back, w_forth_two, w_back_two, w_edge, w_edge_two,
    w_corner, w_cell, w_corner_two, w_cell_two,
    turned, raw, wide, wide_two, terms, cells, main, back, hid, lines, grads, hids, grad,
    sent_one, sent_two, near, near_two, corners, corners_two, out_grads, *refs,
):
    me = lax.axis_index("tile")
    inputs = [
        pltpu.make_async_copy(src, dst, loads.at[n])
        for n, (src, dst) in enumerate(
            (
                (f_hbm, f_ref), (c_hbm, c_ref), (w2_hbm, w2_ref), (w1_hbm, w1_ref),
                (adjacency_hbm, adjacency), (seams_hbm, seams), (places_hbm, places), (places_hbm, rows),
            )
        )
    ]
    for copy in inputs:
        copy.start()
    mesh = Mesh()
    mesh.greet()
    n = len(ROUND)
    one, two, rest = refs[:n], refs[n : 2 * n], refs[2 * n :]
    summed, parts, by_y, by_z, leaving, sent, come = rest
    net = Net(sent, come)
    inputs[0].wait()
    fill_pad(pad_f, f_ref)
    inputs[1].wait()
    fill_pad(pad_c, c_ref)
    put_lines(lines, pad_f, pad_c, pad_place, sent_one)
    mesh.meet()
    first = exchange_steps(mesh, net, index, sent_one, near, corners, one)
    next(first)
    for copy in inputs[2:]:
        copy.wait()
    make_shifts(qp, pad_c)
    next(first)
    find_index(mesh, adjacency, seams, index)
    load_rows(corner_rows, rows)
    next(first)
    w_edge[...] = jnp.zeros_like(w_edge)
    next(first)
    make_shifts(xp, pad_f)
    build_backward(w_back, w_edge, w_corner, w2_ref)
    put_back(back, conv(qp, w_back))
    build_forward(w_forth, w_edge, w_cell, w1_ref)
    put_back(main, conv(xp, w_forth))
    w_edge_two[...] = jnp.zeros_like(w_edge_two)
    build_backward(w_back_two, w_edge_two, w_corner_two, w1_ref)
    build_forward(w_forth_two, w_edge_two, w_cell_two, w2_ref)
    next(first)
    cells[...] = cells_of(corners, places, me)
    add_cells(main, cell_terms(cells, w_cell))
    add_cells(back, corner_sums(corners, corner_rows, me, w_corner))
    next(first)

    codes = codes_of(seams, me)
    edge_terms(near, codes, w_edge, turned, wide, terms)
    add_edges(main, turned, False)
    add_edges(back, turned, True)
    for p in range(NP):
        at = pl.ds(p * R, R)
        pre = main[at, :]
        s = 1.0 / (1.0 + jnp.exp(-pre))
        h = (pre * s).astype(BF)
        g = (back[at, :] * s * (1.0 + pre * (1.0 - s))).astype(BF)
        hid[at, :] = h.astype(F32)
        back[at, :] = g.astype(F32)
        grads[at, :] = g
        hids[at, :] = h
    put_lines(lines, hid, back, flat_place, sent_two)
    second = exchange_steps(mesh, net, index, sent_two, near_two, corners_two, two)
    sofar = len(net.copies)
    next(second)
    net.drain(sofar)

    raw_lines(near, codes, raw)
    halo_in(pad_f, raw, cells)
    patch_shifts(xp, pad_f)
    low = low_lanes(192)
    for a in range(3):
        grad[pl.ds(a * 192, 192), :] = jnp.where(
            low, first_part(xp, grads[...], a), second_part(qp, hids[...], a)
        )
    second_rims(grad, lines, wide, corners, corner_rows, codes, me)
    adding = total_steps(mesh, net, grad, out_grads, summed, parts, by_y, by_z, leaving)
    next(adding)
    next(second)
    next(adding)
    fill_flat(pad_f, hid, True)
    make_shifts(xp, pad_f)
    next(second)
    put_back(main, conv(xp, w_forth_two))
    next(adding)
    next(second)
    fill_flat(pad_c, back, False)
    make_shifts(qp, pad_c)
    put_back(back, conv(qp, w_back_two))
    sofar = len(net.copies)
    next(adding)
    net.drain(sofar)
    next(second)
    cells[...] = cells_of(corners_two, places, me)
    add_cells(main, cell_terms(cells, w_cell_two))
    add_cells(back, corner_sums(corners_two, corner_rows, me, w_corner_two))
    next(second)

    edge_terms(near_two, codes, w_edge_two, turned, wide_two, terms)
    add_edges(main, turned, False)
    add_edges(back, turned, True)
    for p in range(NP):
        at, lanes = pl.ds(p * R, R), slice(p * 128, (p + 1) * 128)
        output[:, lanes] = (f_ref[:, lanes].astype(F32) + main[at, :]).astype(BF)
        field_grad[:, lanes] = (c_ref[:, lanes].astype(F32) + back[at, :]).astype(BF)
    results = [
        pltpu.make_async_copy(src, dst, stores.at[n])
        for n, (src, dst) in enumerate(
            (
                (output, output_hbm), (field_grad, field_grad_hbm),
                (grad_one, grad_one_hbm), (grad_two, grad_two_hbm),
            )
        )
    ]
    results[0].start()
    results[1].start()
    next(adding)
    scale = 1.0 / math.sqrt(2 * 192 * S * S)
    for g in range(8):
        share = out_grads[g].astype(F32)[:SHARE] * scale
        grad_one[pl.ds(g * SHARE, SHARE), :] = share[:, :C]
        grad_two[pl.ds(g * SHARE, SHARE), :] = share[:, C:]
    results[2].start()
    results[3].start()
    net.drain()
    for copy in results:
        copy.wait()


def hand_over(*refs):
    ins, outs, held, come, gone = refs[:4], refs[4:8], refs[8:12], refs[12], refs[13]
    arrive = [pltpu.make_async_copy(a, b, come.at[n]) for n, (a, b) in enumerate(zip(ins, held))]
    leave = [pltpu.make_async_copy(a, b, gone.at[n]) for n, (a, b) in enumerate(zip(held, outs))]
    for copy in arrive:
        copy.start()
    for n in range(4):
        arrive[n].wait()
        leave[n].start()
    for copy in leave:
        copy.wait()


class Mesh:
    def __init__(self):
        self.t = t = lax.axis_index("tile")
        self.b = b = lax.axis_index("batch")
        self.z, self.y, self.x, self.core = z, y, x, core = t // 16, (t // 4) % 4, (t // 2) % 2, t % 2
        self.along_z = [(self.index((z + k) % 4, y, x, core), b) for k in range(1, 4)]
        self.along_y = [(self.index(z, (y + k) % 4, x, core), b) for k in range(1, 4)]
        self.sibling = (self.index(z, y, x, 1 - core), b)
        self.across = (self.index(z, y, 1 - x, core), b)
        self.group = x * 4 + b * 2 + core
        self.near = []
        for k in range(1, 8):
            g = (self.group + k) % 8
            self.near.append((self.index(z, y, g // 4, g % 2), (g // 2) % 2))

    def index(self, z, y, x, core):
        return z * 16 + y * 4 + x * 2 + core

    def greet(self):
        for other in self.along_z + self.along_y + self.near:
            pl.semaphore_signal(
                pltpu.get_barrier_semaphore(), inc=1, device_id=other, device_id_type=MESH
            )

    def meet(self):
        pl.semaphore_wait(pltpu.get_barrier_semaphore(), 13)


class Net:
    def __init__(self, sent, come):
        self.sent, self.come, self.copies, self.waited = sent, come, [], 0

    def send(self, src, dst, other):
        n = len(self.copies)
        copy = pltpu.make_async_remote_copy(
            src_ref=src, dst_ref=dst, send_sem=self.sent.at[n], recv_sem=self.come.at[n],
            device_id=other, device_id_type=MESH,
        )
        copy.start()
        self.copies.append(copy)
        return copy

    def drain(self, stop=None):
        stop = len(self.copies) if stop is None else stop
        for copy in self.copies[self.waited : stop]:
            copy.wait_send()
        self.waited = stop


def find_index(mesh, adjacency, seams, index):
    z, y, x, core = mesh.z, mesh.y, mesh.x, mesh.core

    def decode(device, j):
        tile, code = adjacency[j % 4, device * TL + j // 4], seams[j % 4, device * TL + j // 4]
        source = (tile * 171) >> 9
        return source, (tile - source * 3) * 4 + (code & 3)

    for h in range(2):
        for k in range(4):
            device = mesh.index(z, (y + k) % 4, x, core) if h == 0 else mesh.index((z + k) % 4, y, x, core)
            for j in range(EDGES):
                source, line = decode(device, j)
                p = (source >> 4) if h == 0 else ((source >> 2) & 3)
                index[(h * 4 + k) * 12 + j] = ((source & 1) * 8 + ((source >> 1) & 1) * 4 + p) * EDGES + line
                if k == 0:
                    q = ((source >> 2) & 3) if h == 0 else (source >> 4)
                    index[96 + h * 12 + j] = q * EDGES + j


def exchange_steps(mesh, net, index, x_ref, out_lines, out_corners, refs):
    held_a, held_b, chosen, got_a, got_b, cells, apart, ordered = refs
    held, got = (held_a, held_b), (got_a, got_b)
    z, y, x, core = mesh.z, mesh.y, mesh.x, mesh.core
    remote, sibling, across = net.send, mesh.sibling, mesh.across
    along_z, along_y = mesh.along_z, mesh.along_y
    chains = ((z, y, along_z, along_y), (y, z, along_y, along_z))

    def place(h, p, side):
        return held[h].at[pl.ds((core * 8 + side * 4 + p) * EDGES, EDGES)]

    def column(h, side):
        return held[h].at[pl.ds((core * 8 + side * 4) * EDGES, 4 * EDGES)]

    first, over, passed, turn = [], [], [], []
    cell = ((core * 4 + y) * 4 + z) * 2
    for h, (p, _, _, _) in enumerate(chains):
        turn.append(remote(x_ref.at[pl.ds(h * EDGES, EDGES)], place(h, p, x), across))
    cell_x = remote(x_ref.at[2 * EDGES], cells.at[cell + x], across)
    for h, (p, _, others, _) in enumerate(chains):
        mine = x_ref.at[pl.ds(h * EDGES, EDGES)]
        first.append([remote(mine, place(h, p, x), other) for other in others])
    for h, (p, _, _, _) in enumerate(chains):
        over.append([])
        held[h][pl.ds((core * 8 + x * 4 + p) * EDGES, EDGES)] = x_ref[pl.ds(h * EDGES, EDGES)]
    cells[cell + x] = x_ref[2 * EDGES]
    yield

    for h, (p, _, others, _) in enumerate(chains):
        turn[h].wait_recv()
        here = place(h, p, 1 - x)
        passed.append([remote(here, here, other) for other in others])
    cell_x.wait_recv()
    here = cells.at[pl.ds(cell, 2)]
    cell_z = [remote(here, here, other) for other in along_z]
    for h in range(2):
        for copy in first[h]:
            copy.wait_recv()
        over[h].append(remote(column(h, x), column(h, x), sibling))
    yield

    for copy in cell_z:
        copy.wait_recv()
    here = cells.at[pl.ds((core * 4 + y) * 8, 8)]
    cell_y = [remote(here, here, other) for other in along_y]
    for h in range(2):
        for copy in passed[h]:
            copy.wait_recv()
        over[h].append(remote(column(h, 1 - x), column(h, 1 - x), sibling))
    yield

    second = []
    for h, (p, q, _, others) in enumerate(chains):
        for copy in over[h]:
            copy.wait_recv()
        second.append([])
        for k in (2, 1, 3, 0):
            for j in range(EDGES):
                chosen[h, k, j] = held[h][index[(h * 4 + k) * 12 + j]]
            if k:
                there = got[h].at[pl.ds(q * EDGES, EDGES)]
                second[h].append(remote(chosen.at[h, k], there, others[k - 1]))
            else:
                got[h][pl.ds(q * EDGES, EDGES)] = chosen[h, 0]
    for copy in cell_y:
        copy.wait_recv()
    here = cells.at[pl.ds(core * 32, 32)]
    last = remote(here, here, sibling)
    yield

    last.wait_recv()
    for d in range(64):
        apart[d * HALF : (d + 1) * HALF, :] = cells[
            (((d % 2) * 4 + (d // 4) % 4) * 4 + d // 16) * 2 + (d // 2) % 2
        ].astype(F32)
    for kind in range(4):
        for tile in range(TL):
            ordered[pl.ds(kind * 256 + tile, 64, stride=TL), :] = apart[
                pl.ds(tile * 4 + kind, 64, stride=HALF), :
            ]
        ordered[pl.ds(kind * 256 + 192, 64), :] = jnp.zeros((64, 128), F32)
    out_corners[...] = ordered[...].astype(BF)
    yield

    for h in range(2):
        for copy in second[h]:
            copy.wait_recv()
        for j in range(EDGES):
            out_lines[j * S + h * HALF : j * S + (h + 1) * HALF, :] = got[h][index[96 + h * 12 + j]]
    yield


def total_steps(mesh, net, grads, out_grads, summed, parts, by_y, by_z, leaving):
    z, y, group, remote = mesh.z, mesh.y, mesh.group, net.send

    def piece(ref, g):
        return ref.at[pl.ds(pl.multiple_of(g * SHARE, 8), SHARE)]

    fill = jnp.zeros((8, 128), F32)
    for g in range(8):
        leaving[g] = jnp.concatenate([grads[pl.ds(g * SHARE, SHARE), :], fill], axis=0).astype(BF)
    scatter = [
        remote(leaving.at[(group + k) % 8], parts.at[group], mesh.near[k - 1]) for k in range(1, 8)
    ]
    parts[group] = leaving[group]
    yield
    for copy in scatter:
        copy.wait_recv()
    total = parts[0].astype(F32)
    for g in range(1, 8):
        total = total + parts[g].astype(F32)
    by_y[y] = total[:SHARE]
    add_y = [remote(by_y.at[y], by_y.at[y], other) for other in mesh.along_y]
    yield
    for copy in add_y:
        copy.wait_recv()
    by_z[z] = ((by_y[0] + by_y[1]) + by_y[2]) + by_y[3]
    add_z = [remote(by_z.at[z], by_z.at[z], other) for other in mesh.along_z]
    yield
    for copy in add_z:
        copy.wait_recv()
    total = ((by_z[0] + by_z[1]) + by_z[2]) + by_z[3]
    summed[...] = jnp.concatenate([total, fill], axis=0).astype(BF)
    out_grads[group] = summed[...]
    gather = [remote(summed, out_grads.at[group], other) for other in mesh.near]
    yield
    for copy in gather:
        copy.wait_recv()
    yield


ROUND = [
    pltpu.VMEM((16 * EDGES, HALF, 128), BF),
    pltpu.VMEM((16 * EDGES, HALF, 128), BF),
    pltpu.VMEM((2, 4, EDGES, HALF, 128), BF),
    pltpu.VMEM((4 * EDGES, HALF, 128), BF),
    pltpu.VMEM((4 * EDGES, HALF, 128), BF),
    pltpu.VMEM((64, HALF, 128), BF),
    pltpu.VMEM((1024, 128), F32),
    pltpu.VMEM((1024, 128), F32),
]
COPIES = 2 * (2 + 1 + 6 + 6 + 3 + 2 + 3 + 2 + 6 + 1) + 7 + 3 + 3 + 7


def body(fields, cotangent, first_kernel, second_kernel, adjacency, seam_codes, corner_map):
    f = fields.reshape(R, S * C)
    c = cotangent.reshape(R, S * C)
    tables = (adjacency.T, seam_codes.T, corner_map.T)
    pad, shifts = pltpu.VMEM((PAIRS * PR, 128), F32), pltpu.VMEM((3, PAIRS, R, 128), BF)
    w_conv, w_edge = pltpu.VMEM((3, 512, 256), BF), pltpu.VMEM((384, 768), BF)
    w_corner = pltpu.VMEM((128, 512), BF)
    flat, flat_low = pltpu.VMEM((NP * R, 128), F32), pltpu.VMEM((NP * R, 128), BF)
    turned, shifted = pltpu.VMEM((LINES, 128), F32), pltpu.VMEM((LINES, 384), BF)
    terms, sixteen = pltpu.VMEM((LINES, 768), F32), pltpu.VMEM((16, 128), F32)
    kernel, kernel_sum = pltpu.VMEM((3, 3, C, C), F32), pltpu.VMEM((9 * C, C), F32)
    tile, sums = pltpu.VMEM((R, S * C), BF), pltpu.VMEM((9 * C, 128), F32)
    blocks = pltpu.VMEM((2 * EDGES + 1, HALF, 128), BF)
    near, corners = pltpu.VMEM((LINES, 128), BF), pltpu.VMEM((1024, 128), BF)
    hbm = pl.BlockSpec(memory_space=pltpu.HBM)
    small = pltpu.SMEM((4, 192), jnp.int32)
    sem = pltpu.SemaphoreType.DMA
    shapes = tuple(jax.ShapeDtypeStruct(r.shape, r.dtype) for r in (tile, tile, kernel_sum, kernel_sum))
    results = pl.pallas_call(
        whole_kernel,
        out_shape=shapes,
        in_specs=[hbm] * 7,
        out_specs=(hbm,) * 4,
        scratch_shapes=[tile, tile, kernel, kernel, small, small, small]
        + [pltpu.VMEM((4, 192), jnp.int32), sem((8,)), sem((4,)), pltpu.VMEM((8, 256), jnp.int32)]
        + [pltpu.SMEM((120,), jnp.int32), tile, tile, kernel_sum, kernel_sum]
        + [pad, pad, shifts, shifts, w_conv, w_conv, w_conv, w_conv, w_edge, w_edge]
        + [w_corner] * 4
        + [turned, turned, shifted, shifted, terms, sixteen, flat, flat, flat]
        + [pltpu.VMEM((LINES + HALF, 128), F32), flat_low, flat_low, sums]
        + [blocks, blocks, near, near, corners, corners, pltpu.VMEM((8, SHARE + 8, 128), BF)]
        + ROUND * 2
        + [pltpu.VMEM((SHARE + 8, 128), BF)]
        + [pltpu.VMEM((8, SHARE + 8, 128), BF)]
        + [pltpu.VMEM((k, SHARE, 128), F32) for k in (4, 4)]
        + [pltpu.VMEM((8, SHARE + 8, 128), BF)]
        + [sem((COPIES,))] * 2,
        name="whole",
        compiler_params=pltpu.CompilerParams(
            collective_id=0, has_side_effects=True, vmem_limit_bytes=54 * 2**20
        ),
    )(f, c, first_kernel, second_kernel, *tables)
    output, field_grad, grad_one, grad_two = pl.pallas_call(
        hand_over,
        out_shape=shapes,
        in_specs=[hbm] * 4,
        out_specs=(hbm,) * 4,
        scratch_shapes=[tile, tile, kernel_sum, kernel_sum, sem((4,)), sem((4,))],
        name="hand_over",
        compiler_params=pltpu.CompilerParams(vmem_limit_bytes=58 * 2**20),
    )(*results)
    shape_out = (1, TL, S, S * C)
    return (
        output.reshape(shape_out),
        field_grad.reshape(shape_out),
        grad_one.reshape(3, 3, C, C),
        grad_two.reshape(3, 3, C, C),
    )


def solution(mesh):
    split = P("batch", "tile", None, None)
    return jax.shard_map(
        body,
        mesh=mesh,
        in_specs=(split, split, P(), P(), P(), P(), P()),
        out_specs=(split, split, P(), P()),
        check_vma=False,
    )
```
